256 devices in a mesh: cluster: 32 (over z, y), rep: 8 (over x, core).
Axes of the slice: x: 4, y: 4, z: 8, core: 2. Of those that a mesh axis runs over, the one named last changes fastest.
Arguments:
- vectors: float32 [65536, 768], P(('cluster', 'rep')), may hold values from -6 to 6
- parent_id: int32 [65536], P(('cluster', 'rep')), may hold values from 0 to 1023, as said below
- child_id: int32 [65536], P(('cluster', 'rep')), may hold values from 0 to 7
Outputs:
- centroids: float32 [8192, 768], P('cluster')
- shares: float32 [65536, 8], P(('cluster', 'rep'))
The draws below stay inside these ranges and needn't reach their ends.
Inputs may be any that keep to these rules, and one draw needn't show every extreme that they name: `parent_id`: the vectors of one device (aligned blocks of 256 rows) fall under the parents of one owner block o (ids 32 o to 32 o + 31) at most 24 times for each o, and exactly 24 times for some o.
All inputs are finite; a program needn't handle non-finite values.
Results may differ from the reference program's by a relative error of at most 0.0001.
Values sent between devices are 32-bit elements; how exact they have to be, the bound alone decides.
No kernel may reach another device: no remote copies, remote signals or barrier semaphores. Data moves between devices by JAX's collectives and lax.ppermute only.
A program may use at most 64 MiB of HBM per device.

```python
import jax
import jax.numpy as jnp
from jax import lax

D = 768
K = 8
PAR_DEV = 32
VEC_DEV = 256
PARENTS = 1024
NVEC = 65536
CAP = 24


def draw_parent_id(key, part):
    key = jax.random.fold_in(key, 11)
    owners = PARENTS // PAR_DEV
    blocks = NVEC // VEC_DEV
    rest = VEC_DEV - CAP
    half_span = max(1, (owners - 1) // 2)
    place = jnp.arange(VEC_DEV, dtype=jnp.int32)
    later = place - CAP
    rank = jnp.where(place < CAP, 0, jnp.where(later < rest // 2, 1 + later % (owners - 1), 1 + later % half_span))

    def one_block(bkey):
        keys = jax.random.split(bkey, 5)
        order = jax.random.permutation(keys[0], owners).astype(jnp.int32)
        owner = order[rank]
        local_a = jax.random.randint(keys[1], (VEC_DEV,), 0, PAR_DEV)
        local_b = jax.random.randint(keys[2], (VEC_DEV,), 0, PAR_DEV)
        local_c = jax.random.randint(keys[3], (VEC_DEV,), 0, PAR_DEV)
        local = jnp.minimum(jnp.minimum(local_a, local_b), local_c)
        ids = (owner * PAR_DEV + local).astype(jnp.int32)
        return jax.random.permutation(keys[4], ids)
    return jax.vmap(one_block)(jax.random.split(key, blocks)).reshape(NVEC).astype(jnp.int32)


def set_ends(result, key, low, largest):
    shape = result.shape
    index_at = [jax.random.randint(jax.random.fold_in(key, axis), (), 0, shape[axis]) for axis in range(len(shape))]
    result = result.at[tuple(index_at)].set(low)
    longest = shape.index(max(shape))
    index_at[longest] = (index_at[longest] + 1) % shape[longest]
    return result.at[tuple(index_at)].set(largest)


def steps_of(stream_key, dims, pieces, smallest, largest):
    gain, own = 1.0, jax.random.fold_in(stream_key, 6)
    for position, shards_of in pieces:
        heights = jnp.exp(jax.random.uniform(jax.random.fold_in(own, position), (shards_of,), jnp.float32, smallest / len(pieces), largest / len(pieces)))
        gain = gain * jnp.repeat(heights, dims[position] // shards_of).reshape([-1 if axis == position else 1 for axis in range(len(dims))])
    return gain


def bell_draw(key, dims, width, bound, pieces=(), kind=jnp.bfloat16):
    factor_of = steps_of(key, dims, pieces, -0.22, 0.18) if pieces else 1.0
    array = jax.random.normal(key, dims, jnp.float32) * width * factor_of
    return jnp.minimum(jnp.maximum(array, -bound), bound).astype(kind)


def setup_inputs(seed: int = 0) -> dict:
    key_of = jax.random.split(jax.random.key(seed), 4)
    return {
        "vectors": bell_draw(key_of[0], (NVEC, D), 1.0, 6.0, ((0, 256),), jnp.float32),
        "parent_id": draw_parent_id(jax.random.fold_in(key_of[3], 71), 0),
        "child_id": set_ends(jax.random.randint(key_of[2], (NVEC,), 0, K), jax.random.fold_in(key_of[2], 1), 0, K - 1).astype(jnp.int32),
    }


def reference(vectors, parent_id, child_id):
    slots = PARENTS * K
    slot = parent_id * K + child_id
    sums = jax.ops.segment_sum(vectors, slot, slots)
    counts = jax.ops.segment_sum(jnp.ones(slot.shape, jnp.float32), slot, slots)
    first = sums / (counts + 1.0)[:, None]
    cent3 = first.reshape(PARENTS, K, D)
    cnt2 = counts.reshape(PARENTS, K)

    def block_shares(blk):
        rows, parents = blk
        cent = cent3[parents]
        dist = jnp.sum((rows[:, None, :] - cent) ** 2, axis=-1) / D
        cnt = cnt2[parents]
        mean = jnp.sum(cnt, axis=1, keepdims=True) / K
        pen = dist + 0.5 * cnt / (mean + 1.0)
        weight = (1.0 + pen) ** -4
        return weight / jnp.sum(weight, axis=1, keepdims=True)

    blocks = NVEC // VEC_DEV
    shares = lax.map(block_shares, (vectors.reshape(blocks, VEC_DEV, D), parent_id.reshape(blocks, VEC_DEV)))
    shares = shares.reshape(NVEC, K)
    weighted = jnp.zeros((PARENTS, K, D), jnp.float32)
    total = jnp.zeros((PARENTS, K), jnp.float32)
    for k in range(K):
        weighted = weighted.at[:, k, :].set(jax.ops.segment_sum(shares[:, k:k + 1] * vectors, parent_id, PARENTS))
        total = total.at[:, k].set(jax.ops.segment_sum(shares[:, k], parent_id, PARENTS))
    centroids = weighted.reshape(slots, D) / (total.reshape(slots) + 1.0)[:, None]
    return centroids, shares
```

```python
import functools

import jax
import jax.numpy as jnp
from jax import lax
from jax.experimental import pallas as pl
from jax.experimental.pallas import tpu as pltpu
from jax.sharding import PartitionSpec as P

K = 8
PAR_DEV = 32
OWNERS = 32
REPS = 8
SLOTS = PAR_DEV * K
D = 768
PART = D // REPS
ROWS = PART + 8
VEC = 256
LANES = 128
PAIR = 2 * LANES
STACK = PART + 16 + PART
F32 = jnp.float32
BF16 = jnp.bfloat16
NT = (((1,), (1,)), ((), ()))


def params():
    return pltpu.CompilerParams(vmem_limit_bytes=48 * 2**20)


def iota(shape, dim):
    return lax.broadcasted_iota(jnp.int32, shape, dim)


def parts_of(x):
    high = x.astype(BF16)
    return high, (x - high.astype(F32)).astype(BF16)


def turn_kernel(v_ref, g_ref, out_ref):
    for tile in range(D // LANES):
        turned = v_ref[:, tile * LANES : (tile + 1) * LANES].T
        start = tile * LANES
        while start < (tile + 1) * LANES:
            part, row = divmod(start, PART)
            size = min(PART - row, (tile + 1) * LANES - start)
            at = start - tile * LANES
            out_ref[part, row : row + size, :] = turned[at : at + size, :]
            start += size
    slots = jnp.broadcast_to(g_ref[...], (ROWS - PART, VEC))
    for part in range(REPS):
        out_ref[part, PART:ROWS, :] = slots


def pack_kernel(cap, in_ref, out_ref, target_ref, most_ref, left, column):
    groups = OWNERS * cap // PAIR
    before = (iota((VEC, VEC), 0) < iota((VEC, VEC), 1)).astype(F32).astype(BF16)
    carry = jnp.zeros((OWNERS, 1), F32)
    targets = []
    for src in range(REPS):
        slot = in_ref[src, PART : PART + 1, :].astype(jnp.int32)
        owner = slot >> 8
        local = (slot & (SLOTS - 1)) + 1
        hot = (owner == iota((OWNERS, VEC), 0)).astype(F32)
        ahead = jnp.dot(hot.astype(BF16), before, preferred_element_type=F32) + carry
        position = jnp.sum(hot * ahead, axis=0, keepdims=True)
        carry = carry + jnp.sum(hot, axis=1, keepdims=True)
        target = owner.astype(F32) * cap + position
        targets.append(jnp.where(position < cap, target, -1.0))
        high, low = parts_of(in_ref[src, 0:PART, :])
        left[src, 0:PART, :] = high
        left[src, PART : PART + 16, :] = jnp.broadcast_to(local.astype(F32), (16, VEC)).astype(BF16)
        left[src, PART + 16 : STACK, :] = low
    rows = jnp.concatenate(targets, axis=0)
    target_ref[...] = rows.astype(jnp.int32)
    most_ref[...] = jnp.broadcast_to(jnp.max(carry, axis=0, keepdims=True), (8, LANES))
    turned = jnp.concatenate([rows, jnp.zeros((LANES - REPS, VEC), F32)], axis=0).T
    for src in range(REPS):
        column[src] = jnp.broadcast_to(turned[:, src : src + 1], (VEC, LANES))
    lane = iota((VEC, LANES), 1).astype(F32)

    def group(n, _):
        base = (n * PAIR).astype(F32)
        total = jnp.zeros((STACK, PAIR), F32)
        for src in range(REPS):
            at = column[src] - base
            hot = jnp.concatenate(
                [
                    jnp.where(at == lane, 1.0, 0.0).astype(BF16),
                    jnp.where(at == lane + LANES, 1.0, 0.0).astype(BF16),
                ],
                axis=1,
            )
            total = total + jnp.dot(left[src], hot, preferred_element_type=F32)
        values = total[0:PART] + total[PART + 16 : STACK]
        for half in range(2):
            cut = slice(half * LANES, (half + 1) * LANES)
            out_ref[2 * n + half, 0:PART, :] = values[:, cut]
            out_ref[2 * n + half, PART:ROWS, :] = total[PART : PART + 8, cut]
        return 0

    lax.fori_loop(0, groups, group, 0)


def load_pair(x_ref, n):
    x = jnp.concatenate([x_ref[2 * n, 0:PART, :], x_ref[2 * n + 1, 0:PART, :]], axis=1)
    slot = jnp.concatenate(
        [x_ref[2 * n, PART : PART + 1, :], x_ref[2 * n + 1, PART : PART + 1, :]], axis=1
    )
    return x, slot.astype(jnp.int32)


def stack_of(x):
    high, low = parts_of(x)
    return jnp.concatenate([high, jnp.ones((16, PAIR), BF16), low], axis=0)


def distance_kernel(blocks, x_ref, out_ref, total):
    total[...] = jnp.zeros_like(total)

    def add(n, _):
        x, slot = load_pair(x_ref, n)
        hot = jnp.where(iota((SLOTS, PAIR), 0) + 1 == slot, 1.0, 0.0).astype(BF16)
        total[...] += lax.dot_general(stack_of(x), hot, NT, preferred_element_type=F32)
        return 0

    lax.fori_loop(0, blocks // 2, add, 0)
    sums = total[0:PART, :] + total[PART + 16 : STACK, :]
    counts = total[PART : PART + 8, :]
    first = sums / (counts[0:1] + 1.0)
    turned = jnp.concatenate(
        [first, counts, jnp.zeros((LANES - PART - 8, SLOTS), F32)], axis=0
    ).T
    center = turned[:, 0:PART]
    count = turned[:, PART : PART + 1].reshape(PAR_DEV, K, 1)
    mean = jnp.sum(count, axis=1, keepdims=True) / K
    extra = (0.5 * count / (mean + 1.0)).reshape(SLOTS, 1) / REPS
    own = jnp.sum(center * center, axis=1, keepdims=True) / D + extra
    scaled = center * (-2.0 / D)

    def measure(n, _):
        x, slot = load_pair(x_ref, n)
        cross = jnp.dot(
            scaled, x, precision=lax.Precision.HIGHEST, preferred_element_type=F32
        )
        parent = (slot - 1) >> 3
        terms = (cross + own).reshape(PAR_DEV, K, PAIR)
        picked = jnp.where(iota((PAR_DEV, K, PAIR), 0) == parent[None], terms, 0.0)
        part = jnp.sum(picked, axis=0) + jnp.sum(x * x, axis=0, keepdims=True) / D
        out_ref[2 * n] = part[:, 0:LANES]
        out_ref[2 * n + 1] = part[:, LANES:PAIR]
        return 0

    lax.fori_loop(0, blocks // 2, measure, 0)


def share_kernel(blocks, x_ref, pen_ref, cent_ref, share_ref, total, rest):
    total[...] = jnp.zeros_like(total)
    rest[...] = jnp.zeros_like(rest)

    def add(n, _):
        x, slot = load_pair(x_ref, n)
        grown = 1.0 + jnp.concatenate([pen_ref[2 * n], pen_ref[2 * n + 1]], axis=1)
        square = grown * grown
        weight = 1.0 / (square * square)
        share = weight / jnp.sum(weight, axis=0, keepdims=True)
        share = jnp.where(slot > 0, share, 0.0)
        share_ref[2 * n] = share[:, 0:LANES]
        share_ref[2 * n + 1] = share[:, LANES:PAIR]
        parent = (slot - 1) >> 3
        mixing = jnp.where(
            iota((PAR_DEV, K, PAIR), 0) == parent[None], share[None], 0.0
        ).reshape(SLOTS, PAIR)
        high, low = parts_of(mixing)
        left = stack_of(x)
        total[...] += lax.dot_general(left, high, NT, preferred_element_type=F32)
        rest[...] += lax.dot_general(
            left[0 : PART + 16], low, NT, preferred_element_type=F32
        )
        return 0

    lax.fori_loop(0, blocks // 2, add, 0)
    weighted = total[0:PART, :] + total[PART + 16 : STACK, :] + rest[0:PART, :]
    summed = total[PART : PART + 1, :] + rest[PART : PART + 1, :]
    cent_ref[...] = weighted / (summed + 1.0)


def join_kernel(at_ref, *refs):
    *pieces, out_ref, whole = refs
    x, core = at_ref[0], at_ref[1]
    for index, piece in enumerate(pieces):
        step, other = divmod(index, 2)
        where = ((x - step) & 3) * 2 + (core ^ other)
        whole[pl.ds(pl.multiple_of(where * PART, 8), PART), :] = piece[...]
    for tile in range(D // LANES):
        cut = slice(tile * LANES, (tile + 1) * LANES)
        out_ref[:, cut] = whole[cut, :].T


def take_kernel(blocks, at_ref, back_ref, target_ref, out_ref):
    target = target_ref[pl.ds(at_ref[2], 1), :]
    total = jnp.zeros((3 * K, VEC), F32)
    for n in range(blocks):
        hot = jnp.where(iota((LANES, VEC), 0) + n * LANES == target, 1.0, 0.0).astype(BF16)
        high, low = parts_of(back_ref[n])
        least = (back_ref[n] - high.astype(F32) - low.astype(F32)).astype(BF16)
        left = jnp.concatenate([high.astype(F32), low.astype(F32), least.astype(F32)], axis=0)
        total = total + jnp.dot(left.astype(BF16), hot, preferred_element_type=F32)
    out_ref[...] = total[0:K] + total[K : 2 * K] + total[2 * K : 3 * K]


def shape(*dims, kind=F32):
    return jax.ShapeDtypeStruct(dims, kind)


def cost(flops, data):
    return pl.CostEstimate(flops=flops, bytes_accessed=data, transcendentals=0)


def along_x(step):
    return [(i, ((i // 2 + step) % 4) * 2 + i % 2) for i in range(REPS)]


CORES = [(i, i ^ 1) for i in range(REPS)]


def sum_over_rep(x):
    x = x + lax.ppermute(x, "rep", CORES)
    x = x + lax.ppermute(x, "rep", [(i, i ^ 2) for i in range(REPS)])
    return x + lax.ppermute(x, "rep", [(i, i ^ 6) for i in range(REPS)])


def refine(cap, got):
    blocks = OWNERS * cap // LANES
    packed, target, most = pl.pallas_call(
        functools.partial(pack_kernel, cap),
        out_shape=(
            shape(blocks, ROWS, LANES),
            shape(REPS, VEC, kind=jnp.int32),
            shape(8, LANES),
        ),
        scratch_shapes=[pltpu.VMEM((REPS, STACK, VEC), BF16), pltpu.VMEM((REPS, VEC, LANES), F32)],
        compiler_params=params(),
        cost_estimate=cost(2 * STACK * 2048 * OWNERS * cap, 3_000_000),
        name="pack",
    )(got)
    per = cap // LANES
    rows = lax.all_to_all(
        packed.reshape(OWNERS, per * ROWS, LANES), "cluster", 0, 0, tiled=True
    ).reshape(blocks, ROWS, LANES)
    partial = pl.pallas_call(
        functools.partial(distance_kernel, blocks),
        out_shape=shape(blocks, K, LANES),
        scratch_shapes=[pltpu.VMEM((STACK, SLOTS), F32)],
        compiler_params=params(),
        cost_estimate=cost(2 * 8 * PART * SLOTS * OWNERS * cap, 2_000_000),
        name="distance",
    )(rows)
    pen = sum_over_rep(partial)
    cent, share = pl.pallas_call(
        functools.partial(share_kernel, blocks),
        out_shape=(shape(PART, SLOTS), shape(blocks, K, LANES)),
        scratch_shapes=[
            pltpu.VMEM((STACK, SLOTS), F32),
            pltpu.VMEM((PART + 16, SLOTS), F32),
        ],
        compiler_params=params(),
        cost_estimate=cost(2 * 3 * PART * SLOTS * OWNERS * cap, 2_000_000),
        name="share",
    )(rows, pen)
    back = lax.all_to_all(
        share.reshape(OWNERS, per * K, LANES), "cluster", 0, 0, tiled=True
    ).reshape(blocks, K, LANES)
    pieces = []
    for step in range(4):
        mine = lax.ppermute(cent, "rep", along_x(step)) if step else cent
        pieces += [mine, lax.ppermute(mine, "rep", CORES)]
    return pieces, back, target, most


def finish(cap, pieces, back, target):
    blocks = OWNERS * cap // LANES
    rep = lax.axis_index("rep")
    at = jnp.stack([rep // 2, rep % 2, rep]).astype(jnp.int32)
    smem = pl.BlockSpec(memory_space=pltpu.SMEM)
    vmem = pl.BlockSpec(memory_space=pltpu.VMEM)
    centroids = pl.pallas_call(
        join_kernel,
        out_shape=shape(SLOTS, D),
        in_specs=[smem] + [vmem] * REPS,
        scratch_shapes=[pltpu.VMEM((D, SLOTS), F32)],
        compiler_params=params(),
        cost_estimate=cost(0, 1_600_000),
        name="join",
    )(at, *pieces)
    shares = pl.pallas_call(
        functools.partial(take_kernel, blocks),
        out_shape=shape(K, VEC),
        in_specs=[smem, vmem, vmem],
        compiler_params=params(),
        cost_estimate=cost(2 * 24 * VEC * OWNERS * cap, 200_000),
        name="take",
    )(at, back, target)
    return centroids, shares


def on_device(vectors, parent_id, child_id):
    slot = (parent_id * K + child_id).astype(F32).reshape(1, VEC)
    turned = pl.pallas_call(
        turn_kernel,
        out_shape=shape(REPS, ROWS, VEC),
        compiler_params=params(),
        cost_estimate=cost(0, 1_600_000),
        name="turn",
    )(vectors, slot)
    got = lax.all_to_all(turned, "rep", 0, 0, tiled=True)
    pieces, back, target, most = refine(LANES, got)
    for bit in (1, 2, 4, 8, 16):
        most = jnp.maximum(
            most, lax.ppermute(most, "cluster", [(i, i ^ bit) for i in range(OWNERS)])
        )
    over = most[0, 0] > LANES

    def wide(got, pieces, back, target):
        pieces, back, target, _ = refine(PAIR, got)
        return finish(PAIR, pieces, back, target)

    def narrow(got, pieces, back, target):
        return finish(LANES, pieces, back, target)

    centroids, shares = lax.cond(over, wide, narrow, got, pieces, back, target)
    return centroids, shares.T


def solution(mesh):
    in_specs = (P(("cluster", "rep"), None), P(("cluster", "rep")), P(("cluster", "rep")))
    out_specs = (P("cluster", None), P(("cluster", "rep"), None))
    return jax.shard_map(
        on_device, mesh=mesh, in_specs=in_specs, out_specs=out_specs, check_vma=False
    )
```

```python
import functools

import jax
import jax.numpy as jnp
from jax import lax
from jax.experimental import pallas as pl
from jax.experimental.pallas import tpu as pltpu
from jax.sharding import PartitionSpec as P

K = 8
PAR_DEV = 32
OWNERS = 32
REPS = 8
SLOTS = PAR_DEV * K
D = 768
PART = D // REPS
ROWS = PART + 8
VEC = 256
LANES = 128
PAIR = 2 * LANES
STACK = PART + 16 + PART
F32 = jnp.float32
BF16 = jnp.bfloat16
NT = (((1,), (1,)), ((), ()))


def params():
    return pltpu.CompilerParams(vmem_limit_bytes=48 * 2**20)


def iota(shape, dim):
    return lax.broadcasted_iota(jnp.int32, shape, dim)


def parts_of(x):
    high = x.astype(BF16)
    return high, (x - high.astype(F32)).astype(BF16)


def turn_kernel(v_ref, g_ref, out_ref):
    for tile in range(D // LANES):
        turned = v_ref[:, tile * LANES : (tile + 1) * LANES].T
        start = tile * LANES
        while start < (tile + 1) * LANES:
            part, row = divmod(start, PART)
            size = min(PART - row, (tile + 1) * LANES - start)
            at = start - tile * LANES
            out_ref[part, row : row + size, :] = turned[at : at + size, :]
            start += size
    slots = jnp.broadcast_to(g_ref[...], (ROWS - PART, VEC))
    for part in range(REPS):
        out_ref[part, PART:ROWS, :] = slots


def pack_kernel(cap, in_ref, out_ref, target_ref, left, column):
    groups = OWNERS * cap // PAIR
    before = (iota((VEC, VEC), 0) < iota((VEC, VEC), 1)).astype(F32).astype(BF16)
    carry = jnp.zeros((OWNERS, 1), F32)
    targets = []
    for src in range(REPS):
        slot = in_ref[src, PART : PART + 1, :].astype(jnp.int32)
        owner = slot >> 8
        local = (slot & (SLOTS - 1)) + 1
        hot = (owner == iota((OWNERS, VEC), 0)).astype(F32)
        ahead = jnp.dot(hot.astype(BF16), before, preferred_element_type=F32) + carry
        position = jnp.sum(hot * ahead, axis=0, keepdims=True)
        carry = carry + jnp.sum(hot, axis=1, keepdims=True)
        target = owner.astype(F32) * cap + position
        targets.append(jnp.where(position < cap, target, -1.0))
        high, low = parts_of(in_ref[src, 0:PART, :])
        left[src, 0:PART, :] = high
        left[src, PART : PART + 16, :] = jnp.broadcast_to(local.astype(F32), (16, VEC)).astype(BF16)
        left[src, PART + 16 : STACK, :] = low
    rows = jnp.concatenate(targets, axis=0)
    target_ref[...] = rows.astype(jnp.int32)
    most = jnp.broadcast_to(jnp.max(carry, axis=0, keepdims=True), (8, LANES))
    first_row = iota((8, LANES), 0) == 0
    turned = jnp.concatenate([rows, jnp.zeros((LANES - REPS, VEC), F32)], axis=0).T
    for src in range(REPS):
        column[src] = jnp.broadcast_to(turned[:, src : src + 1], (VEC, LANES))
    lane = iota((VEC, LANES), 1).astype(F32)

    def group(n, _):
        base = (n * PAIR).astype(F32)
        total = jnp.zeros((STACK, PAIR), F32)
        for src in range(REPS):
            at = column[src] - base
            hot = jnp.concatenate(
                [
                    jnp.where(at == lane, 1.0, 0.0).astype(BF16),
                    jnp.where(at == lane + LANES, 1.0, 0.0).astype(BF16),
                ],
                axis=1,
            )
            total = total + jnp.dot(left[src], hot, preferred_element_type=F32)
        values = total[0:PART] + total[PART + 16 : STACK]
        for half in range(2):
            cut = slice(half * LANES, (half + 1) * LANES)
            out_ref[2 * n + half, 0:PART, :] = values[:, cut]
            out_ref[2 * n + half, PART:ROWS, :] = jnp.where(
                first_row, total[PART : PART + 8, cut], most
            )
        return 0

    lax.fori_loop(0, groups, group, 0, unroll=2)


def load_pair(x_ref, n):
    x = jnp.concatenate([x_ref[2 * n, 0:PART, :], x_ref[2 * n + 1, 0:PART, :]], axis=1)
    slot = jnp.concatenate(
        [x_ref[2 * n, PART : PART + 1, :], x_ref[2 * n + 1, PART : PART + 1, :]], axis=1
    )
    return x, slot.astype(jnp.int32)


def stack_of(x):
    high, low = parts_of(x)
    return jnp.concatenate([high, jnp.ones((16, PAIR), BF16), low], axis=0)


def distance_kernel(blocks, x_ref, out_ref, most_ref, total, scaled):
    total[...] = jnp.zeros_like(total)
    most_ref[...] = jnp.max(x_ref[:, PART:ROWS, :], axis=0)

    def add(n, _):
        x, slot = load_pair(x_ref, n)
        hot = jnp.where(iota((SLOTS, PAIR), 0) + 1 == slot, 1.0, 0.0).astype(BF16)
        total[...] += lax.dot_general(stack_of(x), hot, NT, preferred_element_type=F32)
        return 0

    lax.fori_loop(0, blocks // 2, add, 0, unroll=2)
    sums = total[0:PART, :] + total[PART + 16 : STACK, :]
    counts = total[PART : PART + 8, :]
    high, low = parts_of(sums / (counts[0:1] + 1.0))
    high, low = high.astype(F32), low.astype(F32)
    first = high + low
    turned = jnp.concatenate([high, high, low, low], axis=0).T
    scaled[0:SLOTS, :] = (turned[:, 0 : 2 * PART] * -2.0).astype(BF16)
    scaled[SLOTS:, :] = (turned[:, 2 * PART : 4 * PART] * -2.0).astype(BF16)
    own = jnp.broadcast_to(jnp.sum(first * first, axis=0, keepdims=True), (LANES, SLOTS))
    row = iota((LANES, SLOTS), 0)
    columns = jnp.where(row == 0, jnp.broadcast_to(counts[0:1], (LANES, SLOTS)), own).T
    count = columns[:, 0:1].reshape(PAR_DEV, K, 1)
    mean = jnp.sum(count, axis=1, keepdims=True) / K
    extra = (0.5 * count / (mean + 1.0)).reshape(SLOTS, 1) / REPS
    own = columns[:, 1:2]

    def measure(n, _):
        x, slot = load_pair(x_ref, n)
        both = jnp.dot(
            scaled[...], jnp.concatenate(parts_of(x), axis=0), preferred_element_type=F32
        )
        cross = both[0:SLOTS] + both[SLOTS : 2 * SLOTS]
        parent = (slot - 1) >> 3
        terms = ((cross + own) / D + extra).reshape(PAR_DEV, K, PAIR)
        picked = jnp.where(iota((PAR_DEV, K, PAIR), 0) == parent[None], terms, 0.0)
        part = jnp.sum(picked, axis=0) + jnp.sum(x * x, axis=0, keepdims=True) / D
        out_ref[2 * n] = part[:, 0:LANES]
        out_ref[2 * n + 1] = part[:, LANES:PAIR]
        return 0

    lax.fori_loop(0, blocks // 2, measure, 0, unroll=2)


def share_kernel(blocks, x_ref, pen_ref, cent_ref, share_ref, total, rest):
    total[...] = jnp.zeros_like(total)
    rest[...] = jnp.zeros_like(rest)

    def add(n, _):
        x, slot = load_pair(x_ref, n)
        grown = 1.0 + jnp.concatenate([pen_ref[2 * n], pen_ref[2 * n + 1]], axis=1)
        square = grown * grown
        weight = 1.0 / (square * square)
        share = weight / jnp.sum(weight, axis=0, keepdims=True)
        share = jnp.where(slot > 0, share, 0.0)
        share_ref[2 * n] = share[:, 0:LANES]
        share_ref[2 * n + 1] = share[:, LANES:PAIR]
        parent = (slot - 1) >> 3
        mixing = jnp.where(
            iota((PAR_DEV, K, PAIR), 0) == parent[None], share[None], 0.0
        ).reshape(SLOTS, PAIR)
        high, low = parts_of(mixing)
        left = stack_of(x)
        total[...] += lax.dot_general(left, high, NT, preferred_element_type=F32)
        rest[...] += lax.dot_general(
            left[0 : PART + 16], low, NT, preferred_element_type=F32
        )
        return 0

    lax.fori_loop(0, blocks // 2, add, 0, unroll=2)
    weighted = total[0:PART, :] + total[PART + 16 : STACK, :] + rest[0:PART, :]
    summed = total[PART : PART + 1, :] + rest[PART : PART + 1, :]
    cent_ref[...] = weighted / (summed + 1.0)


def join_kernel(at_ref, *refs):
    *pieces, out_ref, whole = refs
    x, core = at_ref[0], at_ref[1]
    for index, piece in enumerate(pieces):
        step, other = divmod(index, 2)
        where = ((x - step) & 3) * 2 + (core ^ other)
        whole[pl.ds(pl.multiple_of(where * PART, 8), PART), :] = piece[...]
    for tile in range(D // LANES):
        cut = slice(tile * LANES, (tile + 1) * LANES)
        out_ref[:, cut] = whole[cut, :].T


def take_kernel(blocks, at_ref, back_ref, target_ref, out_ref):
    target = target_ref[pl.ds(at_ref[2], 1), :]
    total = jnp.zeros((3 * K, VEC), F32)
    for n in range(blocks):
        hot = jnp.where(iota((LANES, VEC), 0) + n * LANES == target, 1.0, 0.0).astype(BF16)
        high, low = parts_of(back_ref[n])
        least = (back_ref[n] - high.astype(F32) - low.astype(F32)).astype(BF16)
        left = jnp.concatenate([high.astype(F32), low.astype(F32), least.astype(F32)], axis=0)
        total = total + jnp.dot(left.astype(BF16), hot, preferred_element_type=F32)
    out_ref[...] = total[0:K] + total[K : 2 * K] + total[2 * K : 3 * K]


def shape(*dims, kind=F32):
    return jax.ShapeDtypeStruct(dims, kind)


def cost(flops, data):
    return pl.CostEstimate(flops=flops, bytes_accessed=data, transcendentals=0)


def along_x(step):
    return [(i, ((i // 2 + step) % 4) * 2 + i % 2) for i in range(REPS)]


CORES = [(i, i ^ 1) for i in range(REPS)]


def sum_over_rep(x):
    x = x + lax.ppermute(x, "rep", CORES)
    x = x + lax.ppermute(x, "rep", [(i, i ^ 2) for i in range(REPS)])
    return x + lax.ppermute(x, "rep", [(i, i ^ 6) for i in range(REPS)])


def refine(cap, got):
    blocks = OWNERS * cap // LANES
    packed, target = pl.pallas_call(
        functools.partial(pack_kernel, cap),
        out_shape=(
            shape(blocks, ROWS, LANES),
            shape(REPS, VEC, kind=jnp.int32),
        ),
        scratch_shapes=[pltpu.VMEM((REPS, STACK, VEC), BF16), pltpu.VMEM((REPS, VEC, LANES), F32)],
        compiler_params=params(),
        cost_estimate=cost(2 * STACK * 2048 * OWNERS * cap, 3_000_000),
        name="pack",
    )(got)
    per = cap // LANES
    rows = lax.all_to_all(
        packed.reshape(OWNERS, per * ROWS, LANES), "cluster", 0, 0, tiled=True
    ).reshape(blocks, ROWS, LANES)
    partial, most = pl.pallas_call(
        functools.partial(distance_kernel, blocks),
        out_shape=(shape(blocks, K, LANES), shape(8, LANES)),
        scratch_shapes=[
            pltpu.VMEM((STACK, SLOTS), F32),
            pltpu.VMEM((2 * SLOTS, 2 * PART), BF16),
        ],
        compiler_params=params(),
        cost_estimate=cost(2 * 8 * PART * SLOTS * OWNERS * cap, 2_000_000),
        name="distance",
    )(rows)
    pen = sum_over_rep(partial)
    cent, share = pl.pallas_call(
        functools.partial(share_kernel, blocks),
        out_shape=(shape(PART, SLOTS), shape(blocks, K, LANES)),
        scratch_shapes=[
            pltpu.VMEM((STACK, SLOTS), F32),
            pltpu.VMEM((PART + 16, SLOTS), F32),
        ],
        compiler_params=params(),
        cost_estimate=cost(2 * 3 * PART * SLOTS * OWNERS * cap, 2_000_000),
        name="share",
    )(rows, pen)
    back = lax.all_to_all(
        share.reshape(OWNERS, per * K, LANES), "cluster", 0, 0, tiled=True
    ).reshape(blocks, K, LANES)
    pieces = []
    for step in range(4):
        mine = lax.ppermute(cent, "rep", along_x(step)) if step else cent
        pieces += [mine, lax.ppermute(mine, "rep", CORES)]
    return pieces, back, target, most


def finish(cap, pieces, back, target):
    blocks = OWNERS * cap // LANES
    rep = lax.axis_index("rep")
    at = jnp.stack([rep // 2, rep % 2, rep]).astype(jnp.int32)
    smem = pl.BlockSpec(memory_space=pltpu.SMEM)
    vmem = pl.BlockSpec(memory_space=pltpu.VMEM)
    centroids = pl.pallas_call(
        join_kernel,
        out_shape=shape(SLOTS, D),
        in_specs=[smem] + [vmem] * REPS,
        scratch_shapes=[pltpu.VMEM((D, SLOTS), F32)],
        compiler_params=params(),
        cost_estimate=cost(0, 1_600_000),
        name="join",
    )(at, *pieces)
    shares = pl.pallas_call(
        functools.partial(take_kernel, blocks),
        out_shape=shape(K, VEC),
        in_specs=[smem, vmem, vmem],
        compiler_params=params(),
        cost_estimate=cost(2 * 24 * VEC * OWNERS * cap, 200_000),
        name="take",
    )(at, back, target)
    return centroids, shares


def on_device(vectors, parent_id, child_id):
    slot = (parent_id * K + child_id).astype(F32).reshape(1, VEC)
    turned = pl.pallas_call(
        turn_kernel,
        out_shape=shape(REPS, ROWS, VEC),
        compiler_params=params(),
        cost_estimate=cost(0, 1_600_000),
        name="turn",
    )(vectors, slot)
    got = lax.all_to_all(turned, "rep", 0, 0, tiled=True)
    pieces, back, target, most = refine(LANES, got)
    over = most[1, 0] > LANES

    def wide(got, pieces, back, target):
        pieces, back, target, _ = refine(PAIR, got)
        return finish(PAIR, pieces, back, target)

    def narrow(got, pieces, back, target):
        return finish(LANES, pieces, back, target)

    centroids, shares = lax.cond(over, wide, narrow, got, pieces, back, target)
    return centroids, shares.T


def solution(mesh):
    in_specs = (P(("cluster", "rep"), None), P(("cluster", "rep")), P(("cluster", "rep")))
    out_specs = (P("cluster", None), P(("cluster", "rep"), None))
    return jax.shard_map(
        on_device, mesh=mesh, in_specs=in_specs, out_specs=out_specs, check_vma=False
    )
```

```python
import functools

import jax
import jax.numpy as jnp
from jax import lax
from jax.experimental import pallas as pl
from jax.experimental.pallas import tpu as pltpu
from jax.sharding import PartitionSpec as P

K = 8
PAR_DEV = 32
OWNERS = 32
DEPTH = 8
WIDTH = 4
REPS = 8
SLOTS = PAR_DEV * K
D = 768
PART = D // REPS
ROWS = PART + 8
VEC = 256
LANES = 128
PAIR = 2 * LANES
STACK = PART + 16 + PART
F32 = jnp.float32
BF16 = jnp.bfloat16
NT = (((1,), (1,)), ((), ()))


def params():
    return pltpu.CompilerParams(vmem_limit_bytes=48 * 2**20)


def iota(shape, dim):
    return lax.broadcasted_iota(jnp.int32, shape, dim)


def parts_of(x):
    high = x.astype(BF16)
    return high, (x - high.astype(F32)).astype(BF16)


def turn_kernel(v_ref, g_ref, out_ref):
    for tile in range(D // LANES):
        turned = v_ref[:, tile * LANES : (tile + 1) * LANES].T
        start = tile * LANES
        while start < (tile + 1) * LANES:
            part, row = divmod(start, PART)
            size = min(PART - row, (tile + 1) * LANES - start)
            at = start - tile * LANES
            out_ref[part, row : row + size, :] = turned[at : at + size, :]
            start += size
    slots = jnp.broadcast_to(g_ref[...], (ROWS - PART, VEC))
    for part in range(REPS):
        out_ref[part, PART:ROWS, :] = slots


def pack_first_kernel(cap, at_ref, in_ref, out_ref, target_ref, most_ref, left, column):
    before = (iota((VEC, VEC), 0) < iota((VEC, VEC), 1)).astype(F32).astype(BF16)
    carry = jnp.zeros((OWNERS, 1), F32)
    targets, places = [], []
    for src in range(REPS):
        slot = in_ref[src, PART : PART + 1, :].astype(jnp.int32)
        owner = slot >> 8
        local = (slot & (SLOTS - 1)) + 1
        hot = (owner == iota((OWNERS, VEC), 0)).astype(F32)
        ahead = jnp.dot(hot.astype(BF16), before, preferred_element_type=F32) + carry
        position = jnp.sum(hot * ahead, axis=0, keepdims=True)
        carry = carry + jnp.sum(hot, axis=1, keepdims=True)
        far = ((owner >> 2) - at_ref[0]) & (DEPTH - 1)
        order = ((owner & (WIDTH - 1)) - at_ref[1] - 1) & (WIDTH - 1)
        block = ((order >> 1) * DEPTH + far) * 2 + (order & 1)
        fits = position < cap
        targets.append(jnp.where(fits, owner.astype(F32) * cap + position, -1.0))
        places.append(jnp.where(fits, block.astype(F32) * cap + position, -1.0))
        high, low = parts_of(in_ref[src, 0:PART, :])
        left[src, 0:PART, :] = high
        left[src, PART : PART + 16, :] = jnp.broadcast_to(local.astype(F32), (16, VEC)).astype(BF16)
        left[src, PART + 16 : STACK, :] = low
    target_ref[...] = jnp.concatenate(targets, axis=0).astype(jnp.int32)
    most_ref[...] = jnp.broadcast_to(jnp.max(carry, axis=0, keepdims=True), (8, LANES))
    turned = jnp.concatenate(places + [jnp.zeros((LANES - REPS, VEC), F32)], axis=0).T
    for src in range(REPS):
        column[src] = jnp.broadcast_to(turned[:, src : src + 1], (VEC, LANES))
    fill(0, left, column, most_ref, out_ref)


def pack_second_kernel(left, column, most_ref, out_ref):
    fill(out_ref.shape[0] // 2, left, column, most_ref, out_ref)


def fill(start, left, column, most_ref, out_ref):
    lane = iota((VEC, LANES), 1).astype(F32)
    first_row = iota((8, LANES), 0) == 0

    def group(n, _):
        base = ((n + start) * PAIR).astype(F32)
        total = jnp.zeros((STACK, PAIR), F32)
        for src in range(REPS):
            at = column[src] - base
            hot = jnp.concatenate(
                [
                    jnp.where(at == lane, 1.0, 0.0).astype(BF16),
                    jnp.where(at == lane + LANES, 1.0, 0.0).astype(BF16),
                ],
                axis=1,
            )
            total = total + jnp.dot(left[src], hot, preferred_element_type=F32)
        values = total[0:PART] + total[PART + 16 : STACK]
        for half in range(2):
            cut = slice(half * LANES, (half + 1) * LANES)
            out_ref[2 * n + half, 0:PART, :] = values[:, cut]
            out_ref[2 * n + half, PART:ROWS, :] = jnp.where(
                first_row, total[PART : PART + 8, cut], most_ref[...]
            )
        return 0

    lax.fori_loop(0, out_ref.shape[0] // 2, group, 0, unroll=2)


def load_pair(x_ref, n):
    x = jnp.concatenate([x_ref[2 * n, 0:PART, :], x_ref[2 * n + 1, 0:PART, :]], axis=1)
    slot = jnp.concatenate(
        [x_ref[2 * n, PART : PART + 1, :], x_ref[2 * n + 1, PART : PART + 1, :]], axis=1
    )
    return x, slot.astype(jnp.int32)


def stack_of(x):
    high, low = parts_of(x)
    return jnp.concatenate([high, jnp.ones((16, PAIR), BF16), low], axis=0)


def distance_kernel(*refs):
    *x_refs, out_ref, most_ref, total, scaled = refs
    blocks = x_refs[0].shape[0]
    total[...] = jnp.zeros_like(total)
    most = jnp.max(x_refs[0][:, PART:ROWS, :], axis=0)
    for x_ref in x_refs:
        most = jnp.maximum(most, jnp.max(x_ref[:, PART:ROWS, :], axis=0))

        def add(n, _, x_ref=x_ref):
            x, slot = load_pair(x_ref, n)
            hot = jnp.where(iota((SLOTS, PAIR), 0) + 1 == slot, 1.0, 0.0).astype(BF16)
            total[...] += lax.dot_general(stack_of(x), hot, NT, preferred_element_type=F32)
            return 0

        lax.fori_loop(0, blocks // 2, add, 0, unroll=2)
    most_ref[...] = most
    sums = total[0:PART, :] + total[PART + 16 : STACK, :]
    counts = total[PART : PART + 8, :]
    high, low = parts_of(sums / (counts[0:1] + 1.0))
    high, low = high.astype(F32), low.astype(F32)
    first = high + low
    turned = jnp.concatenate([high, high, low, low], axis=0).T
    scaled[0:SLOTS, :] = (turned[:, 0 : 2 * PART] * -2.0).astype(BF16)
    scaled[SLOTS:, :] = (turned[:, 2 * PART : 4 * PART] * -2.0).astype(BF16)
    own = jnp.broadcast_to(jnp.sum(first * first, axis=0, keepdims=True), (LANES, SLOTS))
    row = iota((LANES, SLOTS), 0)
    columns = jnp.where(row == 0, jnp.broadcast_to(counts[0:1], (LANES, SLOTS)), own).T
    count = columns[:, 0:1].reshape(PAR_DEV, K, 1)
    mean = jnp.sum(count, axis=1, keepdims=True) / K
    extra = (0.5 * count / (mean + 1.0)).reshape(SLOTS, 1) / REPS
    own = columns[:, 1:2]

    for index, x_ref in enumerate(x_refs):

        def measure(n, _, base=index * blocks, x_ref=x_ref):
            x, slot = load_pair(x_ref, n)
            both = jnp.dot(
                scaled[...], jnp.concatenate(parts_of(x), axis=0), preferred_element_type=F32
            )
            cross = both[0:SLOTS] + both[SLOTS : 2 * SLOTS]
            parent = (slot - 1) >> 3
            terms = ((cross + own) / D + extra).reshape(PAR_DEV, K, PAIR)
            picked = jnp.where(iota((PAR_DEV, K, PAIR), 0) == parent[None], terms, 0.0)
            part = jnp.sum(picked, axis=0) + jnp.sum(x * x, axis=0, keepdims=True) / D
            out_ref[base + 2 * n] = part[:, 0:LANES]
            out_ref[base + 2 * n + 1] = part[:, LANES:PAIR]
            return 0

        lax.fori_loop(0, blocks // 2, measure, 0, unroll=2)


def share_kernel(per, at_ref, pen_ref, *refs):
    *x_refs, cent_ref, share_ref, total, rest = refs
    blocks = DEPTH * per
    total[...] = jnp.zeros_like(total)
    rest[...] = jnp.zeros_like(rest)
    for index, x_ref in enumerate(x_refs):

        def add(n, _, index=index, x_ref=x_ref):
            x, slot = load_pair(x_ref, n)
            base = index * blocks + 2 * n
            grown = 1.0 + jnp.concatenate([pen_ref[base], pen_ref[base + 1]], axis=1)
            square = grown * grown
            weight = 1.0 / (square * square)
            share = weight / jnp.sum(weight, axis=0, keepdims=True)
            share = jnp.where(slot > 0, share, 0.0)
            for half in range(2):
                block = 2 * n + half
                z = (at_ref[0] - block // per) & (DEPTH - 1)
                y = (at_ref[1] - index - 1) & (WIDTH - 1)
                cut = slice(half * LANES, (half + 1) * LANES)
                share_ref[(z * WIDTH + y) * per + block % per] = share[:, cut]
            parent = (slot - 1) >> 3
            mixing = jnp.where(
                iota((PAR_DEV, K, PAIR), 0) == parent[None], share[None], 0.0
            ).reshape(SLOTS, PAIR)
            high, low = parts_of(mixing)
            left = stack_of(x)
            total[...] += lax.dot_general(left, high, NT, preferred_element_type=F32)
            rest[...] += lax.dot_general(
                left[0 : PART + 16], low, NT, preferred_element_type=F32
            )
            return 0

        lax.fori_loop(0, blocks // 2, add, 0, unroll=2)
    weighted = total[0:PART, :] + total[PART + 16 : STACK, :] + rest[0:PART, :]
    summed = total[PART : PART + 1, :] + rest[PART : PART + 1, :]
    cent_ref[...] = weighted / (summed + 1.0)


def join_kernel(at_ref, *refs):
    *pieces, out_ref, whole = refs
    x, core = at_ref[2] >> 1, at_ref[2] & 1
    for index, piece in enumerate(pieces):
        step, other = divmod(index, 2)
        where = ((x - step) & 3) * 2 + (core ^ other)
        whole[pl.ds(pl.multiple_of(where * PART, 8), PART), :] = piece[...]
    for tile in range(D // LANES):
        cut = slice(tile * LANES, (tile + 1) * LANES)
        out_ref[:, cut] = whole[cut, :].T


def take_kernel(blocks, at_ref, back_ref, target_ref, out_ref):
    target = target_ref[pl.ds(at_ref[2], 1), :]
    total = jnp.zeros((3 * K, VEC), F32)
    for n in range(blocks):
        hot = jnp.where(iota((LANES, VEC), 0) + n * LANES == target, 1.0, 0.0).astype(BF16)
        high, low = parts_of(back_ref[n])
        least = (back_ref[n] - high.astype(F32) - low.astype(F32)).astype(BF16)
        left = jnp.concatenate([high.astype(F32), low.astype(F32), least.astype(F32)], axis=0)
        total = total + jnp.dot(left.astype(BF16), hot, preferred_element_type=F32)
    out_ref[...] = total[0:K] + total[K : 2 * K] + total[2 * K : 3 * K]


def shape(*dims, kind=F32):
    return jax.ShapeDtypeStruct(dims, kind)


def cost(flops, data):
    return pl.CostEstimate(flops=flops, bytes_accessed=data, transcendentals=0)


def along_x(step):
    return [(i, ((i // 2 + step) % 4) * 2 + i % 2) for i in range(REPS)]


CORES = [(i, i ^ 1) for i in range(REPS)]


def sum_over_rep(x):
    x = x + lax.ppermute(x, "rep", CORES)
    x = x + lax.ppermute(x, "rep", [(i, i ^ 2) for i in range(REPS)])
    return x + lax.ppermute(x, "rep", [(i, i ^ 6) for i in range(REPS)])


def along(dz, dy):
    return [
        (z * WIDTH + y, (z + dz) % DEPTH * WIDTH + (y + dy) % WIDTH)
        for z in range(DEPTH)
        for y in range(WIDTH)
    ]


def place():
    cluster = lax.axis_index("cluster")
    return jnp.stack([cluster // WIDTH, cluster % WIDTH, lax.axis_index("rep")]).astype(jnp.int32)


def over_depth(packed, per):
    mine = packed.reshape(DEPTH, 2 * per, ROWS, LANES)
    got = [mine[0]] + [None] * (DEPTH - 1)
    for dz in (4, 3, 5, 2, 6, 1, 7):
        got[dz] = lax.ppermute(mine[dz], "cluster", along(dz, 0))
    return [
        jnp.concatenate([part[half * per : (half + 1) * per] for part in got], axis=0)
        for half in range(2)
    ]


SMEM = pl.BlockSpec(memory_space=pltpu.SMEM)
VMEM = pl.BlockSpec(memory_space=pltpu.VMEM)


def refine(cap, got):
    per = cap // LANES
    blocks = OWNERS * per
    at = place()
    packed, target, most, left, column = pl.pallas_call(
        functools.partial(pack_first_kernel, cap),
        out_shape=(
            shape(blocks // 2, ROWS, LANES),
            shape(REPS, VEC, kind=jnp.int32),
            shape(8, LANES),
            shape(REPS, STACK, VEC, kind=BF16),
            shape(REPS, VEC, LANES),
        ),
        in_specs=[SMEM, VMEM],
        compiler_params=params(),
        cost_estimate=cost(STACK * 2048 * OWNERS * cap, 3_000_000),
        name="pack_first",
    )(at, got)
    early = over_depth(packed, per)
    packed = pl.pallas_call(
        pack_second_kernel,
        out_shape=shape(blocks // 2, ROWS, LANES),
        compiler_params=params(),
        cost_estimate=cost(STACK * 2048 * OWNERS * cap, 3_000_000),
        name="pack_second",
    )(left, column, most)
    late = over_depth(packed, per)
    rows = [
        lax.ppermute(early[0], "cluster", along(0, 1)),
        lax.ppermute(early[1], "cluster", along(0, 2)),
        lax.ppermute(late[0], "cluster", along(0, 3)),
        late[1],
    ]
    partial, most = pl.pallas_call(
        distance_kernel,
        out_shape=(shape(blocks, K, LANES), shape(8, LANES)),
        scratch_shapes=[
            pltpu.VMEM((STACK, SLOTS), F32),
            pltpu.VMEM((2 * SLOTS, 2 * PART), BF16),
        ],
        compiler_params=params(),
        cost_estimate=cost(2 * 8 * PART * SLOTS * OWNERS * cap, 2_000_000),
        name="distance",
    )(*rows)
    pen = sum_over_rep(partial)
    cent, share = pl.pallas_call(
        functools.partial(share_kernel, per),
        out_shape=(shape(PART, SLOTS), shape(blocks, K, LANES)),
        in_specs=[SMEM] + [VMEM] * (1 + WIDTH),
        scratch_shapes=[
            pltpu.VMEM((STACK, SLOTS), F32),
            pltpu.VMEM((PART + 16, SLOTS), F32),
        ],
        compiler_params=params(),
        cost_estimate=cost(2 * 3 * PART * SLOTS * OWNERS * cap, 2_000_000),
        name="share",
    )(at, pen, *rows)
    back = lax.all_to_all(
        share.reshape(OWNERS, per * K, LANES), "cluster", 0, 0, tiled=True
    ).reshape(blocks, K, LANES)
    pieces = []
    for step in range(4):
        mine = lax.ppermute(cent, "rep", along_x(step)) if step else cent
        pieces += [mine, lax.ppermute(mine, "rep", CORES)]
    return pieces, back, target, most


def finish(cap, pieces, back, target):
    blocks = OWNERS * cap // LANES
    at = place()
    centroids = pl.pallas_call(
        join_kernel,
        out_shape=shape(SLOTS, D),
        in_specs=[SMEM] + [VMEM] * REPS,
        scratch_shapes=[pltpu.VMEM((D, SLOTS), F32)],
        compiler_params=params(),
        cost_estimate=cost(0, 1_600_000),
        name="join",
    )(at, *pieces)
    shares = pl.pallas_call(
        functools.partial(take_kernel, blocks),
        out_shape=shape(K, VEC),
        in_specs=[SMEM, VMEM, VMEM],
        compiler_params=params(),
        cost_estimate=cost(2 * 24 * VEC * OWNERS * cap, 200_000),
        name="take",
    )(at, back, target)
    return centroids, shares


def on_device(vectors, parent_id, child_id):
    slot = (parent_id * K + child_id).astype(F32).reshape(1, VEC)
    turned = pl.pallas_call(
        turn_kernel,
        out_shape=shape(REPS, ROWS, VEC),
        compiler_params=params(),
        cost_estimate=cost(0, 1_600_000),
        name="turn",
    )(vectors, slot)
    got = lax.all_to_all(turned, "rep", 0, 0, tiled=True)
    pieces, back, target, most = refine(LANES, got)
    over = most[1, 0] > LANES

    def wide(got, pieces, back, target):
        pieces, back, target, _ = refine(PAIR, got)
        return finish(PAIR, pieces, back, target)

    def narrow(got, pieces, back, target):
        return finish(LANES, pieces, back, target)

    centroids, shares = lax.cond(over, wide, narrow, got, pieces, back, target)
    return centroids, shares.T


def solution(mesh):
    in_specs = (P(("cluster", "rep"), None), P(("cluster", "rep")), P(("cluster", "rep")))
    out_specs = (P("cluster", None), P(("cluster", "rep"), None))
    return jax.shard_map(
        on_device, mesh=mesh, in_specs=in_specs, out_specs=out_specs, check_vma=False
    )
```

```python
import functools

import jax
import jax.numpy as jnp
from jax import lax
from jax.experimental import pallas as pl
from jax.experimental.pallas import tpu as pltpu
from jax.sharding import PartitionSpec as P

K = 8
PAR_DEV = 32
OWNERS = 32
REPS = 8
SLOTS = PAR_DEV * K
D = 768
PART = D // REPS
ROWS = PART + 8
VEC = 256
LANES = 128
PAIR = 2 * LANES
STACK = PART + 16 + PART
F32 = jnp.float32
BF16 = jnp.bfloat16
NT = (((1,), (1,)), ((), ()))


def params():
    return pltpu.CompilerParams(vmem_limit_bytes=48 * 2**20)


def iota(shape, dim):
    return lax.broadcasted_iota(jnp.int32, shape, dim)


def parts_of(x):
    high = x.astype(BF16)
    return high, (x - high.astype(F32)).astype(BF16)


def turn_kernel(v_ref, parent_ref, child_ref, out_ref):
    for tile in range(D // LANES):
        turned = v_ref[:, tile * LANES : (tile + 1) * LANES].T
        start = tile * LANES
        while start < (tile + 1) * LANES:
            part, row = divmod(start, PART)
            size = min(PART - row, (tile + 1) * LANES - start)
            at = start - tile * LANES
            out_ref[part, row : row + size, :] = turned[at : at + size, :]
            start += size
    slot = (parent_ref[...] * K + child_ref[...]).astype(F32)
    slots = jnp.broadcast_to(slot, (ROWS - PART, VEC))
    for part in range(REPS):
        out_ref[part, PART:ROWS, :] = slots


def pack_kernel(cap, in_ref, out_ref, target_ref, left, hot, group_of):
    groups = OWNERS * cap // PAIR
    before = (iota((VEC, VEC), 0) < iota((VEC, VEC), 1)).astype(F32).astype(BF16)
    carry = jnp.zeros((OWNERS, 1), F32)
    targets = []
    for src in range(REPS):
        slot = in_ref[src, PART : PART + 1, :].astype(jnp.int32)
        owner = slot >> 8
        local = (slot & (SLOTS - 1)) + 1
        mine = (owner == iota((OWNERS, VEC), 0)).astype(F32)
        ahead = jnp.dot(mine.astype(BF16), before, preferred_element_type=F32) + carry
        position = jnp.sum(mine * ahead, axis=0, keepdims=True)
        carry = carry + jnp.sum(mine, axis=1, keepdims=True)
        target = owner * cap + position.astype(jnp.int32)
        target = jnp.where(position < cap, target, -1)
        targets.append(target)
        group_of[src] = jnp.broadcast_to(target >> 8, (16, VEC))
        high, low = parts_of(in_ref[src, 0:PART, :])
        left[src, 0:PART, :] = high
        left[src, PART : PART + 16, :] = jnp.broadcast_to(local.astype(F32), (16, VEC)).astype(BF16)
        left[src, PART + 16 : STACK, :] = low
    rows = jnp.concatenate(targets, axis=0)
    target_ref[...] = rows
    most = jnp.broadcast_to(jnp.max(carry, axis=0, keepdims=True), (8, LANES))
    first_row = iota((8, LANES), 0) == 0
    inside = (rows & (PAIR - 1)).astype(F32)
    turned = jnp.concatenate([inside, jnp.zeros((LANES - REPS, VEC), F32)], axis=0).T
    lane = iota((VEC, PAIR), 1).astype(F32)
    for src in range(REPS):
        hot[src] = jnp.where(turned[:, src : src + 1] == lane, 1.0, 0.0).astype(BF16)

    def group(n, _):
        total = jnp.zeros((STACK, PAIR), F32)
        for src in range(REPS):
            keep = jnp.where(group_of[src] == n, 1.0, 0.0).astype(BF16)
            kept = left[src] * jnp.concatenate([keep] * (STACK // 16), axis=0)
            total = total + jnp.dot(kept, hot[src], preferred_element_type=F32)
        values = total[0:PART] + total[PART + 16 : STACK]
        for half in range(2):
            cut = slice(half * LANES, (half + 1) * LANES)
            out_ref[2 * n + half, 0:PART, :] = values[:, cut]
            out_ref[2 * n + half, PART:ROWS, :] = jnp.where(
                first_row, total[PART : PART + 8, cut], most
            )
        return 0

    lax.fori_loop(0, groups, group, 0, unroll=2)


def load_pair(x_ref, n):
    x = jnp.concatenate([x_ref[2 * n, 0:PART, :], x_ref[2 * n + 1, 0:PART, :]], axis=1)
    slot = jnp.concatenate(
        [x_ref[2 * n, PART : PART + 1, :], x_ref[2 * n + 1, PART : PART + 1, :]], axis=1
    )
    return x, slot.astype(jnp.int32)


def stack_of(x):
    high, low = parts_of(x)
    return jnp.concatenate([high, jnp.ones((16, PAIR), BF16), low], axis=0)


def distance_kernel(blocks, x_ref, out_ref, most_ref, total, scaled):
    total[...] = jnp.zeros_like(total)
    most_ref[0] = jnp.max(x_ref[:, PART + 1, :]).astype(jnp.int32)

    def add(n, _):
        x, slot = load_pair(x_ref, n)
        hot = jnp.where(iota((SLOTS, PAIR), 0) + 1 == slot, 1.0, 0.0).astype(BF16)
        total[...] += lax.dot_general(stack_of(x), hot, NT, preferred_element_type=F32)
        return 0

    lax.fori_loop(0, blocks // 2, add, 0, unroll=2)
    sums = total[0:PART, :] + total[PART + 16 : STACK, :]
    counts = total[PART : PART + 8, :]
    high, low = parts_of(sums / (counts[0:1] + 1.0))
    high, low = high.astype(F32), low.astype(F32)
    first = high + low
    turned = jnp.concatenate([high, high, low, low], axis=0).T
    scaled[0:SLOTS, :] = (turned[:, 0 : 2 * PART] * -2.0).astype(BF16)
    scaled[SLOTS:, :] = (turned[:, 2 * PART : 4 * PART] * -2.0).astype(BF16)
    own = jnp.broadcast_to(jnp.sum(first * first, axis=0, keepdims=True), (LANES, SLOTS))
    row = iota((LANES, SLOTS), 0)
    columns = jnp.where(row == 0, jnp.broadcast_to(counts[0:1], (LANES, SLOTS)), own).T
    count = columns[:, 0:1].reshape(PAR_DEV, K, 1)
    mean = jnp.sum(count, axis=1, keepdims=True) / K
    extra = (0.5 * count / (mean + 1.0)).reshape(SLOTS, 1) / REPS
    own = columns[:, 1:2]

    def measure(n, _):
        x, slot = load_pair(x_ref, n)
        both = jnp.dot(
            scaled[...], jnp.concatenate(parts_of(x), axis=0), preferred_element_type=F32
        )
        cross = both[0:SLOTS] + both[SLOTS : 2 * SLOTS]
        parent = (slot - 1) >> 3
        terms = ((cross + own) / D + extra).reshape(PAR_DEV, K, PAIR)
        picked = jnp.where(iota((PAR_DEV, K, PAIR), 0) == parent[None], terms, 0.0)
        part = jnp.sum(picked, axis=0) + jnp.sum(x * x, axis=0, keepdims=True) / D
        out_ref[2 * n] = part[:, 0:LANES]
        out_ref[2 * n + 1] = part[:, LANES:PAIR]
        return 0

    lax.fori_loop(0, blocks // 2, measure, 0, unroll=2)


def share_kernel(blocks, x_ref, pen_ref, cent_ref, share_ref, total, rest):
    total[...] = jnp.zeros_like(total)
    rest[...] = jnp.zeros_like(rest)

    def add(n, _):
        x, slot = load_pair(x_ref, n)
        grown = 1.0 + jnp.concatenate([pen_ref[2 * n], pen_ref[2 * n + 1]], axis=1)
        square = grown * grown
        weight = 1.0 / (square * square)
        share = weight / jnp.sum(weight, axis=0, keepdims=True)
        share = jnp.where(slot > 0, share, 0.0)
        share_ref[2 * n] = share[:, 0:LANES]
        share_ref[2 * n + 1] = share[:, LANES:PAIR]
        parent = (slot - 1) >> 3
        mixing = jnp.where(
            iota((PAR_DEV, K, PAIR), 0) == parent[None], share[None], 0.0
        ).reshape(SLOTS, PAIR)
        high, low = parts_of(mixing)
        left = stack_of(x)
        total[...] += lax.dot_general(left, high, NT, preferred_element_type=F32)
        rest[...] += lax.dot_general(
            left[0 : PART + 16], low, NT, preferred_element_type=F32
        )
        return 0

    lax.fori_loop(0, blocks // 2, add, 0, unroll=2)
    weighted = total[0:PART, :] + total[PART + 16 : STACK, :] + rest[0:PART, :]
    summed = total[PART : PART + 1, :] + rest[PART : PART + 1, :]
    cent_ref[...] = weighted / (summed + 1.0)


def join_kernel(at_ref, own_ref, other_ref, out_ref, whole):
    x, core = at_ref[0], at_ref[1]
    for other, piece in enumerate((own_ref, other_ref)):
        for step in range(4):
            where = ((x - step) & 3) * 2 + (core ^ other)
            whole[pl.ds(pl.multiple_of(where * PART, 8), PART), :] = piece[step]
    for tile in range(D // LANES):
        cut = slice(tile * LANES, (tile + 1) * LANES)
        out_ref[:, cut] = whole[cut, :].T


def take_kernel(blocks, at_ref, back_ref, target_ref, out_ref):
    target = target_ref[pl.ds(at_ref[2], 1), :]
    total = jnp.zeros((3 * K, VEC), F32)
    for n in range(blocks):
        hot = jnp.where(iota((LANES, VEC), 0) + n * LANES == target, 1.0, 0.0).astype(BF16)
        high, low = parts_of(back_ref[n])
        least = (back_ref[n] - high.astype(F32) - low.astype(F32)).astype(BF16)
        left = jnp.concatenate([high.astype(F32), low.astype(F32), least.astype(F32)], axis=0)
        total = total + jnp.dot(left.astype(BF16), hot, preferred_element_type=F32)
    out_ref[...] = total[0:K] + total[K : 2 * K] + total[2 * K : 3 * K]


def shape(*dims, kind=F32):
    return jax.ShapeDtypeStruct(dims, kind)


def cost(flops, data):
    return pl.CostEstimate(flops=flops, bytes_accessed=data, transcendentals=0)


def along_x(step):
    return [(i, ((i // 2 + step) % 4) * 2 + i % 2) for i in range(REPS)]


CORES = [(i, i ^ 1) for i in range(REPS)]


def sum_over_rep(x):
    x = x + lax.ppermute(x, "rep", CORES)
    x = x + lax.ppermute(x, "rep", [(i, i ^ 2) for i in range(REPS)])
    return x + lax.ppermute(x, "rep", [(i, i ^ 6) for i in range(REPS)])


SMEM = pl.BlockSpec(memory_space=pltpu.SMEM)
VMEM = pl.BlockSpec(memory_space=pltpu.VMEM)


def refine(cap, got):
    blocks = OWNERS * cap // LANES
    packed, target = pl.pallas_call(
        functools.partial(pack_kernel, cap),
        out_shape=(
            shape(blocks, ROWS, LANES),
            shape(REPS, VEC, kind=jnp.int32),
        ),
        scratch_shapes=[
            pltpu.VMEM((REPS, STACK, VEC), BF16),
            pltpu.VMEM((REPS, VEC, PAIR), BF16),
            pltpu.VMEM((REPS, 16, VEC), jnp.int32),
        ],
        compiler_params=params(),
        cost_estimate=cost(2 * STACK * 2048 * OWNERS * cap, 3_000_000),
        name="pack",
    )(got)
    per = cap // LANES
    rows = lax.all_to_all(
        packed.reshape(OWNERS, per * ROWS, LANES), "cluster", 0, 0, tiled=True
    ).reshape(blocks, ROWS, LANES)
    partial, most = pl.pallas_call(
        functools.partial(distance_kernel, blocks),
        out_shape=(shape(blocks, K, LANES), shape(1, kind=jnp.int32)),
        out_specs=(VMEM, SMEM),
        scratch_shapes=[
            pltpu.VMEM((STACK, SLOTS), F32),
            pltpu.VMEM((2 * SLOTS, 2 * PART), BF16),
        ],
        compiler_params=params(),
        cost_estimate=cost(2 * 8 * PART * SLOTS * OWNERS * cap, 2_000_000),
        name="distance",
    )(rows)
    pen = sum_over_rep(partial)
    cent, share = pl.pallas_call(
        functools.partial(share_kernel, blocks),
        out_shape=(shape(PART, SLOTS), shape(blocks, K, LANES)),
        scratch_shapes=[
            pltpu.VMEM((STACK, SLOTS), F32),
            pltpu.VMEM((PART + 16, SLOTS), F32),
        ],
        compiler_params=params(),
        cost_estimate=cost(2 * 3 * PART * SLOTS * OWNERS * cap, 2_000_000),
        name="share",
    )(rows, pen)
    back = lax.all_to_all(
        share.reshape(OWNERS, per * K, LANES), "cluster", 0, 0, tiled=True
    ).reshape(blocks, K, LANES)
    line = jnp.stack([cent] + [lax.ppermute(cent, "rep", along_x(step)) for step in (1, 2, 3)])
    pieces = [line, lax.ppermute(line, "rep", CORES)]
    return pieces, back, target, most


def place():
    rep = lax.axis_index("rep")
    return jnp.stack([rep // 2, rep % 2, rep]).astype(jnp.int32)


def join(pieces):
    return pl.pallas_call(
        join_kernel,
        out_shape=shape(SLOTS, D),
        in_specs=[SMEM, VMEM, VMEM],
        scratch_shapes=[pltpu.VMEM((D, SLOTS), F32)],
        compiler_params=params(),
        cost_estimate=cost(0, 1_600_000),
        name="join",
    )(place(), *pieces)


def take(cap, back, target):
    blocks = OWNERS * cap // LANES
    return pl.pallas_call(
        functools.partial(take_kernel, blocks),
        out_shape=shape(K, VEC),
        in_specs=[SMEM, VMEM, VMEM],
        compiler_params=params(),
        cost_estimate=cost(2 * 24 * VEC * OWNERS * cap, 200_000),
        name="take",
    )(place(), back, target)


def on_device(vectors, parent_id, child_id):
    turned = pl.pallas_call(
        turn_kernel,
        out_shape=shape(REPS, ROWS, VEC),
        compiler_params=params(),
        cost_estimate=cost(0, 1_600_000),
        name="turn",
    )(vectors, parent_id.reshape(1, VEC), child_id.reshape(1, VEC))
    got = lax.all_to_all(turned, "rep", 0, 0, tiled=True)
    pieces, back, target, most = refine(LANES, got)
    over = most[0] > LANES

    picked = take(LANES, back, target)

    def wide(got, pieces, picked):
        pieces, back, target, _ = refine(PAIR, got)
        return join(pieces), take(PAIR, back, target)

    def narrow(got, pieces, picked):
        return join(pieces), picked

    centroids, shares = lax.cond(over, wide, narrow, got, pieces, picked)
    return centroids, shares.T


def solution(mesh):
    in_specs = (P(("cluster", "rep"), None), P(("cluster", "rep")), P(("cluster", "rep")))
    out_specs = (P("cluster", None), P(("cluster", "rep"), None))
    return jax.shard_map(
        on_device, mesh=mesh, in_specs=in_specs, out_specs=out_specs, check_vma=False
    )
```

```python
import functools

import jax
import jax.numpy as jnp
from jax import lax
from jax.experimental import pallas as pl
from jax.experimental.pallas import tpu as pltpu
from jax.sharding import PartitionSpec as P

K = 8
PAR_DEV = 32
OWNERS = 32
REPS = 8
SLOTS = PAR_DEV * K
D = 768
PART = D // REPS
EARLY = 32
LATE = PART - EARLY
ROWS = EARLY + 8
VEC = 256
LANES = 128
PAIR = 2 * LANES
STACK = PART + 16 + PART
F32 = jnp.float32
BF16 = jnp.bfloat16
NT = (((1,), (1,)), ((), ()))


def params():
    return pltpu.CompilerParams(vmem_limit_bytes=48 * 2**20)


def iota(shape, dim):
    return lax.broadcasted_iota(jnp.int32, shape, dim)


def parts_of(x):
    high = x.astype(BF16)
    return high, (x - high.astype(F32)).astype(BF16)


def turn_kernel(at_ref, v_ref, slot_ref, early_ref, late_ref):
    for tile in range(D // LANES):
        turned = v_ref[:, tile * LANES : (tile + 1) * LANES].T
        for start in range(0, LANES, EARLY):
            part, row = divmod(tile * LANES + start, PART)
            piece = turned[start : start + EARLY, :]
            if row < EARLY:
                early_ref[part, 0:EARLY, :] = piece
            else:
                step = (part - at_ref[2]) & (REPS - 1)
                late_ref[step, row - EARLY : row, :] = piece
    slots = jnp.broadcast_to(slot_ref[...], (ROWS - EARLY, VEC))
    for part in range(REPS):
        early_ref[part, EARLY:ROWS, :] = slots


def pack_early_kernel(cap, in_ref, out_ref, target_ref, hot, group_of, left):
    before = (iota((VEC, VEC), 0) < iota((VEC, VEC), 1)).astype(F32).astype(BF16)
    carry = jnp.zeros((OWNERS, 1), F32)
    targets = []
    for src in range(REPS):
        slot = in_ref[src, EARLY : EARLY + 1, :].astype(jnp.int32)
        owner = slot >> 8
        local = (slot & (SLOTS - 1)) + 1
        mine = (owner == iota((OWNERS, VEC), 0)).astype(F32)
        ahead = jnp.dot(mine.astype(BF16), before, preferred_element_type=F32) + carry
        position = jnp.sum(mine * ahead, axis=0, keepdims=True)
        carry = carry + jnp.sum(mine, axis=1, keepdims=True)
        target = owner * cap + position.astype(jnp.int32)
        target = jnp.where(position < cap, target, -1)
        targets.append(target)
        group_of[src] = jnp.broadcast_to(target >> 8, (16, VEC))
        high, low = parts_of(in_ref[src, 0:EARLY, :])
        slots = jnp.broadcast_to(local.astype(F32), (16, VEC)).astype(BF16)
        left[src] = jnp.concatenate([high, low, slots], axis=0)
    rows = jnp.concatenate(targets, axis=0)
    target_ref[...] = rows
    most = jnp.broadcast_to(jnp.max(carry, axis=0, keepdims=True), (8, LANES))
    first_row = iota((8, LANES), 0) == 0
    inside = (rows & (PAIR - 1)).astype(F32)
    turned = jnp.concatenate([inside, jnp.zeros((LANES - REPS, VEC), F32)], axis=0).T
    lane = iota((VEC, PAIR), 1).astype(F32)
    for src in range(REPS):
        hot[src] = jnp.where(turned[:, src : src + 1] == lane, 1.0, 0.0).astype(BF16)

    def group(n, _):
        total = jnp.zeros((2 * EARLY + 16, PAIR), F32)
        for src in range(REPS):
            total = total + picked(left[src], group_of[src], n, hot[src])
        values = total[0:EARLY] + total[EARLY : 2 * EARLY]
        slots = total[2 * EARLY : 2 * EARLY + 8]
        for half in range(2):
            cut = slice(half * LANES, (half + 1) * LANES)
            out_ref[2 * n + half, 0:EARLY, :] = values[:, cut]
            out_ref[2 * n + half, EARLY:ROWS, :] = jnp.where(first_row, slots[:, cut], most)
        return 0

    lax.fori_loop(0, OWNERS * cap // PAIR, group, 0, unroll=2)


def picked(left, group_of, n, hot):
    keep = jnp.where(group_of == n, 1.0, 0.0).astype(BF16)
    kept = left * jnp.concatenate([keep] * (left.shape[0] // 16), axis=0)
    return jnp.dot(kept, hot, preferred_element_type=F32)


def pack_late_kernel(cap, at_ref, hot, group_of, *refs):
    *in_refs, out_ref, left = refs
    for step, in_ref in enumerate(in_refs):
        high, low = parts_of(in_ref[...])
        left[step] = jnp.concatenate([high, low], axis=0)

    def group(n, _):
        total = jnp.zeros((2 * LATE, PAIR), F32)
        for step in range(REPS):
            src = (at_ref[2] - step) & (REPS - 1)
            total = total + picked(left[step], group_of[src], n, hot[src])
        values = total[0:LATE] + total[LATE : 2 * LATE]
        for half in range(2):
            out_ref[2 * n + half] = values[:, half * LANES : (half + 1) * LANES]
        return 0

    lax.fori_loop(0, OWNERS * cap // PAIR, group, 0, unroll=2)


def load_pair(early_ref, late_ref, n):
    pair = (2 * n, 2 * n + 1)
    x = jnp.concatenate(
        [
            jnp.concatenate([early_ref[i, 0:EARLY, :] for i in pair], axis=1),
            jnp.concatenate([late_ref[i] for i in pair], axis=1),
        ],
        axis=0,
    )
    slot = jnp.concatenate([early_ref[i, EARLY : EARLY + 1, :] for i in pair], axis=1)
    return x, slot.astype(jnp.int32)


def stack_of(x):
    high, low = parts_of(x)
    return jnp.concatenate([high, jnp.ones((16, PAIR), BF16), low], axis=0)


def distance_kernel(blocks, early_ref, late_ref, out_ref, most_ref, total, scaled):
    total[...] = jnp.zeros_like(total)
    most_ref[0] = jnp.max(early_ref[:, EARLY + 1, :]).astype(jnp.int32)

    def add(n, _):
        x, slot = load_pair(early_ref, late_ref, n)
        hot = jnp.where(iota((SLOTS, PAIR), 0) + 1 == slot, 1.0, 0.0).astype(BF16)
        total[...] += lax.dot_general(stack_of(x), hot, NT, preferred_element_type=F32)
        return 0

    lax.fori_loop(0, blocks // 2, add, 0, unroll=2)
    sums = total[0:PART, :] + total[PART + 16 : STACK, :]
    counts = total[PART : PART + 8, :]
    high, low = parts_of(sums / (counts[0:1] + 1.0))
    high, low = high.astype(F32), low.astype(F32)
    first = high + low
    turned = jnp.concatenate([high, high, low, low], axis=0).T
    scaled[0:SLOTS, :] = (turned[:, 0 : 2 * PART] * -2.0).astype(BF16)
    scaled[SLOTS:, :] = (turned[:, 2 * PART : 4 * PART] * -2.0).astype(BF16)
    own = jnp.broadcast_to(jnp.sum(first * first, axis=0, keepdims=True), (LANES, SLOTS))
    row = iota((LANES, SLOTS), 0)
    columns = jnp.where(row == 0, jnp.broadcast_to(counts[0:1], (LANES, SLOTS)), own).T
    count = columns[:, 0:1].reshape(PAR_DEV, K, 1)
    mean = jnp.sum(count, axis=1, keepdims=True) / K
    extra = (0.5 * count / (mean + 1.0)).reshape(SLOTS, 1) / REPS
    own = columns[:, 1:2]

    def measure(n, _):
        x, slot = load_pair(early_ref, late_ref, n)
        both = jnp.dot(
            scaled[...], jnp.concatenate(parts_of(x), axis=0), preferred_element_type=F32
        )
        cross = both[0:SLOTS] + both[SLOTS : 2 * SLOTS]
        parent = (slot - 1) >> 3
        terms = ((cross + own) / D + extra).reshape(PAR_DEV, K, PAIR)
        picked = jnp.where(iota((PAR_DEV, K, PAIR), 0) == parent[None], terms, 0.0)
        part = jnp.sum(picked, axis=0) + jnp.sum(x * x, axis=0, keepdims=True) / D
        out_ref[2 * n] = part[:, 0:LANES]
        out_ref[2 * n + 1] = part[:, LANES:PAIR]
        return 0

    lax.fori_loop(0, blocks // 2, measure, 0, unroll=2)


def share_kernel(blocks, early_ref, late_ref, pen_ref, cent_ref, share_ref, total, rest):
    total[...] = jnp.zeros_like(total)
    rest[...] = jnp.zeros_like(rest)

    def add(n, _):
        x, slot = load_pair(early_ref, late_ref, n)
        grown = 1.0 + jnp.concatenate([pen_ref[2 * n], pen_ref[2 * n + 1]], axis=1)
        square = grown * grown
        weight = 1.0 / (square * square)
        share = weight / jnp.sum(weight, axis=0, keepdims=True)
        share = jnp.where(slot > 0, share, 0.0)
        share_ref[2 * n] = share[:, 0:LANES]
        share_ref[2 * n + 1] = share[:, LANES:PAIR]
        parent = (slot - 1) >> 3
        mixing = jnp.where(
            iota((PAR_DEV, K, PAIR), 0) == parent[None], share[None], 0.0
        ).reshape(SLOTS, PAIR)
        high, low = parts_of(mixing)
        left = stack_of(x)
        total[...] += lax.dot_general(left, high, NT, preferred_element_type=F32)
        rest[...] += lax.dot_general(
            left[0 : PART + 16], low, NT, preferred_element_type=F32
        )
        return 0

    lax.fori_loop(0, blocks // 2, add, 0, unroll=2)
    weighted = total[0:PART, :] + total[PART + 16 : STACK, :] + rest[0:PART, :]
    summed = total[PART : PART + 1, :] + rest[PART : PART + 1, :]
    cent_ref[...] = weighted / (summed + 1.0)


def join_kernel(at_ref, *refs):
    *pieces, out_ref, whole = refs
    x, core = at_ref[0], at_ref[1]
    for index, piece in enumerate(pieces):
        step, other = divmod(index, 2)
        where = ((x - step) & 3) * 2 + (core ^ other)
        whole[pl.ds(pl.multiple_of(where * PART, 8), PART), :] = piece[...]
    for tile in range(D // LANES):
        cut = slice(tile * LANES, (tile + 1) * LANES)
        out_ref[:, cut] = whole[cut, :].T


def take_kernel(blocks, at_ref, back_ref, target_ref, out_ref):
    target = target_ref[pl.ds(at_ref[2], 1), :]
    total = jnp.zeros((3 * K, VEC), F32)
    for n in range(blocks):
        hot = jnp.where(iota((LANES, VEC), 0) + n * LANES == target, 1.0, 0.0).astype(BF16)
        high, low = parts_of(back_ref[n])
        least = (back_ref[n] - high.astype(F32) - low.astype(F32)).astype(BF16)
        left = jnp.concatenate([high.astype(F32), low.astype(F32), least.astype(F32)], axis=0)
        total = total + jnp.dot(left.astype(BF16), hot, preferred_element_type=F32)
    out_ref[...] = total[0:K] + total[K : 2 * K] + total[2 * K : 3 * K]


def shape(*dims, kind=F32):
    return jax.ShapeDtypeStruct(dims, kind)


def cost(flops, data):
    return pl.CostEstimate(flops=flops, bytes_accessed=data, transcendentals=0)


def along_x(step):
    return [(i, ((i // 2 + step) % 4) * 2 + i % 2) for i in range(REPS)]


CORES = [(i, i ^ 1) for i in range(REPS)]


def sum_over_rep(x):
    x = x + lax.ppermute(x, "rep", CORES)
    x = x + lax.ppermute(x, "rep", [(i, i ^ 2) for i in range(REPS)])
    return x + lax.ppermute(x, "rep", [(i, i ^ 6) for i in range(REPS)])


SMEM = pl.BlockSpec(memory_space=pltpu.SMEM)
VMEM = pl.BlockSpec(memory_space=pltpu.VMEM)


def place():
    rep = lax.axis_index("rep")
    return jnp.stack([rep // 2, rep % 2, rep]).astype(jnp.int32)


def to_owners(packed):
    flat = packed.reshape(OWNERS, -1, LANES)
    return lax.all_to_all(flat, "cluster", 0, 0, tiled=True).reshape(packed.shape)


def refine(cap, early, late):
    blocks = OWNERS * cap // LANES
    packed, target, hot, group_of = pl.pallas_call(
        functools.partial(pack_early_kernel, cap),
        out_shape=(
            shape(blocks, ROWS, LANES),
            shape(REPS, VEC, kind=jnp.int32),
            shape(REPS, VEC, PAIR, kind=BF16),
            shape(REPS, 16, VEC, kind=jnp.int32),
        ),
        scratch_shapes=[pltpu.VMEM((REPS, 2 * EARLY + 16, VEC), BF16)],
        compiler_params=params(),
        cost_estimate=cost(2 * 80 * 2048 * OWNERS * cap, 3_000_000),
        name="pack_early",
    )(early)
    rows_early = to_owners(packed)
    packed = pl.pallas_call(
        functools.partial(pack_late_kernel, cap),
        out_shape=shape(blocks, LATE, LANES),
        in_specs=[SMEM] + [VMEM] * (2 + REPS),
        scratch_shapes=[pltpu.VMEM((REPS, 2 * LATE, VEC), BF16)],
        compiler_params=params(),
        cost_estimate=cost(2 * 128 * 2048 * OWNERS * cap, 3_000_000),
        name="pack_late",
    )(place(), hot, group_of, *late)
    rows_late = to_owners(packed)
    partial, most = pl.pallas_call(
        functools.partial(distance_kernel, blocks),
        out_shape=(shape(blocks, K, LANES), shape(1, kind=jnp.int32)),
        out_specs=(VMEM, SMEM),
        scratch_shapes=[
            pltpu.VMEM((STACK, SLOTS), F32),
            pltpu.VMEM((2 * SLOTS, 2 * PART), BF16),
        ],
        compiler_params=params(),
        cost_estimate=cost(2 * 8 * PART * SLOTS * OWNERS * cap, 2_000_000),
        name="distance",
    )(rows_early, rows_late)
    pen = sum_over_rep(partial)
    cent, share = pl.pallas_call(
        functools.partial(share_kernel, blocks),
        out_shape=(shape(PART, SLOTS), shape(blocks, K, LANES)),
        scratch_shapes=[
            pltpu.VMEM((STACK, SLOTS), F32),
            pltpu.VMEM((PART + 16, SLOTS), F32),
        ],
        compiler_params=params(),
        cost_estimate=cost(2 * 3 * PART * SLOTS * OWNERS * cap, 2_000_000),
        name="share",
    )(rows_early, rows_late, pen)
    back = to_owners(share)
    pieces = []
    for step in range(4):
        mine = lax.ppermute(cent, "rep", along_x(step)) if step else cent
        pieces += [mine, lax.ppermute(mine, "rep", CORES)]
    return pieces, back, target, most


def finish(cap, pieces, back, target):
    blocks = OWNERS * cap // LANES
    at = place()
    centroids = pl.pallas_call(
        join_kernel,
        out_shape=shape(SLOTS, D),
        in_specs=[SMEM] + [VMEM] * REPS,
        scratch_shapes=[pltpu.VMEM((D, SLOTS), F32)],
        compiler_params=params(),
        cost_estimate=cost(0, 1_600_000),
        name="join",
    )(at, *pieces)
    shares = pl.pallas_call(
        functools.partial(take_kernel, blocks),
        out_shape=shape(K, VEC),
        in_specs=[SMEM, VMEM, VMEM],
        compiler_params=params(),
        cost_estimate=cost(2 * 24 * VEC * OWNERS * cap, 200_000),
        name="take",
    )(at, back, target)
    return centroids, shares


def on_device(vectors, parent_id, child_id):
    slot = (parent_id * K + child_id).astype(F32).reshape(1, VEC)
    early, late = pl.pallas_call(
        turn_kernel,
        out_shape=(shape(REPS, ROWS, VEC), shape(REPS, LATE, VEC)),
        in_specs=[SMEM, VMEM, VMEM],
        compiler_params=params(),
        cost_estimate=cost(0, 1_600_000),
        name="turn",
    )(place(), vectors, slot)
    early = lax.all_to_all(early, "rep", 0, 0, tiled=True)
    late = [late[0]] + [
        lax.ppermute(late[step], "rep", [(i, (i + step) % REPS) for i in range(REPS)])
        for step in range(1, REPS)
    ]
    pieces, back, target, most = refine(LANES, early, late)
    over = most[0] > LANES

    def wide(early, late, pieces, back, target):
        pieces, back, target, _ = refine(PAIR, early, late)
        return finish(PAIR, pieces, back, target)

    def narrow(early, late, pieces, back, target):
        return finish(LANES, pieces, back, target)

    centroids, shares = lax.cond(over, wide, narrow, early, late, pieces, back, target)
    return centroids, shares.T


def solution(mesh):
    in_specs = (P(("cluster", "rep"), None), P(("cluster", "rep")), P(("cluster", "rep")))
    out_specs = (P("cluster", None), P(("cluster", "rep"), None))
    return jax.shard_map(
        on_device, mesh=mesh, in_specs=in_specs, out_specs=out_specs, check_vma=False
    )
```

```python
import functools

import jax
import jax.numpy as jnp
from jax import lax
from jax.experimental import pallas as pl
from jax.experimental.pallas import tpu as pltpu
from jax.sharding import PartitionSpec as P

K = 8
PAR_DEV = 32
OWNERS = 32
REPS = 8
SLOTS = PAR_DEV * K
D = 768
PART = D // REPS
ROWS = PART + 8
VEC = 256
LANES = 128
PAIR = 2 * LANES
STACK = PART + 16 + PART
F32 = jnp.float32
BF16 = jnp.bfloat16
NT = (((1,), (1,)), ((), ()))


def params():
    return pltpu.CompilerParams(vmem_limit_bytes=48 * 2**20)


def iota(shape, dim):
    return lax.broadcasted_iota(jnp.int32, shape, dim)


def parts_of(x):
    high = x.astype(BF16)
    return high, (x - high.astype(F32)).astype(BF16)


def turn_kernel(v_ref, g_ref, out_ref):
    for tile in range(D // LANES):
        turned = v_ref[:, tile * LANES : (tile + 1) * LANES].T
        start = tile * LANES
        while start < (tile + 1) * LANES:
            part, row = divmod(start, PART)
            size = min(PART - row, (tile + 1) * LANES - start)
            at = start - tile * LANES
            out_ref[BY_CORE.index(part), row : row + size, :] = turned[at : at + size, :]
            start += size
    slots = jnp.broadcast_to(g_ref[...], (ROWS - PART, VEC))
    for part in range(REPS):
        out_ref[part, PART:ROWS, :] = slots


def pack_kernel(cap, in_ref, out_ref, target_ref, left, column):
    groups = OWNERS * cap // PAIR
    before = (iota((VEC, VEC), 0) < iota((VEC, VEC), 1)).astype(F32).astype(BF16)
    carry = jnp.zeros((OWNERS, 1), F32)
    targets = []
    for src in range(REPS):
        slot = in_ref[src, PART : PART + 1, :].astype(jnp.int32)
        owner = slot >> 8
        local = (slot & (SLOTS - 1)) + 1
        hot = (owner == iota((OWNERS, VEC), 0)).astype(F32)
        ahead = jnp.dot(hot.astype(BF16), before, preferred_element_type=F32) + carry
        position = jnp.sum(hot * ahead, axis=0, keepdims=True)
        carry = carry + jnp.sum(hot, axis=1, keepdims=True)
        target = owner.astype(F32) * cap + position
        targets.append(jnp.where(position < cap, target, -1.0))
        high, low = parts_of(in_ref[src, 0:PART, :])
        left[src, 0:PART, :] = high
        left[src, PART : PART + 16, :] = jnp.broadcast_to(local.astype(F32), (16, VEC)).astype(BF16)
        left[src, PART + 16 : STACK, :] = low
    rows = jnp.concatenate(targets, axis=0)
    target_ref[...] = rows.astype(jnp.int32)
    most = jnp.broadcast_to(jnp.max(carry, axis=0, keepdims=True), (8, LANES))
    first_row = iota((8, LANES), 0) == 0
    turned = jnp.concatenate([rows, jnp.zeros((LANES - REPS, VEC), F32)], axis=0).T
    for src in range(REPS):
        column[src] = jnp.broadcast_to(turned[:, src : src + 1], (VEC, LANES))
    lane = iota((VEC, LANES), 1).astype(F32)

    def group(n, _):
        base = (n * PAIR).astype(F32)
        total = jnp.zeros((STACK, PAIR), F32)
        for src in range(REPS):
            at = column[src] - base
            hot = jnp.concatenate(
                [
                    jnp.where(at == lane, 1.0, 0.0).astype(BF16),
                    jnp.where(at == lane + LANES, 1.0, 0.0).astype(BF16),
                ],
                axis=1,
            )
            total = total + jnp.dot(left[src], hot, preferred_element_type=F32)
        values = total[0:PART] + total[PART + 16 : STACK]
        for half in range(2):
            cut = slice(half * LANES, (half + 1) * LANES)
            out_ref[2 * n + half, 0:PART, :] = values[:, cut]
            out_ref[2 * n + half, PART:ROWS, :] = jnp.where(
                first_row, total[PART : PART + 8, cut], most
            )
        return 0

    lax.fori_loop(0, groups, group, 0, unroll=2)


def load_pair(x_ref, n):
    x = jnp.concatenate([x_ref[2 * n, 0:PART, :], x_ref[2 * n + 1, 0:PART, :]], axis=1)
    slot = jnp.concatenate(
        [x_ref[2 * n, PART : PART + 1, :], x_ref[2 * n + 1, PART : PART + 1, :]], axis=1
    )
    return x, slot.astype(jnp.int32)


def stack_of(x):
    high, low = parts_of(x)
    return jnp.concatenate([high, jnp.ones((16, PAIR), BF16), low], axis=0)


def distance_kernel(blocks, x_ref, out_ref, most_ref, total, scaled):
    total[...] = jnp.zeros_like(total)
    most_ref[0] = jnp.max(x_ref[:, PART + 1, :]).astype(jnp.int32)

    def add(n, _):
        x, slot = load_pair(x_ref, n)
        hot = jnp.where(iota((SLOTS, PAIR), 0) + 1 == slot, 1.0, 0.0).astype(BF16)
        total[...] += lax.dot_general(stack_of(x), hot, NT, preferred_element_type=F32)
        return 0

    lax.fori_loop(0, blocks // 2, add, 0, unroll=4)
    sums = total[0:PART, :] + total[PART + 16 : STACK, :]
    counts = total[PART : PART + 8, :]
    high, low = parts_of(sums / (counts[0:1] + 1.0))
    high, low = high.astype(F32), low.astype(F32)
    first = high + low
    turned = jnp.concatenate([high, high, low, low], axis=0).T
    scaled[0:SLOTS, :] = (turned[:, 0 : 2 * PART] * -2.0).astype(BF16)
    scaled[SLOTS:, :] = (turned[:, 2 * PART : 4 * PART] * -2.0).astype(BF16)
    own = jnp.broadcast_to(jnp.sum(first * first, axis=0, keepdims=True), (LANES, SLOTS))
    row = iota((LANES, SLOTS), 0)
    columns = jnp.where(row == 0, jnp.broadcast_to(counts[0:1], (LANES, SLOTS)), own).T
    count = columns[:, 0:1].reshape(PAR_DEV, K, 1)
    mean = jnp.sum(count, axis=1, keepdims=True) / K
    extra = (0.5 * count / (mean + 1.0)).reshape(SLOTS, 1) / REPS
    own = columns[:, 1:2]

    def measure(n, _):
        x, slot = load_pair(x_ref, n)
        both = jnp.dot(
            scaled[...], jnp.concatenate(parts_of(x), axis=0), preferred_element_type=F32
        )
        cross = both[0:SLOTS] + both[SLOTS : 2 * SLOTS]
        parent = (slot - 1) >> 3
        terms = ((cross + own) / D + extra).reshape(PAR_DEV, K, PAIR)
        picked = jnp.where(iota((PAR_DEV, K, PAIR), 0) == parent[None], terms, 0.0)
        part = jnp.sum(picked, axis=0) + jnp.sum(x * x, axis=0, keepdims=True) / D
        out_ref[2 * n] = part[:, 0:LANES]
        out_ref[2 * n + 1] = part[:, LANES:PAIR]
        return 0

    lax.fori_loop(0, blocks // 2, measure, 0, unroll=4)


def share_kernel(blocks, x_ref, pen_ref, cent_ref, share_ref, total, rest):
    total[...] = jnp.zeros_like(total)
    rest[...] = jnp.zeros_like(rest)

    def add(n, _):
        x, slot = load_pair(x_ref, n)
        grown = 1.0 + jnp.concatenate([pen_ref[2 * n], pen_ref[2 * n + 1]], axis=1)
        square = grown * grown
        weight = 1.0 / (square * square)
        share = weight / jnp.sum(weight, axis=0, keepdims=True)
        share = jnp.where(slot > 0, share, 0.0)
        share_ref[2 * n] = share[:, 0:LANES]
        share_ref[2 * n + 1] = share[:, LANES:PAIR]
        parent = (slot - 1) >> 3
        mixing = jnp.where(
            iota((PAR_DEV, K, PAIR), 0) == parent[None], share[None], 0.0
        ).reshape(SLOTS, PAIR)
        high, low = parts_of(mixing)
        left = stack_of(x)
        total[...] += lax.dot_general(left, high, NT, preferred_element_type=F32)
        rest[...] += lax.dot_general(
            left[0 : PART + 16], low, NT, preferred_element_type=F32
        )
        return 0

    lax.fori_loop(0, blocks // 2, add, 0, unroll=4)
    weighted = total[0:PART, :] + total[PART + 16 : STACK, :] + rest[0:PART, :]
    summed = total[PART : PART + 1, :] + rest[PART : PART + 1, :]
    cent_ref[...] = weighted / (summed + 1.0)


def join_kernel(at_ref, *refs):
    *pieces, out_ref, whole = refs
    x, core = at_ref[0], at_ref[1]
    for index, piece in enumerate(pieces):
        step, other = divmod(index, 2)
        where = ((x - step) & 3) * 2 + (core ^ other)
        whole[pl.ds(pl.multiple_of(where * PART, 8), PART), :] = piece[...]
    for tile in range(D // LANES):
        cut = slice(tile * LANES, (tile + 1) * LANES)
        out_ref[:, cut] = whole[cut, :].T


def take_kernel(blocks, at_ref, back_ref, target_ref, out_ref):
    target = target_ref[pl.ds(at_ref[2], 1), :]
    total = jnp.zeros((3 * K, VEC), F32)
    for n in range(blocks):
        hot = jnp.where(iota((LANES, VEC), 0) + n * LANES == target, 1.0, 0.0).astype(BF16)
        high, low = parts_of(back_ref[n])
        least = (back_ref[n] - high.astype(F32) - low.astype(F32)).astype(BF16)
        left = jnp.concatenate([high.astype(F32), low.astype(F32), least.astype(F32)], axis=0)
        total = total + jnp.dot(left.astype(BF16), hot, preferred_element_type=F32)
    out_ref[...] = total[0:K] + total[K : 2 * K] + total[2 * K : 3 * K]


def shape(*dims, kind=F32):
    return jax.ShapeDtypeStruct(dims, kind)


def cost(flops, data):
    return pl.CostEstimate(flops=flops, bytes_accessed=data, transcendentals=0)


def along_x(step):
    return [(i, ((i // 2 + step) % 4) * 2 + i % 2) for i in range(REPS)]


BY_CORE = [0, 2, 4, 6, 1, 3, 5, 7]
CORES = [(i, i ^ 1) for i in range(REPS)]


def sum_over_rep(x):
    x = x + lax.ppermute(x, "rep", CORES)
    x = x + lax.ppermute(x, "rep", [(i, i ^ 2) for i in range(REPS)])
    return x + lax.ppermute(x, "rep", [(i, i ^ 6) for i in range(REPS)])


SMEM = pl.BlockSpec(memory_space=pltpu.SMEM)
VMEM = pl.BlockSpec(memory_space=pltpu.VMEM)


def refine(cap, got):
    blocks = OWNERS * cap // LANES
    packed, target = pl.pallas_call(
        functools.partial(pack_kernel, cap),
        out_shape=(
            shape(blocks, ROWS, LANES),
            shape(REPS, VEC, kind=jnp.int32),
        ),
        scratch_shapes=[pltpu.VMEM((REPS, STACK, VEC), BF16), pltpu.VMEM((REPS, VEC, LANES), F32)],
        compiler_params=params(),
        cost_estimate=cost(2 * STACK * 2048 * OWNERS * cap, 3_000_000),
        name="pack",
    )(got)
    per = cap // LANES
    rows = lax.all_to_all(
        packed.reshape(OWNERS, per * ROWS, LANES), "cluster", 0, 0, tiled=True
    ).reshape(blocks, ROWS, LANES)
    partial, most = pl.pallas_call(
        functools.partial(distance_kernel, blocks),
        out_shape=(shape(blocks, K, LANES), shape(1, kind=jnp.int32)),
        out_specs=(VMEM, SMEM),
        scratch_shapes=[
            pltpu.VMEM((STACK, SLOTS), F32),
            pltpu.VMEM((2 * SLOTS, 2 * PART), BF16),
        ],
        compiler_params=params(),
        cost_estimate=cost(2 * 8 * PART * SLOTS * OWNERS * cap, 2_000_000),
        name="distance",
    )(rows)
    pen = sum_over_rep(partial)
    cent, share = pl.pallas_call(
        functools.partial(share_kernel, blocks),
        out_shape=(shape(PART, SLOTS), shape(blocks, K, LANES)),
        scratch_shapes=[
            pltpu.VMEM((STACK, SLOTS), F32),
            pltpu.VMEM((PART + 16, SLOTS), F32),
        ],
        compiler_params=params(),
        cost_estimate=cost(2 * 3 * PART * SLOTS * OWNERS * cap, 2_000_000),
        name="share",
    )(rows, pen)
    back = lax.all_to_all(
        share.reshape(OWNERS, per * K, LANES), "cluster", 0, 0, tiled=True
    ).reshape(blocks, K, LANES)
    pieces = []
    for step in range(4):
        mine = lax.ppermute(cent, "rep", along_x(step)) if step else cent
        pieces += [mine, lax.ppermute(mine, "rep", CORES)]
    return pieces, back, target, most


def place():
    rep = lax.axis_index("rep")
    return jnp.stack([rep // 2, rep % 2, rep % 2 * 4 + rep // 2]).astype(jnp.int32)


def join(pieces):
    return pl.pallas_call(
        join_kernel,
        out_shape=shape(SLOTS, D),
        in_specs=[SMEM] + [VMEM] * REPS,
        scratch_shapes=[pltpu.VMEM((D, SLOTS), F32)],
        compiler_params=params(),
        cost_estimate=cost(0, 1_600_000),
        name="join",
    )(place(), *pieces)


def take(cap, back, target):
    blocks = OWNERS * cap // LANES
    return pl.pallas_call(
        functools.partial(take_kernel, blocks),
        out_shape=shape(K, VEC),
        in_specs=[SMEM, VMEM, VMEM],
        compiler_params=params(),
        cost_estimate=cost(2 * 24 * VEC * OWNERS * cap, 200_000),
        name="take",
    )(place(), back, target)


def on_device(vectors, parent_id, child_id):
    slot = (parent_id * K + child_id).astype(F32).reshape(1, VEC)
    turned = pl.pallas_call(
        turn_kernel,
        out_shape=shape(REPS, ROWS, VEC),
        compiler_params=params(),
        cost_estimate=cost(0, 1_600_000),
        name="turn",
    )(vectors, slot)
    got = lax.all_to_all(
        turned, "rep", 0, 0, axis_index_groups=[BY_CORE], tiled=True
    )
    pieces, back, target, most = refine(LANES, got)
    over = most[0] > LANES

    picked = take(LANES, back, target)

    def wide(got, pieces, picked):
        pieces, back, target, _ = refine(PAIR, got)
        return join(pieces), take(PAIR, back, target)

    def narrow(got, pieces, picked):
        return join(pieces), picked

    centroids, shares = lax.cond(over, wide, narrow, got, pieces, picked)
    return centroids, shares.T


def solution(mesh):
    in_specs = (P(("cluster", "rep"), None), P(("cluster", "rep")), P(("cluster", "rep")))
    out_specs = (P("cluster", None), P(("cluster", "rep"), None))
    return jax.shard_map(
        on_device, mesh=mesh, in_specs=in_specs, out_specs=out_specs, check_vma=False
    )
```

```python
import functools

import jax
import jax.numpy as jnp
from jax import lax
from jax.experimental import pallas as pl
from jax.experimental.pallas import tpu as pltpu
from jax.sharding import PartitionSpec as P

K = 8
PAR_DEV = 32
OWNERS = 32
REPS = 8
SLOTS = PAR_DEV * K
D = 768
PART = D // REPS
ROWS = PART + 8
VEC = 256
LANES = 128
PAIR = 2 * LANES
STACK = PART + 16 + PART
F32 = jnp.float32
BF16 = jnp.bfloat16
NT = (((1,), (1,)), ((), ()))


def params():
    return pltpu.CompilerParams(vmem_limit_bytes=48 * 2**20)


def iota(shape, dim):
    return lax.broadcasted_iota(jnp.int32, shape, dim)


def parts_of(x):
    high = x.astype(BF16)
    return high, (x - high.astype(F32)).astype(BF16)


def turn_kernel(v_ref, g_ref, out_ref):
    for tile in range(D // LANES):
        turned = v_ref[:, tile * LANES : (tile + 1) * LANES].T
        start = tile * LANES
        while start < (tile + 1) * LANES:
            part, row = divmod(start, PART)
            size = min(PART - row, (tile + 1) * LANES - start)
            at = start - tile * LANES
            out_ref[BY_CORE.index(part), row : row + size, :] = turned[at : at + size, :]
            start += size
    slots = jnp.broadcast_to(g_ref[...], (ROWS - PART, VEC))
    for part in range(REPS):
        out_ref[part, PART:ROWS, :] = slots


def pack_kernel(cap, in_ref, out_ref, target_ref, left, column):
    groups = OWNERS * cap // PAIR
    before = (iota((VEC, VEC), 0) < iota((VEC, VEC), 1)).astype(F32).astype(BF16)
    carry = jnp.zeros((OWNERS, 1), F32)
    targets = []
    for src in range(REPS):
        slot = in_ref[src, PART : PART + 1, :].astype(jnp.int32)
        owner = slot >> 8
        local = (slot & (SLOTS - 1)) + 1
        hot = (owner == iota((OWNERS, VEC), 0)).astype(F32)
        ahead = jnp.dot(hot.astype(BF16), before, preferred_element_type=F32) + carry
        position = jnp.sum(hot * ahead, axis=0, keepdims=True)
        carry = carry + jnp.sum(hot, axis=1, keepdims=True)
        target = owner.astype(F32) * cap + position
        targets.append(jnp.where(position < cap, target, -1.0))
        high, low = parts_of(in_ref[src, 0:PART, :])
        left[src, 0:PART, :] = high
        left[src, PART : PART + 16, :] = jnp.broadcast_to(local.astype(F32), (16, VEC)).astype(BF16)
        left[src, PART + 16 : STACK, :] = low
    rows = jnp.concatenate(targets, axis=0)
    target_ref[...] = rows.astype(jnp.int32)
    most = jnp.broadcast_to(jnp.max(carry, axis=0, keepdims=True), (8, LANES))
    first_row = iota((8, LANES), 0) == 0
    turned = jnp.concatenate([rows, jnp.zeros((LANES - REPS, VEC), F32)], axis=0).T
    for src in range(REPS):
        column[src] = jnp.broadcast_to(turned[:, src : src + 1], (VEC, LANES))
    lane = iota((VEC, LANES), 1).astype(F32)

    def group(n, _):
        base = (n * PAIR).astype(F32)
        total = jnp.zeros((STACK, PAIR), F32)
        for src in range(REPS):
            at = column[src] - base
            hot = jnp.concatenate(
                [
                    jnp.where(at == lane, 1.0, 0.0).astype(BF16),
                    jnp.where(at == lane + LANES, 1.0, 0.0).astype(BF16),
                ],
                axis=1,
            )
            total = total + jnp.dot(left[src], hot, preferred_element_type=F32)
        values = total[0:PART] + total[PART + 16 : STACK]
        for half in range(2):
            cut = slice(half * LANES, (half + 1) * LANES)
            out_ref[2 * n + half, 0:PART, :] = values[:, cut]
            out_ref[2 * n + half, PART:ROWS, :] = jnp.where(
                first_row, total[PART : PART + 8, cut], most
            )
        return 0

    lax.fori_loop(0, groups, group, 0, unroll=4)


def load_pair(x_ref, n):
    x = jnp.concatenate([x_ref[2 * n, 0:PART, :], x_ref[2 * n + 1, 0:PART, :]], axis=1)
    slot = jnp.concatenate(
        [x_ref[2 * n, PART : PART + 1, :], x_ref[2 * n + 1, PART : PART + 1, :]], axis=1
    )
    return x, slot.astype(jnp.int32)


def stack_of(x):
    high, low = parts_of(x)
    return jnp.concatenate([high, jnp.ones((16, PAIR), BF16), low], axis=0)


def distance_kernel(blocks, x_ref, out_ref, most_ref, total, scaled):
    total[...] = jnp.zeros_like(total)
    most_ref[0] = jnp.max(x_ref[:, PART + 1, :]).astype(jnp.int32)

    def add(n, _):
        x, slot = load_pair(x_ref, n)
        hot = jnp.where(iota((SLOTS, PAIR), 0) + 1 == slot, 1.0, 0.0).astype(BF16)
        total[...] += lax.dot_general(stack_of(x), hot, NT, preferred_element_type=F32)
        return 0

    lax.fori_loop(0, blocks // 2, add, 0, unroll=8)
    sums = total[0:PART, :] + total[PART + 16 : STACK, :]
    counts = total[PART : PART + 8, :]
    high, low = parts_of(sums / (counts[0:1] + 1.0))
    high, low = high.astype(F32), low.astype(F32)
    first = high + low
    turned = jnp.concatenate([high, high, low, low], axis=0).T
    scaled[0:SLOTS, :] = (turned[:, 0 : 2 * PART] * -2.0).astype(BF16)
    scaled[SLOTS:, :] = (turned[:, 2 * PART : 4 * PART] * -2.0).astype(BF16)
    own = jnp.broadcast_to(jnp.sum(first * first, axis=0, keepdims=True), (LANES, SLOTS))
    row = iota((LANES, SLOTS), 0)
    columns = jnp.where(row == 0, jnp.broadcast_to(counts[0:1], (LANES, SLOTS)), own).T
    count = columns[:, 0:1].reshape(PAR_DEV, K, 1)
    mean = jnp.sum(count, axis=1, keepdims=True) / K
    extra = (0.5 * count / (mean + 1.0)).reshape(SLOTS, 1) / REPS
    own = columns[:, 1:2]

    def measure(n, _):
        x, slot = load_pair(x_ref, n)
        both = jnp.dot(
            scaled[...], jnp.concatenate(parts_of(x), axis=0), preferred_element_type=F32
        )
        cross = both[0:SLOTS] + both[SLOTS : 2 * SLOTS]
        parent = (slot - 1) >> 3
        terms = ((cross + own) / D + extra).reshape(PAR_DEV, K, PAIR)
        picked = jnp.where(iota((PAR_DEV, K, PAIR), 0) == parent[None], terms, 0.0)
        part = jnp.sum(picked, axis=0) + jnp.sum(x * x, axis=0, keepdims=True) / D
        out_ref[2 * n] = part[:, 0:LANES]
        out_ref[2 * n + 1] = part[:, LANES:PAIR]
        return 0

    lax.fori_loop(0, blocks // 2, measure, 0, unroll=8)


def share_kernel(blocks, x_ref, pen_ref, cent_ref, share_ref, total, rest):
    total[...] = jnp.zeros_like(total)
    rest[...] = jnp.zeros_like(rest)

    def add(n, _):
        x, slot = load_pair(x_ref, n)
        grown = 1.0 + jnp.concatenate([pen_ref[2 * n], pen_ref[2 * n + 1]], axis=1)
        square = grown * grown
        weight = 1.0 / (square * square)
        share = weight / jnp.sum(weight, axis=0, keepdims=True)
        share = jnp.where(slot > 0, share, 0.0)
        share_ref[2 * n] = share[:, 0:LANES]
        share_ref[2 * n + 1] = share[:, LANES:PAIR]
        parent = (slot - 1) >> 3
        mixing = jnp.where(
            iota((PAR_DEV, K, PAIR), 0) == parent[None], share[None], 0.0
        ).reshape(SLOTS, PAIR)
        high, low = parts_of(mixing)
        left = stack_of(x)
        total[...] += lax.dot_general(left, high, NT, preferred_element_type=F32)
        rest[...] += lax.dot_general(
            left[0 : PART + 16], low, NT, preferred_element_type=F32
        )
        return 0

    lax.fori_loop(0, blocks // 2, add, 0, unroll=8)
    weighted = total[0:PART, :] + total[PART + 16 : STACK, :] + rest[0:PART, :]
    summed = total[PART : PART + 1, :] + rest[PART : PART + 1, :]
    cent_ref[...] = weighted / (summed + 1.0)


def join_kernel(at_ref, *refs):
    *pieces, out_ref, whole = refs
    x, core = at_ref[0], at_ref[1]
    for index, piece in enumerate(pieces):
        step, other = divmod(index, 2)
        where = ((x - step) & 3) * 2 + (core ^ other)
        whole[pl.ds(pl.multiple_of(where * PART, 8), PART), :] = piece[...]
    for tile in range(D // LANES):
        cut = slice(tile * LANES, (tile + 1) * LANES)
        out_ref[:, cut] = whole[cut, :].T


def take_kernel(blocks, at_ref, back_ref, target_ref, out_ref):
    target = target_ref[pl.ds(at_ref[2], 1), :]
    total = jnp.zeros((3 * K, VEC), F32)
    for n in range(blocks):
        hot = jnp.where(iota((LANES, VEC), 0) + n * LANES == target, 1.0, 0.0).astype(BF16)
        high, low = parts_of(back_ref[n])
        least = (back_ref[n] - high.astype(F32) - low.astype(F32)).astype(BF16)
        left = jnp.concatenate([high.astype(F32), low.astype(F32), least.astype(F32)], axis=0)
        total = total + jnp.dot(left.astype(BF16), hot, preferred_element_type=F32)
    out_ref[...] = total[0:K] + total[K : 2 * K] + total[2 * K : 3 * K]


def shape(*dims, kind=F32):
    return jax.ShapeDtypeStruct(dims, kind)


def cost(flops, data):
    return pl.CostEstimate(flops=flops, bytes_accessed=data, transcendentals=0)


def along_x(step):
    return [(i, ((i // 2 + step) % 4) * 2 + i % 2) for i in range(REPS)]


BY_CORE = [0, 2, 4, 6, 1, 3, 5, 7]
CORES = [(i, i ^ 1) for i in range(REPS)]


def sum_over_rep(x):
    x = x + lax.ppermute(x, "rep", CORES)
    x = x + lax.ppermute(x, "rep", [(i, i ^ 2) for i in range(REPS)])
    return x + lax.ppermute(x, "rep", [(i, i ^ 6) for i in range(REPS)])


SMEM = pl.BlockSpec(memory_space=pltpu.SMEM)
VMEM = pl.BlockSpec(memory_space=pltpu.VMEM)


def refine(cap, got):
    blocks = OWNERS * cap // LANES
    packed, target = pl.pallas_call(
        functools.partial(pack_kernel, cap),
        out_shape=(
            shape(blocks, ROWS, LANES),
            shape(REPS, VEC, kind=jnp.int32),
        ),
        scratch_shapes=[pltpu.VMEM((REPS, STACK, VEC), BF16), pltpu.VMEM((REPS, VEC, LANES), F32)],
        compiler_params=params(),
        cost_estimate=cost(2 * STACK * 2048 * OWNERS * cap, 3_000_000),
        name="pack",
    )(got)
    per = cap // LANES
    rows = lax.all_to_all(
        packed.reshape(OWNERS, per * ROWS, LANES), "cluster", 0, 0, tiled=True
    ).reshape(blocks, ROWS, LANES)
    partial, most = pl.pallas_call(
        functools.partial(distance_kernel, blocks),
        out_shape=(shape(blocks, K, LANES), shape(1, kind=jnp.int32)),
        out_specs=(VMEM, SMEM),
        scratch_shapes=[
            pltpu.VMEM((STACK, SLOTS), F32),
            pltpu.VMEM((2 * SLOTS, 2 * PART), BF16),
        ],
        compiler_params=params(),
        cost_estimate=cost(2 * 8 * PART * SLOTS * OWNERS * cap, 2_000_000),
        name="distance",
    )(rows)
    pen = sum_over_rep(partial)
    cent, share = pl.pallas_call(
        functools.partial(share_kernel, blocks),
        out_shape=(shape(PART, SLOTS), shape(blocks, K, LANES)),
        scratch_shapes=[
            pltpu.VMEM((STACK, SLOTS), F32),
            pltpu.VMEM((PART + 16, SLOTS), F32),
        ],
        compiler_params=params(),
        cost_estimate=cost(2 * 3 * PART * SLOTS * OWNERS * cap, 2_000_000),
        name="share",
    )(rows, pen)
    back = lax.all_to_all(
        share.reshape(OWNERS, per * K, LANES), "cluster", 0, 0, tiled=True
    ).reshape(blocks, K, LANES)
    pieces = []
    for step in range(4):
        mine = lax.ppermute(cent, "rep", along_x(step)) if step else cent
        pieces += [mine, lax.ppermute(mine, "rep", CORES)]
    return pieces, back, target, most


def place():
    rep = lax.axis_index("rep")
    return jnp.stack([rep // 2, rep % 2, rep % 2 * 4 + rep // 2]).astype(jnp.int32)


def join(pieces):
    return pl.pallas_call(
        join_kernel,
        out_shape=shape(SLOTS, D),
        in_specs=[SMEM] + [VMEM] * REPS,
        scratch_shapes=[pltpu.VMEM((D, SLOTS), F32)],
        compiler_params=params(),
        cost_estimate=cost(0, 1_600_000),
        name="join",
    )(place(), *pieces)


def take(cap, back, target):
    blocks = OWNERS * cap // LANES
    return pl.pallas_call(
        functools.partial(take_kernel, blocks),
        out_shape=shape(K, VEC),
        in_specs=[SMEM, VMEM, VMEM],
        compiler_params=params(),
        cost_estimate=cost(2 * 24 * VEC * OWNERS * cap, 200_000),
        name="take",
    )(place(), back, target)


def on_device(vectors, parent_id, child_id):
    slot = (parent_id * K + child_id).astype(F32).reshape(1, VEC)
    turned = pl.pallas_call(
        turn_kernel,
        out_shape=shape(REPS, ROWS, VEC),
        compiler_params=params(),
        cost_estimate=cost(0, 1_600_000),
        name="turn",
    )(vectors, slot)
    got = lax.all_to_all(
        turned, "rep", 0, 0, axis_index_groups=[BY_CORE], tiled=True
    )
    pieces, back, target, most = refine(LANES, got)
    over = most[0] > LANES

    picked = take(LANES, back, target)

    def wide(got, pieces, picked):
        pieces, back, target, _ = refine(PAIR, got)
        return join(pieces), take(PAIR, back, target)

    def narrow(got, pieces, picked):
        return join(pieces), picked

    centroids, shares = lax.cond(over, wide, narrow, got, pieces, picked)
    return centroids, shares.T


def solution(mesh):
    in_specs = (P(("cluster", "rep"), None), P(("cluster", "rep")), P(("cluster", "rep")))
    out_specs = (P("cluster", None), P(("cluster", "rep"), None))
    return jax.shard_map(
        on_device, mesh=mesh, in_specs=in_specs, out_specs=out_specs, check_vma=False
    )
```

```python
import functools

import jax
import jax.numpy as jnp
from jax import lax
from jax.experimental import pallas as pl
from jax.experimental.pallas import tpu as pltpu
from jax.sharding import PartitionSpec as P

K = 8
PAR_DEV = 32
OWNERS = 32
DEPTH = 8
WIDTH = 4
REPS = 8
SLOTS = PAR_DEV * K
D = 768
PART = D // REPS
ROWS = PART + 8
VEC = 256
LANES = 128
PAIR = 2 * LANES
STACK = PART + 16 + PART
F32 = jnp.float32
BF16 = jnp.bfloat16
NT = (((1,), (1,)), ((), ()))


def params():
    return pltpu.CompilerParams(vmem_limit_bytes=48 * 2**20)


def iota(shape, dim):
    return lax.broadcasted_iota(jnp.int32, shape, dim)


def parts_of(x):
    high = x.astype(BF16)
    return high, (x - high.astype(F32)).astype(BF16)


def turn_kernel(v_ref, g_ref, out_ref):
    for tile in range(D // LANES):
        turned = v_ref[:, tile * LANES : (tile + 1) * LANES].T
        start = tile * LANES
        while start < (tile + 1) * LANES:
            part, row = divmod(start, PART)
            size = min(PART - row, (tile + 1) * LANES - start)
            at = start - tile * LANES
            out_ref[BY_CORE.index(part), row : row + size, :] = turned[at : at + size, :]
            start += size
    slots = jnp.broadcast_to(g_ref[...], (ROWS - PART, VEC))
    for part in range(REPS):
        out_ref[part, PART:ROWS, :] = slots


def pack_kernel(cap, at_ref, in_ref, out_ref, target_ref, left, column):
    groups = OWNERS * cap // PAIR
    before = (iota((VEC, VEC), 0) < iota((VEC, VEC), 1)).astype(F32).astype(BF16)
    carry = jnp.zeros((OWNERS, 1), F32)
    targets, places = [], []
    for src in range(REPS):
        slot = in_ref[src, PART : PART + 1, :].astype(jnp.int32)
        owner = slot >> 8
        local = (slot & (SLOTS - 1)) + 1
        hot = (owner == iota((OWNERS, VEC), 0)).astype(F32)
        ahead = jnp.dot(hot.astype(BF16), before, preferred_element_type=F32) + carry
        position = jnp.sum(hot * ahead, axis=0, keepdims=True)
        carry = carry + jnp.sum(hot, axis=1, keepdims=True)
        far = ((owner >> 2) - at_ref[3]) & (DEPTH - 1)
        side = ((owner & (WIDTH - 1)) - at_ref[4]) & (WIDTH - 1)
        block = (far * WIDTH + side).astype(F32)
        fits = position < cap
        targets.append(jnp.where(fits, owner.astype(F32) * cap + position, -1.0))
        places.append(jnp.where(fits, block * cap + position, -1.0))
        high, low = parts_of(in_ref[src, 0:PART, :])
        left[src, 0:PART, :] = high
        left[src, PART : PART + 16, :] = jnp.broadcast_to(local.astype(F32), (16, VEC)).astype(BF16)
        left[src, PART + 16 : STACK, :] = low
    target_ref[...] = jnp.concatenate(targets, axis=0).astype(jnp.int32)
    rows = jnp.concatenate(places, axis=0)
    most = jnp.broadcast_to(jnp.max(carry, axis=0, keepdims=True), (8, LANES))
    first_row = iota((8, LANES), 0) == 0
    turned = jnp.concatenate([rows, jnp.zeros((LANES - REPS, VEC), F32)], axis=0).T
    for src in range(REPS):
        column[src] = jnp.broadcast_to(turned[:, src : src + 1], (VEC, LANES))
    lane = iota((VEC, LANES), 1).astype(F32)

    def group(n, _):
        base = (n * PAIR).astype(F32)
        total = jnp.zeros((STACK, PAIR), F32)
        for src in range(REPS):
            at = column[src] - base
            hot = jnp.concatenate(
                [
                    jnp.where(at == lane, 1.0, 0.0).astype(BF16),
                    jnp.where(at == lane + LANES, 1.0, 0.0).astype(BF16),
                ],
                axis=1,
            )
            total = total + jnp.dot(left[src], hot, preferred_element_type=F32)
        values = total[0:PART] + total[PART + 16 : STACK]
        for half in range(2):
            cut = slice(half * LANES, (half + 1) * LANES)
            out_ref[2 * n + half, 0:PART, :] = values[:, cut]
            out_ref[2 * n + half, PART:ROWS, :] = jnp.where(
                first_row, total[PART : PART + 8, cut], most
            )
        return 0

    lax.fori_loop(0, groups, group, 0, unroll=4)


def load_pair(x_ref, n):
    x = jnp.concatenate([x_ref[2 * n, 0:PART, :], x_ref[2 * n + 1, 0:PART, :]], axis=1)
    slot = jnp.concatenate(
        [x_ref[2 * n, PART : PART + 1, :], x_ref[2 * n + 1, PART : PART + 1, :]], axis=1
    )
    return x, slot.astype(jnp.int32)


def stack_of(x):
    high, low = parts_of(x)
    return jnp.concatenate([high, jnp.ones((16, PAIR), BF16), low], axis=0)


def distance_kernel(*refs):
    *x_refs, out_ref, most_ref, total, scaled = refs
    blocks = x_refs[0].shape[0]
    total[...] = jnp.zeros_like(total)
    most = x_refs[0][:, PART + 1, :]
    for x_ref in x_refs:
        most = jnp.maximum(most, x_ref[:, PART + 1, :])

        def add(n, _, x_ref=x_ref):
            x, slot = load_pair(x_ref, n)
            hot = jnp.where(iota((SLOTS, PAIR), 0) + 1 == slot, 1.0, 0.0).astype(BF16)
            total[...] += lax.dot_general(stack_of(x), hot, NT, preferred_element_type=F32)
            return 0

        lax.fori_loop(0, blocks // 2, add, 0, unroll=4)
    most_ref[0] = jnp.max(most).astype(jnp.int32)
    sums = total[0:PART, :] + total[PART + 16 : STACK, :]
    counts = total[PART : PART + 8, :]
    high, low = parts_of(sums / (counts[0:1] + 1.0))
    high, low = high.astype(F32), low.astype(F32)
    first = high + low
    turned = jnp.concatenate([high, high, low, low], axis=0).T
    scaled[0:SLOTS, :] = (turned[:, 0 : 2 * PART] * -2.0).astype(BF16)
    scaled[SLOTS:, :] = (turned[:, 2 * PART : 4 * PART] * -2.0).astype(BF16)
    own = jnp.broadcast_to(jnp.sum(first * first, axis=0, keepdims=True), (LANES, SLOTS))
    row = iota((LANES, SLOTS), 0)
    columns = jnp.where(row == 0, jnp.broadcast_to(counts[0:1], (LANES, SLOTS)), own).T
    count = columns[:, 0:1].reshape(PAR_DEV, K, 1)
    mean = jnp.sum(count, axis=1, keepdims=True) / K
    extra = (0.5 * count / (mean + 1.0)).reshape(SLOTS, 1) / REPS
    own = columns[:, 1:2]

    for index, x_ref in enumerate(x_refs):

        def measure(n, _, base=index * blocks, x_ref=x_ref):
            x, slot = load_pair(x_ref, n)
            both = jnp.dot(
                scaled[...], jnp.concatenate(parts_of(x), axis=0), preferred_element_type=F32
            )
            cross = both[0:SLOTS] + both[SLOTS : 2 * SLOTS]
            parent = (slot - 1) >> 3
            terms = ((cross + own) / D + extra).reshape(PAR_DEV, K, PAIR)
            picked = jnp.where(iota((PAR_DEV, K, PAIR), 0) == parent[None], terms, 0.0)
            part = jnp.sum(picked, axis=0) + jnp.sum(x * x, axis=0, keepdims=True) / D
            out_ref[base + 2 * n] = part[:, 0:LANES]
            out_ref[base + 2 * n + 1] = part[:, LANES:PAIR]
            return 0

        lax.fori_loop(0, blocks // 2, measure, 0, unroll=4)


def share_kernel(per, at_ref, pen_ref, *refs):
    *x_refs, cent_ref, share_ref, total, rest = refs
    blocks = DEPTH * per
    total[...] = jnp.zeros_like(total)
    rest[...] = jnp.zeros_like(rest)
    for index, x_ref in enumerate(x_refs):

        def add(n, _, index=index, x_ref=x_ref):
            x, slot = load_pair(x_ref, n)
            base = index * blocks + 2 * n
            grown = 1.0 + jnp.concatenate([pen_ref[base], pen_ref[base + 1]], axis=1)
            square = grown * grown
            weight = 1.0 / (square * square)
            share = weight / jnp.sum(weight, axis=0, keepdims=True)
            share = jnp.where(slot > 0, share, 0.0)
            for half in range(2):
                block = 2 * n + half
                z = (at_ref[3] - block // per) & (DEPTH - 1)
                y = (at_ref[4] - index) & (WIDTH - 1)
                cut = slice(half * LANES, (half + 1) * LANES)
                share_ref[(z * WIDTH + y) * per + block % per] = share[:, cut]
            parent = (slot - 1) >> 3
            mixing = jnp.where(
                iota((PAR_DEV, K, PAIR), 0) == parent[None], share[None], 0.0
            ).reshape(SLOTS, PAIR)
            high, low = parts_of(mixing)
            left = stack_of(x)
            total[...] += lax.dot_general(left, high, NT, preferred_element_type=F32)
            rest[...] += lax.dot_general(
                left[0 : PART + 16], low, NT, preferred_element_type=F32
            )
            return 0

        lax.fori_loop(0, blocks // 2, add, 0, unroll=4)
    weighted = total[0:PART, :] + total[PART + 16 : STACK, :] + rest[0:PART, :]
    summed = total[PART : PART + 1, :] + rest[PART : PART + 1, :]
    cent_ref[...] = weighted / (summed + 1.0)


def join_kernel(at_ref, *refs):
    *pieces, out_ref, whole = refs
    x, core = at_ref[0], at_ref[1]
    for index, piece in enumerate(pieces):
        step, other = divmod(index, 2)
        where = ((x - step) & 3) * 2 + (core ^ other)
        whole[pl.ds(pl.multiple_of(where * PART, 8), PART), :] = piece[...]
    for tile in range(D // LANES):
        cut = slice(tile * LANES, (tile + 1) * LANES)
        out_ref[:, cut] = whole[cut, :].T


def take_kernel(blocks, at_ref, back_ref, target_ref, out_ref):
    target = target_ref[pl.ds(at_ref[2], 1), :]
    total = jnp.zeros((3 * K, VEC), F32)
    for n in range(blocks):
        hot = jnp.where(iota((LANES, VEC), 0) + n * LANES == target, 1.0, 0.0).astype(BF16)
        high, low = parts_of(back_ref[n])
        least = (back_ref[n] - high.astype(F32) - low.astype(F32)).astype(BF16)
        left = jnp.concatenate([high.astype(F32), low.astype(F32), least.astype(F32)], axis=0)
        total = total + jnp.dot(left.astype(BF16), hot, preferred_element_type=F32)
    out_ref[...] = total[0:K] + total[K : 2 * K] + total[2 * K : 3 * K]


def shape(*dims, kind=F32):
    return jax.ShapeDtypeStruct(dims, kind)


def cost(flops, data):
    return pl.CostEstimate(flops=flops, bytes_accessed=data, transcendentals=0)


def along_x(step):
    return [(i, ((i // 2 + step) % 4) * 2 + i % 2) for i in range(REPS)]


BY_CORE = [0, 2, 4, 6, 1, 3, 5, 7]
CORES = [(i, i ^ 1) for i in range(REPS)]


def sum_over_rep(x):
    x = x + lax.ppermute(x, "rep", CORES)
    x = x + lax.ppermute(x, "rep", [(i, i ^ 2) for i in range(REPS)])
    return x + lax.ppermute(x, "rep", [(i, i ^ 6) for i in range(REPS)])


SMEM = pl.BlockSpec(memory_space=pltpu.SMEM)
VMEM = pl.BlockSpec(memory_space=pltpu.VMEM)


def along(dz, dy):
    return [
        (z * WIDTH + y, (z + dz) % DEPTH * WIDTH + (y + dy) % WIDTH)
        for z in range(DEPTH)
        for y in range(WIDTH)
    ]


def to_owners(packed, per):
    mine = packed.reshape(DEPTH, WIDTH * per, ROWS, LANES)
    got = [mine[0]] + [None] * (DEPTH - 1)
    for dz in (4, 3, 5, 2, 6, 1, 7):
        got[dz] = lax.ppermute(mine[dz], "cluster", along(dz, 0))
    sides = [
        jnp.concatenate([part[dy * per : (dy + 1) * per] for part in got], axis=0)
        for dy in range(WIDTH)
    ]
    return [sides[0]] + [
        lax.ppermute(sides[dy], "cluster", along(0, dy)) for dy in range(1, WIDTH)
    ]


def refine(cap, got):
    per = cap // LANES
    blocks = OWNERS * per
    packed, target = pl.pallas_call(
        functools.partial(pack_kernel, cap),
        in_specs=[SMEM, VMEM],
        out_shape=(
            shape(blocks, ROWS, LANES),
            shape(REPS, VEC, kind=jnp.int32),
        ),
        scratch_shapes=[pltpu.VMEM((REPS, STACK, VEC), BF16), pltpu.VMEM((REPS, VEC, LANES), F32)],
        compiler_params=params(),
        cost_estimate=cost(2 * STACK * 2048 * OWNERS * cap, 3_000_000),
        name="pack",
    )(place(), got)
    rows = to_owners(packed, per)
    partial, most = pl.pallas_call(
        distance_kernel,
        out_shape=(shape(blocks, K, LANES), shape(1, kind=jnp.int32)),
        out_specs=(VMEM, SMEM),
        scratch_shapes=[
            pltpu.VMEM((STACK, SLOTS), F32),
            pltpu.VMEM((2 * SLOTS, 2 * PART), BF16),
        ],
        compiler_params=params(),
        cost_estimate=cost(2 * 8 * PART * SLOTS * OWNERS * cap, 2_000_000),
        name="distance",
    )(*rows)
    pen = sum_over_rep(partial)
    cent, share = pl.pallas_call(
        functools.partial(share_kernel, per),
        in_specs=[SMEM] + [VMEM] * (1 + WIDTH),
        out_shape=(shape(PART, SLOTS), shape(blocks, K, LANES)),
        scratch_shapes=[
            pltpu.VMEM((STACK, SLOTS), F32),
            pltpu.VMEM((PART + 16, SLOTS), F32),
        ],
        compiler_params=params(),
        cost_estimate=cost(2 * 3 * PART * SLOTS * OWNERS * cap, 2_000_000),
        name="share",
    )(place(), pen, *rows)
    back = lax.all_to_all(
        share.reshape(OWNERS, per * K, LANES), "cluster", 0, 0, tiled=True
    ).reshape(blocks, K, LANES)
    pieces = []
    for step in range(4):
        mine = lax.ppermute(cent, "rep", along_x(step)) if step else cent
        pieces += [mine, lax.ppermute(mine, "rep", CORES)]
    return pieces, back, target, most


def place():
    rep = lax.axis_index("rep")
    cluster = lax.axis_index("cluster")
    return jnp.stack(
        [rep // 2, rep % 2, rep % 2 * 4 + rep // 2, cluster // WIDTH, cluster % WIDTH]
    ).astype(jnp.int32)


def join(pieces):
    return pl.pallas_call(
        join_kernel,
        out_shape=shape(SLOTS, D),
        in_specs=[SMEM] + [VMEM] * REPS,
        scratch_shapes=[pltpu.VMEM((D, SLOTS), F32)],
        compiler_params=params(),
        cost_estimate=cost(0, 1_600_000),
        name="join",
    )(place(), *pieces)


def take(cap, back, target):
    blocks = OWNERS * cap // LANES
    return pl.pallas_call(
        functools.partial(take_kernel, blocks),
        out_shape=shape(K, VEC),
        in_specs=[SMEM, VMEM, VMEM],
        compiler_params=params(),
        cost_estimate=cost(2 * 24 * VEC * OWNERS * cap, 200_000),
        name="take",
    )(place(), back, target)


def on_device(vectors, parent_id, child_id):
    slot = (parent_id * K + child_id).astype(F32).reshape(1, VEC)
    turned = pl.pallas_call(
        turn_kernel,
        out_shape=shape(REPS, ROWS, VEC),
        compiler_params=params(),
        cost_estimate=cost(0, 1_600_000),
        name="turn",
    )(vectors, slot)
    got = lax.all_to_all(
        turned, "rep", 0, 0, axis_index_groups=[BY_CORE], tiled=True
    )
    pieces, back, target, most = refine(LANES, got)
    over = most[0] > LANES

    picked = take(LANES, back, target)

    def wide(got, pieces, picked):
        pieces, back, target, _ = refine(PAIR, got)
        return join(pieces), take(PAIR, back, target)

    def narrow(got, pieces, picked):
        return join(pieces), picked

    centroids, shares = lax.cond(over, wide, narrow, got, pieces, picked)
    return centroids, shares.T


def solution(mesh):
    in_specs = (P(("cluster", "rep"), None), P(("cluster", "rep")), P(("cluster", "rep")))
    out_specs = (P("cluster", None), P(("cluster", "rep"), None))
    return jax.shard_map(
        on_device, mesh=mesh, in_specs=in_specs, out_specs=out_specs, check_vma=False
    )
```

```python
import functools

import jax
import jax.numpy as jnp
from jax import lax
from jax.experimental import pallas as pl
from jax.experimental.pallas import tpu as pltpu
from jax.sharding import PartitionSpec as P

K = 8
PAR_DEV = 32
OWNERS = 32
REPS = 8
SLOTS = PAR_DEV * K
D = 768
PART = D // REPS
ROWS = PART + 8
VEC = 256
LANES = 128
TILES = D // LANES
PAIR = 2 * LANES
STACK = PART + 16 + PART
F32 = jnp.float32
BF16 = jnp.bfloat16
NT = (((1,), (1,)), ((), ()))


def params(limit=48 * 1024):
    return pltpu.CompilerParams(vmem_limit_bytes=limit * 1024)


def iota(shape, dim):
    return lax.broadcasted_iota(jnp.int32, shape, dim)


def parts_of(x):
    high = x.astype(BF16)
    return high, (x - high.astype(F32)).astype(BF16)


def turn_kernel(v_ref, g_ref, out_ref):
    for tile in range(TILES):
        turned = v_ref[:, tile * LANES : (tile + 1) * LANES].T
        start = tile * LANES
        while start < (tile + 1) * LANES:
            part, row = divmod(start, PART)
            size = min(PART - row, (tile + 1) * LANES - start)
            at = start - tile * LANES
            out_ref[BY_CORE.index(part), row : row + size, :] = turned[at : at + size, :]
            start += size
    slots = jnp.broadcast_to(g_ref[...], (ROWS - PART, VEC))
    for part in range(REPS):
        out_ref[part, PART:ROWS, :] = slots


def pack_kernel(cap, in_ref, out_ref, target_ref, left, hot, group_of):
    groups = OWNERS * cap // PAIR
    before = (iota((VEC, VEC), 0) < iota((VEC, VEC), 1)).astype(F32).astype(BF16)
    carry = jnp.zeros((OWNERS, 1), F32)
    targets = []
    for src in range(REPS):
        slot = in_ref[src, PART : PART + 1, :].astype(jnp.int32)
        owner = slot >> 8
        local = (slot & (SLOTS - 1)) + 1
        mine = (owner == iota((OWNERS, VEC), 0)).astype(F32)
        ahead = jnp.dot(mine.astype(BF16), before, preferred_element_type=F32) + carry
        position = jnp.sum(mine * ahead, axis=0, keepdims=True)
        carry = carry + jnp.sum(mine, axis=1, keepdims=True)
        target = owner * cap + position.astype(jnp.int32)
        target = jnp.where(position < cap, target, -1)
        targets.append(target)
        group_of[src] = jnp.broadcast_to(target >> 8, (16, VEC))
        high, low = parts_of(in_ref[src, 0:PART, :])
        left[src, 0:PART, :] = high
        left[src, PART : PART + 16, :] = jnp.broadcast_to(local.astype(F32), (16, VEC)).astype(BF16)
        left[src, PART + 16 : STACK, :] = low
    rows = jnp.concatenate(targets, axis=0)
    target_ref[...] = rows
    most = jnp.broadcast_to(jnp.max(carry, axis=0, keepdims=True), (8, LANES))
    first_row = iota((8, LANES), 0) == 0
    inside = (rows & (PAIR - 1)).astype(F32)
    turned = jnp.concatenate([inside, jnp.zeros((LANES - REPS, VEC), F32)], axis=0).T
    lane = iota((VEC, PAIR), 1).astype(F32)
    for src in range(REPS):
        hot[src] = jnp.where(turned[:, src : src + 1] == lane, 1.0, 0.0).astype(BF16)

    def group(n, _):
        total = jnp.zeros((STACK, PAIR), F32)
        for src in range(REPS):
            keep = jnp.where(group_of[src] == n, 1.0, 0.0).astype(BF16)
            kept = left[src] * jnp.concatenate([keep] * (STACK // 16), axis=0)
            total = total + jnp.dot(kept, hot[src], preferred_element_type=F32)
        values = total[0:PART] + total[PART + 16 : STACK]
        for half in range(2):
            cut = slice(half * LANES, (half + 1) * LANES)
            out_ref[2 * n + half, 0:PART, :] = values[:, cut]
            out_ref[2 * n + half, PART:ROWS, :] = jnp.where(
                first_row, total[PART : PART + 8, cut], most
            )
        return 0

    lax.fori_loop(0, groups, group, 0, unroll=4)


def load_pair(x_ref, n):
    x = jnp.concatenate([x_ref[2 * n, 0:PART, :], x_ref[2 * n + 1, 0:PART, :]], axis=1)
    slot = jnp.concatenate(
        [x_ref[2 * n, PART : PART + 1, :], x_ref[2 * n + 1, PART : PART + 1, :]], axis=1
    )
    return x, slot.astype(jnp.int32)


def stack_of(x):
    high, low = parts_of(x)
    return jnp.concatenate([high, jnp.ones((16, PAIR), BF16), low], axis=0)


def distance_kernel(blocks, x_ref, out_ref, most_ref, total, scaled):
    total[...] = jnp.zeros_like(total)
    most_ref[0] = jnp.max(x_ref[:, PART + 1, :]).astype(jnp.int32)

    def add(n, _):
        x, slot = load_pair(x_ref, n)
        hot = jnp.where(iota((SLOTS, PAIR), 0) + 1 == slot, 1.0, 0.0).astype(BF16)
        total[...] += lax.dot_general(stack_of(x), hot, NT, preferred_element_type=F32)
        return 0

    lax.fori_loop(0, blocks // 2, add, 0, unroll=8)
    sums = total[0:PART, :] + total[PART + 16 : STACK, :]
    counts = total[PART : PART + 8, :]
    high, low = parts_of(sums / (counts[0:1] + 1.0))
    high, low = high.astype(F32), low.astype(F32)
    first = high + low
    turned = jnp.concatenate([high, high, low, low], axis=0).T
    scaled[0:SLOTS, :] = (turned[:, 0 : 2 * PART] * -2.0).astype(BF16)
    scaled[SLOTS:, :] = (turned[:, 2 * PART : 4 * PART] * -2.0).astype(BF16)
    own = jnp.broadcast_to(jnp.sum(first * first, axis=0, keepdims=True), (LANES, SLOTS))
    row = iota((LANES, SLOTS), 0)
    columns = jnp.where(row == 0, jnp.broadcast_to(counts[0:1], (LANES, SLOTS)), own).T
    count = columns[:, 0:1].reshape(PAR_DEV, K, 1)
    mean = jnp.sum(count, axis=1, keepdims=True) / K
    extra = (0.5 * count / (mean + 1.0)).reshape(SLOTS, 1) / REPS
    own = columns[:, 1:2]

    def measure(n, _):
        x, slot = load_pair(x_ref, n)
        both = jnp.dot(
            scaled[...], jnp.concatenate(parts_of(x), axis=0), preferred_element_type=F32
        )
        cross = both[0:SLOTS] + both[SLOTS : 2 * SLOTS]
        parent = (slot - 1) >> 3
        terms = ((cross + own) / D + extra).reshape(PAR_DEV, K, PAIR)
        picked = jnp.where(iota((PAR_DEV, K, PAIR), 0) == parent[None], terms, 0.0)
        part = jnp.sum(picked, axis=0) + jnp.sum(x * x, axis=0, keepdims=True) / D
        out_ref[2 * n] = part[:, 0:LANES]
        out_ref[2 * n + 1] = part[:, LANES:PAIR]
        return 0

    lax.fori_loop(0, blocks // 2, measure, 0, unroll=8)


def share_kernel(blocks, x_ref, pen_ref, cent_ref, share_ref, total, rest):
    total[...] = jnp.zeros_like(total)
    rest[...] = jnp.zeros_like(rest)

    def add(n, _):
        x, slot = load_pair(x_ref, n)
        grown = 1.0 + jnp.concatenate([pen_ref[2 * n], pen_ref[2 * n + 1]], axis=1)
        square = grown * grown
        weight = 1.0 / (square * square)
        share = weight / jnp.sum(weight, axis=0, keepdims=True)
        share = jnp.where(slot > 0, share, 0.0)
        share_ref[2 * n] = share[:, 0:LANES]
        share_ref[2 * n + 1] = share[:, LANES:PAIR]
        parent = (slot - 1) >> 3
        mixing = jnp.where(
            iota((PAR_DEV, K, PAIR), 0) == parent[None], share[None], 0.0
        ).reshape(SLOTS, PAIR)
        high, low = parts_of(mixing)
        left = stack_of(x)
        total[...] += lax.dot_general(left, high, NT, preferred_element_type=F32)
        rest[...] += lax.dot_general(
            left[0 : PART + 16], low, NT, preferred_element_type=F32
        )
        return 0

    lax.fori_loop(0, blocks // 2, add, 0, unroll=8)
    weighted = total[0:PART, :] + total[PART + 16 : STACK, :] + rest[0:PART, :]
    summed = total[PART : PART + 1, :] + rest[PART : PART + 1, :]
    cent_ref[...] = weighted / (summed + 1.0)


def join_kernel(at_ref, *refs):
    *pieces, out_ref, whole, columns, sems = refs
    x, core = at_ref[0], at_ref[1]
    for index, piece in enumerate(pieces):
        step, other = divmod(index, 2)
        where = ((x - step) & 3) * 2 + (core ^ other)
        whole[pl.ds(pl.multiple_of(where * PART, 8), PART), :] = piece[...]
    copies = []
    for tile in range(TILES):
        columns[tile] = whole[tile * LANES : (tile + 1) * LANES, :].T
        copies.append(
            pltpu.make_async_copy(
                columns.at[tile], out_ref.at[:, pl.ds(tile * LANES, LANES)], sems.at[tile]
            )
        )
        copies[-1].start()
    for copy in copies:
        copy.wait()


def take_kernel(blocks, at_ref, back_ref, target_ref, out_ref):
    target = target_ref[pl.ds(at_ref[2], 1), :]
    total = jnp.zeros((3 * K, VEC), F32)
    for n in range(blocks):
        hot = jnp.where(iota((LANES, VEC), 0) + n * LANES == target, 1.0, 0.0).astype(BF16)
        high, low = parts_of(back_ref[n])
        least = (back_ref[n] - high.astype(F32) - low.astype(F32)).astype(BF16)
        left = jnp.concatenate([high.astype(F32), low.astype(F32), least.astype(F32)], axis=0)
        total = total + jnp.dot(left.astype(BF16), hot, preferred_element_type=F32)
    out_ref[...] = total[0:K] + total[K : 2 * K] + total[2 * K : 3 * K]


def shape(*dims, kind=F32):
    return jax.ShapeDtypeStruct(dims, kind)


def cost(flops, data):
    return pl.CostEstimate(flops=flops, bytes_accessed=data, transcendentals=0)


def along_x(step):
    return [(i, ((i // 2 + step) % 4) * 2 + i % 2) for i in range(REPS)]


BY_CORE = [0, 2, 4, 6, 1, 3, 5, 7]
CORES = [(i, i ^ 1) for i in range(REPS)]


def sum_over_rep(x):
    x = x + lax.ppermute(x, "rep", CORES)
    x = x + lax.ppermute(x, "rep", [(i, i ^ 2) for i in range(REPS)])
    return x + lax.ppermute(x, "rep", [(i, i ^ 6) for i in range(REPS)])


SMEM = pl.BlockSpec(memory_space=pltpu.SMEM)
VMEM = pl.BlockSpec(memory_space=pltpu.VMEM)
ANY = pl.BlockSpec(memory_space=pltpu.HBM)


def refine(cap, got):
    blocks = OWNERS * cap // LANES
    packed, target = pl.pallas_call(
        functools.partial(pack_kernel, cap),
        out_shape=(
            shape(blocks, ROWS, LANES),
            shape(REPS, VEC, kind=jnp.int32),
        ),
        scratch_shapes=[
            pltpu.VMEM((REPS, STACK, VEC), BF16),
            pltpu.VMEM((REPS, VEC, PAIR), BF16),
            pltpu.VMEM((REPS, 16, VEC), jnp.int32),
        ],
        compiler_params=params(),
        cost_estimate=cost(2 * STACK * 2048 * OWNERS * cap, 3_000_000),
        name="pack",
    )(got)
    per = cap // LANES
    rows = lax.all_to_all(
        packed.reshape(OWNERS, per * ROWS, LANES), "cluster", 0, 0, tiled=True
    ).reshape(blocks, ROWS, LANES)
    partial, most = pl.pallas_call(
        functools.partial(distance_kernel, blocks),
        out_shape=(shape(blocks, K, LANES), shape(1, kind=jnp.int32)),
        out_specs=(VMEM, SMEM),
        scratch_shapes=[
            pltpu.VMEM((STACK, SLOTS), F32),
            pltpu.VMEM((2 * SLOTS, 2 * PART), BF16),
        ],
        compiler_params=params(),
        cost_estimate=cost(2 * 8 * PART * SLOTS * OWNERS * cap, 2_000_000),
        name="distance",
    )(rows)
    pen = sum_over_rep(partial)
    cent, share = pl.pallas_call(
        functools.partial(share_kernel, blocks),
        out_shape=(shape(PART, SLOTS), shape(blocks, K, LANES)),
        scratch_shapes=[
            pltpu.VMEM((STACK, SLOTS), F32),
            pltpu.VMEM((PART + 16, SLOTS), F32),
        ],
        compiler_params=params(),
        cost_estimate=cost(2 * 3 * PART * SLOTS * OWNERS * cap, 2_000_000),
        name="share",
    )(rows, pen)
    back = lax.all_to_all(
        share.reshape(OWNERS, per * K, LANES), "cluster", 0, 0, tiled=True
    ).reshape(blocks, K, LANES)
    pieces = []
    for step in range(4):
        mine = lax.ppermute(cent, "rep", along_x(step)) if step else cent
        pieces += [mine, lax.ppermute(mine, "rep", CORES)]
    return pieces, back, target, most


def place():
    rep = lax.axis_index("rep")
    return jnp.stack([rep // 2, rep % 2, rep % 2 * 4 + rep // 2]).astype(jnp.int32)


def join(pieces):
    return pl.pallas_call(
        join_kernel,
        out_shape=shape(SLOTS, D),
        in_specs=[SMEM] + [VMEM] * REPS,
        out_specs=ANY,
        scratch_shapes=[
            pltpu.VMEM((D, SLOTS), F32),
            pltpu.VMEM((TILES, SLOTS, LANES), F32),
            pltpu.SemaphoreType.DMA((TILES,)),
        ],
        compiler_params=params(63700),
        cost_estimate=cost(0, 1_600_000),
        name="join",
    )(place(), *pieces)


def take(cap, back, target):
    blocks = OWNERS * cap // LANES
    return pl.pallas_call(
        functools.partial(take_kernel, blocks),
        out_shape=shape(K, VEC),
        in_specs=[SMEM, VMEM, VMEM],
        compiler_params=params(),
        cost_estimate=cost(2 * 24 * VEC * OWNERS * cap, 200_000),
        name="take",
    )(place(), back, target)


def on_device(vectors, parent_id, child_id):
    slot = (parent_id * K + child_id).astype(F32).reshape(1, VEC)
    turned = pl.pallas_call(
        turn_kernel,
        out_shape=shape(REPS, ROWS, VEC),
        compiler_params=params(),
        cost_estimate=cost(0, 1_600_000),
        name="turn",
    )(vectors, slot)
    got = lax.all_to_all(
        turned, "rep", 0, 0, axis_index_groups=[BY_CORE], tiled=True
    )
    pieces, back, target, most = refine(LANES, got)
    over = most[0] > LANES

    picked = take(LANES, back, target)

    def wide(got, pieces, picked):
        pieces, back, target, _ = refine(PAIR, got)
        return join(pieces), take(PAIR, back, target)

    def narrow(got, pieces, picked):
        return join(pieces), picked

    centroids, shares = lax.cond(over, wide, narrow, got, pieces, picked)
    return centroids, shares.T


def solution(mesh):
    in_specs = (P(("cluster", "rep"), None), P(("cluster", "rep")), P(("cluster", "rep")))
    out_specs = (P("cluster", None), P(("cluster", "rep"), None))
    return jax.shard_map(
        on_device, mesh=mesh, in_specs=in_specs, out_specs=out_specs, check_vma=False
    )
```

```python
import functools

import jax
import jax.numpy as jnp
from jax import lax
from jax.experimental import pallas as pl
from jax.experimental.pallas import tpu as pltpu
from jax.sharding import PartitionSpec as P

K = 8
PAR_DEV = 32
OWNERS = 32
REPS = 8
SLOTS = PAR_DEV * K
D = 768
PART = D // REPS
ROWS = PART + 8
VEC = 256
LANES = 128
PAIR = 2 * LANES
STACK = PART + 16 + PART
F32 = jnp.float32
BF16 = jnp.bfloat16
NT = (((1,), (1,)), ((), ()))


def params():
    return pltpu.CompilerParams(vmem_limit_bytes=48 * 2**20)


def iota(shape, dim):
    return lax.broadcasted_iota(jnp.int32, shape, dim)


def parts_of(x):
    high = x.astype(BF16)
    return high, (x - high.astype(F32)).astype(BF16)


def turn_kernel(v_ref, g_ref, out_ref):
    for tile in range(D // LANES):
        turned = v_ref[:, tile * LANES : (tile + 1) * LANES].T
        start = tile * LANES
        while start < (tile + 1) * LANES:
            part, row = divmod(start, PART)
            size = min(PART - row, (tile + 1) * LANES - start)
            at = start - tile * LANES
            out_ref[BY_CORE.index(part), row : row + size, :] = turned[at : at + size, :]
            start += size
    slots = jnp.broadcast_to(g_ref[...], (ROWS - PART, VEC))
    for part in range(REPS):
        out_ref[part, PART:ROWS, :] = slots


def pack_kernel(cap, in_ref, out_ref, target_ref, left, column):
    groups = OWNERS * cap // PAIR
    before = (iota((VEC, VEC), 0) < iota((VEC, VEC), 1)).astype(F32).astype(BF16)
    carry = jnp.zeros((OWNERS, 1), F32)
    targets = []
    for src in range(REPS):
        slot = in_ref[src, PART : PART + 1, :].astype(jnp.int32)
        owner = slot >> 8
        local = (slot & (SLOTS - 1)) + 1
        hot = (owner == iota((OWNERS, VEC), 0)).astype(F32)
        ahead = jnp.dot(hot.astype(BF16), before, preferred_element_type=F32) + carry
        position = jnp.sum(hot * ahead, axis=0, keepdims=True)
        carry = carry + jnp.sum(hot, axis=1, keepdims=True)
        target = owner.astype(F32) * cap + position
        targets.append(jnp.where(position < cap, target, -1.0))
        high, low = parts_of(in_ref[src, 0:PART, :])
        left[src, 0:PART, :] = high
        left[src, PART : PART + 16, :] = jnp.broadcast_to(local.astype(F32), (16, VEC)).astype(BF16)
        left[src, PART + 16 : STACK, :] = low
    rows = jnp.concatenate(targets, axis=0)
    target_ref[...] = rows.astype(jnp.int32)
    most = jnp.broadcast_to(jnp.max(carry, axis=0, keepdims=True), (8, LANES))
    first_row = iota((8, LANES), 0) == 0
    turned = jnp.concatenate([rows, jnp.zeros((LANES - REPS, VEC), F32)], axis=0).T
    for src in range(REPS):
        column[src] = jnp.broadcast_to(turned[:, src : src + 1], (VEC, LANES))
    lane = iota((VEC, LANES), 1).astype(F32)

    def group(n, _):
        base = (n * PAIR).astype(F32)
        total = jnp.zeros((STACK, PAIR), F32)
        for src in range(REPS):
            at = column[src] - base
            hot = jnp.concatenate(
                [
                    jnp.where(at == lane, 1.0, 0.0).astype(BF16),
                    jnp.where(at == lane + LANES, 1.0, 0.0).astype(BF16),
                ],
                axis=1,
            )
            total = total + jnp.dot(left[src], hot, preferred_element_type=F32)
        values = total[0:PART] + total[PART + 16 : STACK]
        for half in range(2):
            cut = slice(half * LANES, (half + 1) * LANES)
            out_ref[2 * n + half, 0:PART, :] = values[:, cut]
            out_ref[2 * n + half, PART:ROWS, :] = jnp.where(
                first_row, total[PART : PART + 8, cut], most
            )
        return 0

    lax.fori_loop(0, groups, group, 0, unroll=4)


def load_pair(x_ref, n):
    x = jnp.concatenate([x_ref[2 * n, 0:PART, :], x_ref[2 * n + 1, 0:PART, :]], axis=1)
    slot = jnp.concatenate(
        [x_ref[2 * n, PART : PART + 1, :], x_ref[2 * n + 1, PART : PART + 1, :]], axis=1
    )
    return x, slot.astype(jnp.int32)


def stack_of(x):
    high, low = parts_of(x)
    return jnp.concatenate([high, jnp.ones((16, PAIR), BF16), low], axis=0)


def distance_kernel(blocks, x_ref, out_ref, most_ref, total, scaled):
    total[...] = jnp.zeros_like(total)
    most_ref[0] = jnp.max(x_ref[:, PART + 1, :]).astype(jnp.int32)

    def add(n, _):
        x, slot = load_pair(x_ref, n)
        hot = jnp.where(iota((SLOTS, PAIR), 0) + 1 == slot, 1.0, 0.0).astype(BF16)
        total[...] += lax.dot_general(stack_of(x), hot, NT, preferred_element_type=F32)
        return 0

    lax.fori_loop(0, blocks // 2, add, 0, unroll=8)
    sums = total[0:PART, :] + total[PART + 16 : STACK, :]
    counts = total[PART : PART + 8, :]
    high, low = parts_of(sums / (counts[0:1] + 1.0))
    high, low = high.astype(F32), low.astype(F32)
    first = high + low
    turned = jnp.concatenate([high, high, low, low], axis=0).T
    scaled[0:SLOTS, :] = (turned[:, 0 : 2 * PART] * -2.0).astype(BF16)
    scaled[SLOTS:, :] = (turned[:, 2 * PART : 4 * PART] * -2.0).astype(BF16)
    own = jnp.broadcast_to(jnp.sum(first * first, axis=0, keepdims=True), (LANES, SLOTS))
    row = iota((LANES, SLOTS), 0)
    columns = jnp.where(row == 0, jnp.broadcast_to(counts[0:1], (LANES, SLOTS)), own).T
    count = columns[:, 0:1].reshape(PAR_DEV, K, 1)
    mean = jnp.sum(count, axis=1, keepdims=True) / K
    extra = (0.5 * count / (mean + 1.0)).reshape(SLOTS, 1) / REPS
    own = columns[:, 1:2]

    def measure(n, _):
        x, slot = load_pair(x_ref, n)
        both = jnp.dot(
            scaled[...], jnp.concatenate(parts_of(x), axis=0), preferred_element_type=F32
        )
        cross = both[0:SLOTS] + both[SLOTS : 2 * SLOTS]
        parent = (slot - 1) >> 3
        terms = ((cross + own) / D + extra).reshape(PAR_DEV, K, PAIR)
        picked = jnp.where(iota((PAR_DEV, K, PAIR), 0) == parent[None], terms, 0.0)
        part = jnp.sum(picked, axis=0) + jnp.sum(x * x, axis=0, keepdims=True) / D
        out_ref[2 * n] = part[:, 0:LANES]
        out_ref[2 * n + 1] = part[:, LANES:PAIR]
        return 0

    lax.fori_loop(0, blocks // 2, measure, 0, unroll=8)


def share_kernel(blocks, x_ref, pen_ref, cent_ref, share_ref, total, rest):
    total[...] = jnp.zeros_like(total)
    rest[...] = jnp.zeros_like(rest)

    def add(n, _):
        x, slot = load_pair(x_ref, n)
        grown = 1.0 + jnp.concatenate([pen_ref[2 * n], pen_ref[2 * n + 1]], axis=1)
        square = grown * grown
        weight = 1.0 / (square * square)
        share = weight / jnp.sum(weight, axis=0, keepdims=True)
        share = jnp.where(slot > 0, share, 0.0)
        share_ref[2 * n] = share[:, 0:LANES]
        share_ref[2 * n + 1] = share[:, LANES:PAIR]
        parent = (slot - 1) >> 3
        mixing = jnp.where(
            iota((PAR_DEV, K, PAIR), 0) == parent[None], share[None], 0.0
        ).reshape(SLOTS, PAIR)
        high, low = parts_of(mixing)
        left = stack_of(x)
        total[...] += lax.dot_general(left, high, NT, preferred_element_type=F32)
        rest[...] += lax.dot_general(
            left[0 : PART + 16], low, NT, preferred_element_type=F32
        )
        return 0

    lax.fori_loop(0, blocks // 2, add, 0, unroll=8)
    weighted = total[0:PART, :] + total[PART + 16 : STACK, :] + rest[0:PART, :]
    summed = total[PART : PART + 1, :] + rest[PART : PART + 1, :]
    cent_ref[...] = weighted / (summed + 1.0)


def join_kernel(at_ref, *refs):
    *pieces, out_ref, whole = refs
    x, core = at_ref[0], at_ref[1]
    for index, piece in enumerate(pieces):
        other, far = divmod(index, 2)
        for step in range(2):
            where = ((x - 2 * far - step) & 3) * 2 + (core ^ other)
            whole[pl.ds(pl.multiple_of(where * PART, 8), PART), :] = piece[step]
    for tile in range(D // LANES):
        cut = slice(tile * LANES, (tile + 1) * LANES)
        out_ref[:, cut] = whole[cut, :].T


def take_kernel(blocks, at_ref, back_ref, target_ref, out_ref):
    target = target_ref[pl.ds(at_ref[2], 1), :]
    total = jnp.zeros((3 * K, VEC), F32)
    for n in range(blocks):
        hot = jnp.where(iota((LANES, VEC), 0) + n * LANES == target, 1.0, 0.0).astype(BF16)
        high, low = parts_of(back_ref[n])
        least = (back_ref[n] - high.astype(F32) - low.astype(F32)).astype(BF16)
        left = jnp.concatenate([high.astype(F32), low.astype(F32), least.astype(F32)], axis=0)
        total = total + jnp.dot(left.astype(BF16), hot, preferred_element_type=F32)
    out_ref[...] = total[0:K] + total[K : 2 * K] + total[2 * K : 3 * K]


def shape(*dims, kind=F32):
    return jax.ShapeDtypeStruct(dims, kind)


def cost(flops, data):
    return pl.CostEstimate(flops=flops, bytes_accessed=data, transcendentals=0)


def along_x(step):
    return [(i, ((i // 2 + step) % 4) * 2 + i % 2) for i in range(REPS)]


BY_CORE = [0, 2, 4, 6, 1, 3, 5, 7]
CORES = [(i, i ^ 1) for i in range(REPS)]


def sum_over_rep(x):
    x = x + lax.ppermute(x, "rep", CORES)
    x = x + lax.ppermute(x, "rep", [(i, i ^ 2) for i in range(REPS)])
    return x + lax.ppermute(x, "rep", [(i, i ^ 6) for i in range(REPS)])


SMEM = pl.BlockSpec(memory_space=pltpu.SMEM)
VMEM = pl.BlockSpec(memory_space=pltpu.VMEM)


def refine(cap, got):
    blocks = OWNERS * cap // LANES
    packed, target = pl.pallas_call(
        functools.partial(pack_kernel, cap),
        out_shape=(
            shape(blocks, ROWS, LANES),
            shape(REPS, VEC, kind=jnp.int32),
        ),
        scratch_shapes=[pltpu.VMEM((REPS, STACK, VEC), BF16), pltpu.VMEM((REPS, VEC, LANES), F32)],
        compiler_params=params(),
        cost_estimate=cost(2 * STACK * 2048 * OWNERS * cap, 3_000_000),
        name="pack",
    )(got)
    per = cap // LANES
    rows = lax.all_to_all(
        packed.reshape(OWNERS, per * ROWS, LANES), "cluster", 0, 0, tiled=True
    ).reshape(blocks, ROWS, LANES)
    partial, most = pl.pallas_call(
        functools.partial(distance_kernel, blocks),
        out_shape=(shape(blocks, K, LANES), shape(1, kind=jnp.int32)),
        out_specs=(VMEM, SMEM),
        scratch_shapes=[
            pltpu.VMEM((STACK, SLOTS), F32),
            pltpu.VMEM((2 * SLOTS, 2 * PART), BF16),
        ],
        compiler_params=params(),
        cost_estimate=cost(2 * 8 * PART * SLOTS * OWNERS * cap, 2_000_000),
        name="distance",
    )(rows)
    pen = sum_over_rep(partial)
    cent, share = pl.pallas_call(
        functools.partial(share_kernel, blocks),
        out_shape=(shape(PART, SLOTS), shape(blocks, K, LANES)),
        scratch_shapes=[
            pltpu.VMEM((STACK, SLOTS), F32),
            pltpu.VMEM((PART + 16, SLOTS), F32),
        ],
        compiler_params=params(),
        cost_estimate=cost(2 * 3 * PART * SLOTS * OWNERS * cap, 2_000_000),
        name="share",
    )(rows, pen)
    back = lax.all_to_all(
        share.reshape(OWNERS, per * K, LANES), "cluster", 0, 0, tiled=True
    ).reshape(blocks, K, LANES)
    near = jnp.stack([cent, lax.ppermute(cent, "rep", along_x(1))])
    far = jnp.stack([lax.ppermute(cent, "rep", along_x(step)) for step in (2, 3)])
    pieces = [near, far, lax.ppermute(near, "rep", CORES), lax.ppermute(far, "rep", CORES)]
    return pieces, back, target, most


def place():
    rep = lax.axis_index("rep")
    return jnp.stack([rep // 2, rep % 2, rep % 2 * 4 + rep // 2]).astype(jnp.int32)


def join(pieces):
    return pl.pallas_call(
        join_kernel,
        out_shape=shape(SLOTS, D),
        in_specs=[SMEM] + [VMEM] * 4,
        scratch_shapes=[pltpu.VMEM((D, SLOTS), F32)],
        compiler_params=params(),
        cost_estimate=cost(0, 1_600_000),
        name="join",
    )(place(), *pieces)


def take(cap, back, target):
    blocks = OWNERS * cap // LANES
    return pl.pallas_call(
        functools.partial(take_kernel, blocks),
        out_shape=shape(K, VEC),
        in_specs=[SMEM, VMEM, VMEM],
        compiler_params=params(),
        cost_estimate=cost(2 * 24 * VEC * OWNERS * cap, 200_000),
        name="take",
    )(place(), back, target)


def on_device(vectors, parent_id, child_id):
    slot = (parent_id * K + child_id).astype(F32).reshape(1, VEC)
    turned = pl.pallas_call(
        turn_kernel,
        out_shape=shape(REPS, ROWS, VEC),
        compiler_params=params(),
        cost_estimate=cost(0, 1_600_000),
        name="turn",
    )(vectors, slot)
    got = lax.all_to_all(
        turned, "rep", 0, 0, axis_index_groups=[BY_CORE], tiled=True
    )
    pieces, back, target, most = refine(LANES, got)
    over = most[0] > LANES

    picked = take(LANES, back, target)

    def wide(got, pieces, picked):
        pieces, back, target, _ = refine(PAIR, got)
        return join(pieces), take(PAIR, back, target)

    def narrow(got, pieces, picked):
        return join(pieces), picked

    centroids, shares = lax.cond(over, wide, narrow, got, pieces, picked)
    return centroids, shares.T


def solution(mesh):
    in_specs = (P(("cluster", "rep"), None), P(("cluster", "rep")), P(("cluster", "rep")))
    out_specs = (P("cluster", None), P(("cluster", "rep"), None))
    return jax.shard_map(
        on_device, mesh=mesh, in_specs=in_specs, out_specs=out_specs, check_vma=False
    )
```

```python
import functools

import jax
import jax.numpy as jnp
from jax import lax
from jax.experimental import pallas as pl
from jax.experimental.pallas import tpu as pltpu
from jax.sharding import PartitionSpec as P

K = 8
PAR_DEV = 32
OWNERS = 32
REPS = 8
SLOTS = PAR_DEV * K
D = 768
PART = D // REPS
ROWS = PART + 8
VEC = 256
LANES = 128
PAIR = 2 * LANES
STACK = PART + 16 + PART
F32 = jnp.float32
BF16 = jnp.bfloat16
NT = (((1,), (1,)), ((), ()))


def params():
    return pltpu.CompilerParams(vmem_limit_bytes=48 * 2**20)


def iota(shape, dim):
    return lax.broadcasted_iota(jnp.int32, shape, dim)


def parts_of(x):
    high = x.astype(BF16)
    return high, (x - high.astype(F32)).astype(BF16)


def turn_kernel(v_ref, g_ref, out_ref):
    for tile in range(D // LANES):
        turned = v_ref[:, tile * LANES : (tile + 1) * LANES].T
        start = tile * LANES
        while start < (tile + 1) * LANES:
            part, row = divmod(start, PART)
            size = min(PART - row, (tile + 1) * LANES - start)
            at = start - tile * LANES
            out_ref[BY_CORE.index(part), row : row + size, :] = turned[at : at + size, :]
            start += size
    slots = jnp.broadcast_to(g_ref[...], (ROWS - PART, VEC))
    for part in range(REPS):
        out_ref[part, PART:ROWS, :] = slots


def pack_kernel(cap, in_ref, out_ref, target_ref, left, column):
    groups = OWNERS * cap // PAIR
    before = (iota((VEC, VEC), 0) < iota((VEC, VEC), 1)).astype(F32).astype(BF16)
    carry = jnp.zeros((OWNERS, 1), F32)
    targets = []
    for src in range(REPS):
        slot = in_ref[src, PART : PART + 1, :].astype(jnp.int32)
        owner = slot >> 8
        local = (slot & (SLOTS - 1)) + 1
        hot = (owner == iota((OWNERS, VEC), 0)).astype(F32)
        ahead = jnp.dot(hot.astype(BF16), before, preferred_element_type=F32) + carry
        position = jnp.sum(hot * ahead, axis=0, keepdims=True)
        carry = carry + jnp.sum(hot, axis=1, keepdims=True)
        target = owner.astype(F32) * cap + position
        targets.append(jnp.where(position < cap, target, -1.0))
        high, low = parts_of(in_ref[src, 0:PART, :])
        left[src, 0:PART, :] = high
        left[src, PART : PART + 16, :] = jnp.broadcast_to(local.astype(F32), (16, VEC)).astype(BF16)
        left[src, PART + 16 : STACK, :] = low
    rows = jnp.concatenate(targets, axis=0)
    target_ref[...] = rows.astype(jnp.int32)
    most = jnp.broadcast_to(jnp.max(carry, axis=0, keepdims=True), (8, LANES))
    first_row = iota((8, LANES), 0) == 0
    turned = jnp.concatenate([rows, jnp.zeros((LANES - REPS, VEC), F32)], axis=0).T
    for src in range(REPS):
        column[src] = jnp.broadcast_to(turned[:, src : src + 1], (VEC, LANES))
    lane = iota((VEC, LANES), 1).astype(F32)

    def group(n, _):
        base = (n * PAIR).astype(F32)
        total = jnp.zeros((STACK, PAIR), F32)
        for src in range(REPS):
            at = column[src] - base
            hot = jnp.concatenate(
                [
                    jnp.where(at == lane, 1.0, 0.0).astype(BF16),
                    jnp.where(at == lane + LANES, 1.0, 0.0).astype(BF16),
                ],
                axis=1,
            )
            total = total + jnp.dot(left[src], hot, preferred_element_type=F32)
        values = total[0:PART] + total[PART + 16 : STACK]
        for half in range(2):
            cut = slice(half * LANES, (half + 1) * LANES)
            out_ref[2 * n + half, 0:PART, :] = values[:, cut]
            out_ref[2 * n + half, PART:ROWS, :] = jnp.where(
                first_row, total[PART : PART + 8, cut], most
            )
        return 0

    lax.fori_loop(0, groups, group, 0, unroll=8)


def load_pair(x_ref, n):
    x = jnp.concatenate([x_ref[2 * n, 0:PART, :], x_ref[2 * n + 1, 0:PART, :]], axis=1)
    slot = jnp.concatenate(
        [x_ref[2 * n, PART : PART + 1, :], x_ref[2 * n + 1, PART : PART + 1, :]], axis=1
    )
    return x, slot.astype(jnp.int32)


def stack_of(x):
    high, low = parts_of(x)
    return jnp.concatenate([high, jnp.ones((16, PAIR), BF16), low], axis=0)


def distance_kernel(blocks, x_ref, out_ref, most_ref, total, scaled):
    total[...] = jnp.zeros_like(total)
    most_ref[0] = jnp.max(x_ref[:, PART + 1, :]).astype(jnp.int32)

    def add(n, _):
        x, slot = load_pair(x_ref, n)
        hot = jnp.where(iota((SLOTS, PAIR), 0) + 1 == slot, 1.0, 0.0).astype(BF16)
        total[...] += lax.dot_general(stack_of(x), hot, NT, preferred_element_type=F32)
        return 0

    lax.fori_loop(0, blocks // 2, add, 0, unroll=16)
    sums = total[0:PART, :] + total[PART + 16 : STACK, :]
    counts = total[PART : PART + 8, :]
    high, low = parts_of(sums / (counts[0:1] + 1.0))
    high, low = high.astype(F32), low.astype(F32)
    first = high + low
    turned = jnp.concatenate([high, high, low, low], axis=0).T
    scaled[0:SLOTS, :] = (turned[:, 0 : 2 * PART] * -2.0).astype(BF16)
    scaled[SLOTS:, :] = (turned[:, 2 * PART : 4 * PART] * -2.0).astype(BF16)
    own = jnp.broadcast_to(jnp.sum(first * first, axis=0, keepdims=True), (LANES, SLOTS))
    row = iota((LANES, SLOTS), 0)
    columns = jnp.where(row == 0, jnp.broadcast_to(counts[0:1], (LANES, SLOTS)), own).T
    count = columns[:, 0:1].reshape(PAR_DEV, K, 1)
    mean = jnp.sum(count, axis=1, keepdims=True) / K
    extra = (0.5 * count / (mean + 1.0)).reshape(SLOTS, 1) / REPS
    own = columns[:, 1:2]

    def measure(n, _):
        x, slot = load_pair(x_ref, n)
        both = jnp.dot(
            scaled[...], jnp.concatenate(parts_of(x), axis=0), preferred_element_type=F32
        )
        cross = both[0:SLOTS] + both[SLOTS : 2 * SLOTS]
        parent = (slot - 1) >> 3
        terms = ((cross + own) / D + extra).reshape(PAR_DEV, K, PAIR)
        picked = jnp.where(iota((PAR_DEV, K, PAIR), 0) == parent[None], terms, 0.0)
        part = jnp.sum(picked, axis=0) + jnp.sum(x * x, axis=0, keepdims=True) / D
        out_ref[2 * n] = part[:, 0:LANES]
        out_ref[2 * n + 1] = part[:, LANES:PAIR]
        return 0

    lax.fori_loop(0, blocks // 2, measure, 0, unroll=16)


def share_kernel(blocks, x_ref, pen_ref, cent_ref, share_ref, total, rest):
    total[...] = jnp.zeros_like(total)
    rest[...] = jnp.zeros_like(rest)

    def add(n, _):
        x, slot = load_pair(x_ref, n)
        grown = 1.0 + jnp.concatenate([pen_ref[2 * n], pen_ref[2 * n + 1]], axis=1)
        square = grown * grown
        weight = 1.0 / (square * square)
        share = weight / jnp.sum(weight, axis=0, keepdims=True)
        share = jnp.where(slot > 0, share, 0.0)
        share_ref[2 * n] = share[:, 0:LANES]
        share_ref[2 * n + 1] = share[:, LANES:PAIR]
        parent = (slot - 1) >> 3
        mixing = jnp.where(
            iota((PAR_DEV, K, PAIR), 0) == parent[None], share[None], 0.0
        ).reshape(SLOTS, PAIR)
        high, low = parts_of(mixing)
        left = stack_of(x)
        total[...] += lax.dot_general(left, high, NT, preferred_element_type=F32)
        rest[...] += lax.dot_general(
            left[0 : PART + 16], low, NT, preferred_element_type=F32
        )
        return 0

    lax.fori_loop(0, blocks // 2, add, 0, unroll=16)
    weighted = total[0:PART, :] + total[PART + 16 : STACK, :] + rest[0:PART, :]
    summed = total[PART : PART + 1, :] + rest[PART : PART + 1, :]
    cent_ref[...] = weighted / (summed + 1.0)


def join_kernel(at_ref, *refs):
    *pieces, out_ref, whole = refs
    x, core = at_ref[0], at_ref[1]
    for index, piece in enumerate(pieces):
        step, other = divmod(index, 2)
        where = ((x - step) & 3) * 2 + (core ^ other)
        whole[pl.ds(pl.multiple_of(where * PART, 8), PART), :] = piece[...]
    for tile in range(D // LANES):
        cut = slice(tile * LANES, (tile + 1) * LANES)
        out_ref[:, cut] = whole[cut, :].T


def take_kernel(blocks, at_ref, back_ref, target_ref, out_ref):
    target = target_ref[pl.ds(at_ref[2], 1), :]
    total = jnp.zeros((3 * K, VEC), F32)
    for n in range(blocks):
        hot = jnp.where(iota((LANES, VEC), 0) + n * LANES == target, 1.0, 0.0).astype(BF16)
        high, low = parts_of(back_ref[n])
        least = (back_ref[n] - high.astype(F32) - low.astype(F32)).astype(BF16)
        left = jnp.concatenate([high.astype(F32), low.astype(F32), least.astype(F32)], axis=0)
        total = total + jnp.dot(left.astype(BF16), hot, preferred_element_type=F32)
    out_ref[...] = total[0:K] + total[K : 2 * K] + total[2 * K : 3 * K]


def shape(*dims, kind=F32):
    return jax.ShapeDtypeStruct(dims, kind)


def cost(flops, data):
    return pl.CostEstimate(flops=flops, bytes_accessed=data, transcendentals=0)


def along_x(step):
    return [(i, ((i // 2 + step) % 4) * 2 + i % 2) for i in range(REPS)]


BY_CORE = [0, 2, 4, 6, 1, 3, 5, 7]
CORES = [(i, i ^ 1) for i in range(REPS)]


def sum_over_rep(x):
    x = x + lax.ppermute(x, "rep", CORES)
    x = x + lax.ppermute(x, "rep", [(i, i ^ 2) for i in range(REPS)])
    return x + lax.ppermute(x, "rep", [(i, i ^ 6) for i in range(REPS)])


SMEM = pl.BlockSpec(memory_space=pltpu.SMEM)
VMEM = pl.BlockSpec(memory_space=pltpu.VMEM)


def refine(cap, got):
    blocks = OWNERS * cap // LANES
    packed, target = pl.pallas_call(
        functools.partial(pack_kernel, cap),
        out_shape=(
            shape(blocks, ROWS, LANES),
            shape(REPS, VEC, kind=jnp.int32),
        ),
        scratch_shapes=[pltpu.VMEM((REPS, STACK, VEC), BF16), pltpu.VMEM((REPS, VEC, LANES), F32)],
        compiler_params=params(),
        cost_estimate=cost(2 * STACK * 2048 * OWNERS * cap, 3_000_000),
        name="pack",
    )(got)
    per = cap // LANES
    rows = lax.all_to_all(
        packed.reshape(OWNERS, per * ROWS, LANES), "cluster", 0, 0, tiled=True
    ).reshape(blocks, ROWS, LANES)
    partial, most = pl.pallas_call(
        functools.partial(distance_kernel, blocks),
        out_shape=(shape(blocks, K, LANES), shape(1, kind=jnp.int32)),
        out_specs=(VMEM, SMEM),
        scratch_shapes=[
            pltpu.VMEM((STACK, SLOTS), F32),
            pltpu.VMEM((2 * SLOTS, 2 * PART), BF16),
        ],
        compiler_params=params(),
        cost_estimate=cost(2 * 8 * PART * SLOTS * OWNERS * cap, 2_000_000),
        name="distance",
    )(rows)
    pen = sum_over_rep(partial)
    cent, share = pl.pallas_call(
        functools.partial(share_kernel, blocks),
        out_shape=(shape(PART, SLOTS), shape(blocks, K, LANES)),
        scratch_shapes=[
            pltpu.VMEM((STACK, SLOTS), F32),
            pltpu.VMEM((PART + 16, SLOTS), F32),
        ],
        compiler_params=params(),
        cost_estimate=cost(2 * 3 * PART * SLOTS * OWNERS * cap, 2_000_000),
        name="share",
    )(rows, pen)
    back = lax.all_to_all(
        share.reshape(OWNERS, per * K, LANES), "cluster", 0, 0, tiled=True
    ).reshape(blocks, K, LANES)
    pieces = []
    for step in range(4):
        mine = lax.ppermute(cent, "rep", along_x(step)) if step else cent
        pieces += [mine, lax.ppermute(mine, "rep", CORES)]
    return pieces, back, target, most


def place():
    rep = lax.axis_index("rep")
    return jnp.stack([rep // 2, rep % 2, rep % 2 * 4 + rep // 2]).astype(jnp.int32)


def join(pieces):
    return pl.pallas_call(
        join_kernel,
        out_shape=shape(SLOTS, D),
        in_specs=[SMEM] + [VMEM] * REPS,
        scratch_shapes=[pltpu.VMEM((D, SLOTS), F32)],
        compiler_params=params(),
        cost_estimate=cost(0, 1_600_000),
        name="join",
    )(place(), *pieces)


def take(cap, back, target):
    blocks = OWNERS * cap // LANES
    return pl.pallas_call(
        functools.partial(take_kernel, blocks),
        out_shape=shape(K, VEC),
        in_specs=[SMEM, VMEM, VMEM],
        compiler_params=params(),
        cost_estimate=cost(2 * 24 * VEC * OWNERS * cap, 200_000),
        name="take",
    )(place(), back, target)


def on_device(vectors, parent_id, child_id):
    slot = (parent_id * K + child_id).astype(F32).reshape(1, VEC)
    turned = pl.pallas_call(
        turn_kernel,
        out_shape=shape(REPS, ROWS, VEC),
        compiler_params=params(),
        cost_estimate=cost(0, 1_600_000),
        name="turn",
    )(vectors, slot)
    got = lax.all_to_all(
        turned, "rep", 0, 0, axis_index_groups=[BY_CORE], tiled=True
    )
    pieces, back, target, most = refine(LANES, got)
    over = most[0] > LANES

    picked = take(LANES, back, target)

    def wide(got, pieces, picked):
        pieces, back, target, _ = refine(PAIR, got)
        return join(pieces), take(PAIR, back, target)

    def narrow(got, pieces, picked):
        return join(pieces), picked

    centroids, shares = lax.cond(over, wide, narrow, got, pieces, picked)
    return centroids, shares.T


def solution(mesh):
    in_specs = (P(("cluster", "rep"), None), P(("cluster", "rep")), P(("cluster", "rep")))
    out_specs = (P("cluster", None), P(("cluster", "rep"), None))
    return jax.shard_map(
        on_device, mesh=mesh, in_specs=in_specs, out_specs=out_specs, check_vma=False
    )
```

```python
import functools

import jax
import jax.numpy as jnp
from jax import lax
from jax.experimental import pallas as pl
from jax.experimental.pallas import tpu as pltpu
from jax.sharding import PartitionSpec as P

K = 8
PAR_DEV = 32
OWNERS = 32
REPS = 8
SLOTS = PAR_DEV * K
D = 768
PART = D // REPS
ROWS = PART + 8
VEC = 256
LANES = 128
PAIR = 2 * LANES
STACK = PART + 16 + PART
F32 = jnp.float32
BF16 = jnp.bfloat16
NT = (((1,), (1,)), ((), ()))


def params():
    return pltpu.CompilerParams(vmem_limit_bytes=48 * 2**20)


def iota(shape, dim):
    return lax.broadcasted_iota(jnp.int32, shape, dim)


def parts_of(x):
    high = x.astype(BF16)
    return high, (x - high.astype(F32)).astype(BF16)


def turn_kernel(v_ref, g_ref, out_ref):
    for tile in range(D // LANES):
        turned = v_ref[:, tile * LANES : (tile + 1) * LANES].T
        start = tile * LANES
        while start < (tile + 1) * LANES:
            part, row = divmod(start, PART)
            size = min(PART - row, (tile + 1) * LANES - start)
            at = start - tile * LANES
            out_ref[BY_CORE.index(part), row : row + size, :] = turned[at : at + size, :]
            start += size
    slots = jnp.broadcast_to(g_ref[...], (ROWS - PART, VEC))
    for part in range(REPS):
        out_ref[part, PART:ROWS, :] = slots


def pack_kernel(cap, in_ref, out_ref, target_ref, left, column):
    groups = OWNERS * cap // PAIR
    before = (iota((VEC, VEC), 0) < iota((VEC, VEC), 1)).astype(F32).astype(BF16)
    carry = jnp.zeros((OWNERS, 1), F32)
    targets = []
    for src in range(REPS):
        slot = in_ref[src, PART : PART + 1, :].astype(jnp.int32)
        owner = slot >> 8
        local = (slot & (SLOTS - 1)) + 1
        hot = (owner == iota((OWNERS, VEC), 0)).astype(F32)
        ahead = jnp.dot(hot.astype(BF16), before, preferred_element_type=F32) + carry
        position = jnp.sum(hot * ahead, axis=0, keepdims=True)
        carry = carry + jnp.sum(hot, axis=1, keepdims=True)
        target = owner.astype(F32) * cap + position
        targets.append(jnp.where(position < cap, target, -1.0))
        high, low = parts_of(in_ref[src, 0:PART, :])
        left[src, 0:PART, :] = high
        left[src, PART : PART + 16, :] = jnp.broadcast_to(local.astype(F32), (16, VEC)).astype(BF16)
        left[src, PART + 16 : STACK, :] = low
    rows = jnp.concatenate(targets, axis=0)
    target_ref[...] = rows.astype(jnp.int32)
    most = jnp.broadcast_to(jnp.max(carry, axis=0, keepdims=True), (8, LANES))
    first_row = iota((8, LANES), 0) == 0
    turned = jnp.concatenate([rows, jnp.zeros((LANES - REPS, VEC), F32)], axis=0).T
    for src in range(REPS):
        column[src] = jnp.broadcast_to(turned[:, src : src + 1], (VEC, LANES))
    lane = iota((VEC, LANES), 1).astype(F32)

    def group(n, _):
        base = (n * PAIR).astype(F32)
        total = jnp.zeros((STACK, PAIR), F32)
        for src in range(REPS):
            at = column[src] - base
            hot = jnp.concatenate(
                [
                    jnp.where(at == lane, 1.0, 0.0).astype(BF16),
                    jnp.where(at == lane + LANES, 1.0, 0.0).astype(BF16),
                ],
                axis=1,
            )
            total = total + jnp.dot(left[src], hot, preferred_element_type=F32)
        values = total[0:PART] + total[PART + 16 : STACK]
        for half in range(2):
            cut = slice(half * LANES, (half + 1) * LANES)
            out_ref[2 * n + half, 0:PART, :] = values[:, cut]
            out_ref[2 * n + half, PART:ROWS, :] = jnp.where(
                first_row, total[PART : PART + 8, cut], most
            )
        return 0

    lax.fori_loop(0, groups, group, 0, unroll=8)


def load_pair(x_ref, n):
    x = jnp.concatenate([x_ref[2 * n, 0:PART, :], x_ref[2 * n + 1, 0:PART, :]], axis=1)
    slot = jnp.concatenate(
        [x_ref[2 * n, PART : PART + 1, :], x_ref[2 * n + 1, PART : PART + 1, :]], axis=1
    )
    return x, slot.astype(jnp.int32)


def stack_of(x):
    high, low = parts_of(x)
    return jnp.concatenate([high, jnp.ones((16, PAIR), BF16), low], axis=0)


def distance_kernel(blocks, x_ref, out_ref, most_ref, total, scaled):
    total[...] = jnp.zeros_like(total)
    most_ref[0] = jnp.max(x_ref[:, PART + 1, :]).astype(jnp.int32)

    def add(n, _):
        x, slot = load_pair(x_ref, n)
        hot = jnp.where(iota((SLOTS, PAIR), 0) + 1 == slot, 1.0, 0.0).astype(BF16)
        total[...] += lax.dot_general(stack_of(x), hot, NT, preferred_element_type=F32)
        return 0

    lax.fori_loop(0, blocks // 2, add, 0, unroll=8)
    sums = total[0:PART, :] + total[PART + 16 : STACK, :]
    counts = total[PART : PART + 8, :]
    high, low = parts_of(sums / (counts[0:1] + 1.0))
    high, low = high.astype(F32), low.astype(F32)
    first = high + low
    turned = jnp.concatenate([high, high, low, low], axis=0).T
    scaled[0:SLOTS, :] = (turned[:, 0 : 2 * PART] * -2.0).astype(BF16)
    scaled[SLOTS:, :] = (turned[:, 2 * PART : 4 * PART] * -2.0).astype(BF16)
    own = jnp.broadcast_to(jnp.sum(first * first, axis=0, keepdims=True), (LANES, SLOTS))
    row = iota((LANES, SLOTS), 0)
    columns = jnp.where(row == 0, jnp.broadcast_to(counts[0:1], (LANES, SLOTS)), own).T
    count = columns[:, 0:1].reshape(PAR_DEV, K, 1)
    mean = jnp.sum(count, axis=1, keepdims=True) / K
    extra = (0.5 * count / (mean + 1.0)).reshape(SLOTS, 1) / REPS
    own = columns[:, 1:2]

    def measure(n, _):
        x, slot = load_pair(x_ref, n)
        both = jnp.dot(
            scaled[...], jnp.concatenate(parts_of(x), axis=0), preferred_element_type=F32
        )
        cross = both[0:SLOTS] + both[SLOTS : 2 * SLOTS]
        parent = (slot - 1) >> 3
        terms = ((cross + own) / D + extra).reshape(PAR_DEV, K, PAIR)
        picked = jnp.where(iota((PAR_DEV, K, PAIR), 0) == parent[None], terms, 0.0)
        part = jnp.sum(picked, axis=0) + jnp.sum(x * x, axis=0, keepdims=True) / D
        out_ref[2 * n] = part[:, 0:LANES]
        out_ref[2 * n + 1] = part[:, LANES:PAIR]
        return 0

    lax.fori_loop(0, blocks // 2, measure, 0, unroll=8)


def share_kernel(blocks, x_ref, pen_ref, cent_ref, share_ref, total, rest):
    total[...] = jnp.zeros_like(total)
    rest[...] = jnp.zeros_like(rest)

    def add(n, _):
        x, slot = load_pair(x_ref, n)
        grown = 1.0 + jnp.concatenate([pen_ref[2 * n], pen_ref[2 * n + 1]], axis=1)
        square = grown * grown
        weight = 1.0 / (square * square)
        share = weight / jnp.sum(weight, axis=0, keepdims=True)
        share = jnp.where(slot > 0, share, 0.0)
        share_ref[2 * n] = share[:, 0:LANES]
        share_ref[2 * n + 1] = share[:, LANES:PAIR]
        parent = (slot - 1) >> 3
        mixing = jnp.where(
            iota((PAR_DEV, K, PAIR), 0) == parent[None], share[None], 0.0
        ).reshape(SLOTS, PAIR)
        high, low = parts_of(mixing)
        left = stack_of(x)
        total[...] += lax.dot_general(left, high, NT, preferred_element_type=F32)
        rest[...] += lax.dot_general(
            left[0 : PART + 16], low, NT, preferred_element_type=F32
        )
        return 0

    lax.fori_loop(0, blocks // 2, add, 0, unroll=8)
    weighted = total[0:PART, :] + total[PART + 16 : STACK, :] + rest[0:PART, :]
    summed = total[PART : PART + 1, :] + rest[PART : PART + 1, :]
    cent_ref[...] = weighted / (summed + 1.0)


def join_kernel(at_ref, *refs):
    *pieces, out_ref, whole = refs
    x, core = at_ref[0], at_ref[1]
    for index, piece in enumerate(pieces):
        step, other = divmod(index, 2)
        where = ((x - step) & 3) * 2 + (core ^ other)
        whole[pl.ds(pl.multiple_of(where * PART, 8), PART), :] = piece[...]
    for tile in range(D // LANES):
        cut = slice(tile * LANES, (tile + 1) * LANES)
        out_ref[:, cut] = whole[cut, :].T


def take_kernel(blocks, at_ref, back_ref, target_ref, out_ref):
    target = target_ref[pl.ds(at_ref[2], 1), :]
    total = jnp.zeros((3 * K, VEC), F32)
    for n in range(blocks):
        hot = jnp.where(iota((LANES, VEC), 0) + n * LANES == target, 1.0, 0.0).astype(BF16)
        high, low = parts_of(back_ref[n])
        least = (back_ref[n] - high.astype(F32) - low.astype(F32)).astype(BF16)
        left = jnp.concatenate([high.astype(F32), low.astype(F32), least.astype(F32)], axis=0)
        total = total + jnp.dot(left.astype(BF16), hot, preferred_element_type=F32)
    out_ref[...] = total[0:K] + total[K : 2 * K] + total[2 * K : 3 * K]


def shape(*dims, kind=F32):
    return jax.ShapeDtypeStruct(dims, kind)


def cost(flops, data):
    return pl.CostEstimate(flops=flops, bytes_accessed=data, transcendentals=0)


def along_x(step):
    return [(i, ((i // 2 + step) % 4) * 2 + i % 2) for i in range(REPS)]


BY_CORE = [0, 2, 4, 6, 1, 3, 5, 7]
CORES = [(i, i ^ 1) for i in range(REPS)]


def sum_over_rep(x):
    x = x + lax.ppermute(x, "rep", CORES)
    x = x + lax.ppermute(x, "rep", [(i, i ^ 2) for i in range(REPS)])
    return x + lax.ppermute(x, "rep", [(i, i ^ 6) for i in range(REPS)])


SMEM = pl.BlockSpec(memory_space=pltpu.SMEM)
VMEM = pl.BlockSpec(memory_space=pltpu.VMEM)


def refine(cap, got):
    blocks = OWNERS * cap // LANES
    packed, target = pl.pallas_call(
        functools.partial(pack_kernel, cap),
        out_shape=(
            shape(blocks, ROWS, LANES),
            shape(REPS, VEC, kind=jnp.int32),
        ),
        scratch_shapes=[pltpu.VMEM((REPS, STACK, VEC), BF16), pltpu.VMEM((REPS, VEC, LANES), F32)],
        compiler_params=params(),
        cost_estimate=cost(2 * STACK * 2048 * OWNERS * cap, 3_000_000),
        name="pack",
    )(got)
    per = cap // LANES
    rows = lax.all_to_all(
        packed.reshape(OWNERS, per * ROWS, LANES), "cluster", 0, 0, tiled=True
    ).reshape(blocks, ROWS, LANES)
    partial, most = pl.pallas_call(
        functools.partial(distance_kernel, blocks),
        out_shape=(shape(blocks, K, LANES), shape(1, kind=jnp.int32)),
        out_specs=(VMEM, SMEM),
        scratch_shapes=[
            pltpu.VMEM((STACK, SLOTS), F32),
            pltpu.VMEM((2 * SLOTS, 2 * PART), BF16),
        ],
        compiler_params=params(),
        cost_estimate=cost(2 * 8 * PART * SLOTS * OWNERS * cap, 2_000_000),
        name="distance",
    )(rows)
    pen = sum_over_rep(partial)
    cent, share = pl.pallas_call(
        functools.partial(share_kernel, blocks),
        out_shape=(shape(PART, SLOTS), shape(blocks, K, LANES)),
        scratch_shapes=[
            pltpu.VMEM((STACK, SLOTS), F32),
            pltpu.VMEM((PART + 16, SLOTS), F32),
        ],
        compiler_params=params(),
        cost_estimate=cost(2 * 3 * PART * SLOTS * OWNERS * cap, 2_000_000),
        name="share",
    )(rows, pen)
    back = lax.all_to_all(
        share.reshape(OWNERS, per * K, LANES), "cluster", 0, 0, tiled=True
    ).reshape(blocks, K, LANES)
    pieces = []
    for step in range(4):
        mine = lax.ppermute(cent, "rep", along_x(step)) if step else cent
        pieces += [mine, lax.ppermute(mine, "rep", CORES)]
    return pieces, back, target, most


def place():
    rep = lax.axis_index("rep")
    return jnp.stack([rep // 2, rep % 2, rep % 2 * 4 + rep // 2]).astype(jnp.int32)


def join(pieces):
    return pl.pallas_call(
        join_kernel,
        out_shape=shape(SLOTS, D),
        in_specs=[SMEM] + [VMEM] * REPS,
        scratch_shapes=[pltpu.VMEM((D, SLOTS), F32)],
        compiler_params=params(),
        cost_estimate=cost(0, 1_600_000),
        name="join",
    )(place(), *pieces)


def take(cap, back, target):
    blocks = OWNERS * cap // LANES
    return pl.pallas_call(
        functools.partial(take_kernel, blocks),
        out_shape=shape(K, VEC),
        in_specs=[SMEM, VMEM, VMEM],
        compiler_params=params(),
        cost_estimate=cost(2 * 24 * VEC * OWNERS * cap, 200_000),
        name="take",
    )(place(), back, target)


def on_device(vectors, parent_id, child_id):
    slot = (parent_id * K + child_id).astype(F32).reshape(1, VEC)
    turned = pl.pallas_call(
        turn_kernel,
        out_shape=shape(REPS, ROWS, VEC),
        compiler_params=params(),
        cost_estimate=cost(0, 1_600_000),
        name="turn",
    )(vectors, slot)
    got = lax.all_to_all(
        turned, "rep", 0, 0, axis_index_groups=[BY_CORE], tiled=True
    )
    pieces, back, target, most = refine(LANES, got)
    over = most[0] > LANES

    picked = take(LANES, back, target)

    def wide(got, pieces, picked):
        pieces, back, target, _ = refine(PAIR, got)
        return join(pieces), take(PAIR, back, target)

    def narrow(got, pieces, picked):
        return join(pieces), picked

    centroids, shares = lax.cond(over, wide, narrow, got, pieces, picked)
    return centroids, shares.T


def solution(mesh):
    in_specs = (P(("cluster", "rep"), None), P(("cluster", "rep")), P(("cluster", "rep")))
    out_specs = (P("cluster", None), P(("cluster", "rep"), None))
    return jax.shard_map(
        on_device, mesh=mesh, in_specs=in_specs, out_specs=out_specs, check_vma=False
    )
```

```python
import functools

import jax
import jax.numpy as jnp
from jax import lax
from jax.experimental import pallas as pl
from jax.experimental.pallas import tpu as pltpu
from jax.sharding import PartitionSpec as P

K = 8
PAR_DEV = 32
OWNERS = 32
REPS = 8
SLOTS = PAR_DEV * K
D = 768
PART = D // REPS
ROWS = PART + 8
VEC = 256
LANES = 128
PAIR = 2 * LANES
STACK = PART + 16 + PART
F32 = jnp.float32
BF16 = jnp.bfloat16
NT = (((1,), (1,)), ((), ()))


def params():
    return pltpu.CompilerParams(vmem_limit_bytes=48 * 2**20)


def iota(shape, dim):
    return lax.broadcasted_iota(jnp.int32, shape, dim)


def parts_of(x):
    high = x.astype(BF16)
    return high, (x - high.astype(F32)).astype(BF16)


def turn_kernel(v_ref, g_ref, out_ref):
    for tile in range(D // LANES):
        turned = v_ref[:, tile * LANES : (tile + 1) * LANES].T
        start = tile * LANES
        while start < (tile + 1) * LANES:
            part, row = divmod(start, PART)
            size = min(PART - row, (tile + 1) * LANES - start)
            at = start - tile * LANES
            out_ref[BY_CORE.index(part), row : row + size, :] = turned[at : at + size, :]
            start += size
    slots = jnp.broadcast_to(g_ref[...], (ROWS - PART, VEC))
    for part in range(REPS):
        out_ref[part, PART:ROWS, :] = slots


def pack_kernel(cap, in_ref, out_ref, target_ref, left, column):
    groups = OWNERS * cap // PAIR
    before = (iota((VEC, VEC), 0) < iota((VEC, VEC), 1)).astype(F32).astype(BF16)
    carry = jnp.zeros((OWNERS, 1), F32)
    targets = []
    for src in range(REPS):
        slot = in_ref[src, PART : PART + 1, :].astype(jnp.int32)
        owner = slot >> 8
        local = (slot & (SLOTS - 1)) + 1
        hot = (owner == iota((OWNERS, VEC), 0)).astype(F32)
        ahead = jnp.dot(hot.astype(BF16), before, preferred_element_type=F32) + carry
        position = jnp.sum(hot * ahead, axis=0, keepdims=True)
        carry = carry + jnp.sum(hot, axis=1, keepdims=True)
        target = owner.astype(F32) * cap + position
        targets.append(jnp.where(position < cap, target, -1.0))
        high, low = parts_of(in_ref[src, 0:PART, :])
        left[src, 0:PART, :] = high
        left[src, PART : PART + 16, :] = jnp.broadcast_to(local.astype(F32), (16, VEC)).astype(BF16)
        left[src, PART + 16 : STACK, :] = low
    rows = jnp.concatenate(targets, axis=0)
    target_ref[...] = rows.astype(jnp.int32)
    most = jnp.broadcast_to(jnp.max(carry, axis=0, keepdims=True), (8, LANES))
    first_row = iota((8, LANES), 0) == 0
    turned = jnp.concatenate([rows, jnp.zeros((LANES - REPS, VEC), F32)], axis=0).T
    for src in range(REPS):
        column[src] = jnp.broadcast_to(turned[:, src : src + 1], (VEC, LANES))
    lane = iota((VEC, LANES), 1).astype(F32)

    def group(n, _):
        base = (n * PAIR).astype(F32)
        total = jnp.zeros((STACK, PAIR), F32)
        for src in range(REPS):
            at = column[src] - base
            hot = jnp.concatenate(
                [
                    jnp.where(at == lane, 1.0, 0.0).astype(BF16),
                    jnp.where(at == lane + LANES, 1.0, 0.0).astype(BF16),
                ],
                axis=1,
            )
            total = total + jnp.dot(left[src], hot, preferred_element_type=F32)
        values = total[0:PART] + total[PART + 16 : STACK]
        for half in range(2):
            cut = slice(half * LANES, (half + 1) * LANES)
            out_ref[2 * n + half, 0:PART, :] = values[:, cut]
            out_ref[2 * n + half, PART:ROWS, :] = jnp.where(
                first_row, total[PART : PART + 8, cut], most
            )
        return 0

    lax.fori_loop(0, groups, group, 0, unroll=8)


def load_pair(x_ref, n):
    x = jnp.concatenate([x_ref[2 * n, 0:PART, :], x_ref[2 * n + 1, 0:PART, :]], axis=1)
    slot = jnp.concatenate(
        [x_ref[2 * n, PART : PART + 1, :], x_ref[2 * n + 1, PART : PART + 1, :]], axis=1
    )
    return x, slot.astype(jnp.int32)


def stack_of(x):
    high, low = parts_of(x)
    return jnp.concatenate([high, jnp.ones((16, PAIR), BF16), low], axis=0)


def distance_kernel(blocks, x_ref, out_ref, most_ref, total, scaled):
    total[...] = jnp.zeros_like(total)
    most_ref[0] = jnp.max(x_ref[:, PART + 1, :]).astype(jnp.int32)

    def add(n, _):
        x, slot = load_pair(x_ref, n)
        hot = jnp.where(iota((SLOTS, PAIR), 0) + 1 == slot, 1.0, 0.0).astype(BF16)
        total[...] += lax.dot_general(stack_of(x), hot, NT, preferred_element_type=F32)
        return 0

    lax.fori_loop(0, blocks // 2, add, 0, unroll=8)
    sums = total[0:PART, :] + total[PART + 16 : STACK, :]
    counts = total[PART : PART + 8, :]
    high, low = parts_of(sums / (counts[0:1] + 1.0))
    high, low = high.astype(F32), low.astype(F32)
    first = high + low
    turned = jnp.concatenate([high, high, low, low], axis=0).T
    scaled[0:SLOTS, :] = (turned[:, 0 : 2 * PART] * -2.0).astype(BF16)
    scaled[SLOTS:, :] = (turned[:, 2 * PART : 4 * PART] * -2.0).astype(BF16)
    own = jnp.broadcast_to(jnp.sum(first * first, axis=0, keepdims=True), (LANES, SLOTS))
    row = iota((LANES, SLOTS), 0)
    columns = jnp.where(row == 0, jnp.broadcast_to(counts[0:1], (LANES, SLOTS)), own).T
    count = columns[:, 0:1].reshape(PAR_DEV, K, 1)
    mean = jnp.sum(count, axis=1, keepdims=True) / K
    extra = (0.5 * count / (mean + 1.0)).reshape(SLOTS, 1) / REPS
    own = columns[:, 1:2]

    def measure(n, _):
        x, slot = load_pair(x_ref, n)
        both = jnp.dot(
            scaled[...], jnp.concatenate(parts_of(x), axis=0), preferred_element_type=F32
        )
        cross = both[0:SLOTS] + both[SLOTS : 2 * SLOTS]
        parent = (slot - 1) >> 3
        terms = ((cross + own) / D + extra).reshape(PAR_DEV, K, PAIR)
        picked = jnp.where(iota((PAR_DEV, K, PAIR), 0) == parent[None], terms, 0.0)
        part = jnp.sum(picked, axis=0) + jnp.sum(x * x, axis=0, keepdims=True) / D
        out_ref[2 * n] = part[:, 0:LANES]
        out_ref[2 * n + 1] = part[:, LANES:PAIR]
        return 0

    lax.fori_loop(0, blocks // 2, measure, 0, unroll=8)


def share_kernel(blocks, x_ref, pen_ref, cent_ref, share_ref, total, rest):
    total[...] = jnp.zeros_like(total)
    rest[...] = jnp.zeros_like(rest)

    def add(n, _):
        x, slot = load_pair(x_ref, n)
        grown = 1.0 + jnp.concatenate([pen_ref[2 * n], pen_ref[2 * n + 1]], axis=1)
        square = grown * grown
        weight = 1.0 / (square * square)
        share = weight / jnp.sum(weight, axis=0, keepdims=True)
        share = jnp.where(slot > 0, share, 0.0)
        share_ref[2 * n] = share[:, 0:LANES]
        share_ref[2 * n + 1] = share[:, LANES:PAIR]
        parent = (slot - 1) >> 3
        mixing = jnp.where(
            iota((PAR_DEV, K, PAIR), 0) == parent[None], share[None], 0.0
        ).reshape(SLOTS, PAIR)
        high, low = parts_of(mixing)
        left = stack_of(x)
        total[...] += lax.dot_general(left, high, NT, preferred_element_type=F32)
        rest[...] += lax.dot_general(
            left[0 : PART + 16], low, NT, preferred_element_type=F32
        )
        return 0

    lax.fori_loop(0, blocks // 2, add, 0, unroll=8)
    weighted = total[0:PART, :] + total[PART + 16 : STACK, :] + rest[0:PART, :]
    summed = total[PART : PART + 1, :] + rest[PART : PART + 1, :]
    cent_ref[...] = weighted / (summed + 1.0)


def join_kernel(at_ref, *refs):
    *pieces, out_ref, whole = refs
    x, core = at_ref[0], at_ref[1]
    for index, piece in enumerate(pieces):
        step, other = divmod(index, 2)
        where = ((x - step) & 3) * 2 + (core ^ other)
        whole[pl.ds(pl.multiple_of(where * PART, 8), PART), :] = piece[...]
    for tile in range(D // LANES):
        cut = slice(tile * LANES, (tile + 1) * LANES)
        out_ref[:, cut] = whole[cut, :].T


def take_kernel(blocks, at_ref, back_ref, target_ref, out_ref):
    target = target_ref[pl.ds(at_ref[2], 1), :]
    total = jnp.zeros((3 * K, VEC), F32)
    for n in range(blocks // 2):
        hot = jnp.where(iota((PAIR, VEC), 0) + n * PAIR == target, 1.0, 0.0).astype(BF16)
        back = jnp.concatenate([back_ref[2 * n], back_ref[2 * n + 1]], axis=1)
        high, low = parts_of(back)
        least = (back - high.astype(F32) - low.astype(F32)).astype(BF16)
        left = jnp.concatenate([high.astype(F32), low.astype(F32), least.astype(F32)], axis=0)
        total = total + jnp.dot(left.astype(BF16), hot, preferred_element_type=F32)
    out_ref[...] = total[0:K] + total[K : 2 * K] + total[2 * K : 3 * K]


def shape(*dims, kind=F32):
    return jax.ShapeDtypeStruct(dims, kind)


def cost(flops, data):
    return pl.CostEstimate(flops=flops, bytes_accessed=data, transcendentals=0)


def along_x(step):
    return [(i, ((i // 2 + step) % 4) * 2 + i % 2) for i in range(REPS)]


BY_CORE = [0, 2, 4, 6, 1, 3, 5, 7]
CORES = [(i, i ^ 1) for i in range(REPS)]


def sum_over_rep(x):
    x = x + lax.ppermute(x, "rep", CORES)
    x = x + lax.ppermute(x, "rep", [(i, i ^ 2) for i in range(REPS)])
    return x + lax.ppermute(x, "rep", [(i, i ^ 6) for i in range(REPS)])


SMEM = pl.BlockSpec(memory_space=pltpu.SMEM)
VMEM = pl.BlockSpec(memory_space=pltpu.VMEM)


def refine(cap, got):
    blocks = OWNERS * cap // LANES
    packed, target = pl.pallas_call(
        functools.partial(pack_kernel, cap),
        out_shape=(
            shape(blocks, ROWS, LANES),
            shape(REPS, VEC, kind=jnp.int32),
        ),
        scratch_shapes=[pltpu.VMEM((REPS, STACK, VEC), BF16), pltpu.VMEM((REPS, VEC, LANES), F32)],
        compiler_params=params(),
        cost_estimate=cost(2 * STACK * 2048 * OWNERS * cap, 3_000_000),
        name="pack",
    )(got)
    per = cap // LANES
    rows = lax.all_to_all(
        packed.reshape(OWNERS, per * ROWS, LANES), "cluster", 0, 0, tiled=True
    ).reshape(blocks, ROWS, LANES)
    partial, most = pl.pallas_call(
        functools.partial(distance_kernel, blocks),
        out_shape=(shape(blocks, K, LANES), shape(1, kind=jnp.int32)),
        out_specs=(VMEM, SMEM),
        scratch_shapes=[
            pltpu.VMEM((STACK, SLOTS), F32),
            pltpu.VMEM((2 * SLOTS, 2 * PART), BF16),
        ],
        compiler_params=params(),
        cost_estimate=cost(2 * 8 * PART * SLOTS * OWNERS * cap, 2_000_000),
        name="distance",
    )(rows)
    pen = sum_over_rep(partial)
    cent, share = pl.pallas_call(
        functools.partial(share_kernel, blocks),
        out_shape=(shape(PART, SLOTS), shape(blocks, K, LANES)),
        scratch_shapes=[
            pltpu.VMEM((STACK, SLOTS), F32),
            pltpu.VMEM((PART + 16, SLOTS), F32),
        ],
        compiler_params=params(),
        cost_estimate=cost(2 * 3 * PART * SLOTS * OWNERS * cap, 2_000_000),
        name="share",
    )(rows, pen)
    back = lax.all_to_all(
        share.reshape(OWNERS, per * K, LANES), "cluster", 0, 0, tiled=True
    ).reshape(blocks, K, LANES)
    pieces = []
    for step in range(4):
        mine = lax.ppermute(cent, "rep", along_x(step)) if step else cent
        pieces += [mine, lax.ppermute(mine, "rep", CORES)]
    return pieces, back, target, most


def place():
    rep = lax.axis_index("rep")
    return jnp.stack([rep // 2, rep % 2, rep % 2 * 4 + rep // 2]).astype(jnp.int32)


def join(pieces):
    return pl.pallas_call(
        join_kernel,
        out_shape=shape(SLOTS, D),
        in_specs=[SMEM] + [VMEM] * REPS,
        scratch_shapes=[pltpu.VMEM((D, SLOTS), F32)],
        compiler_params=params(),
        cost_estimate=cost(0, 1_600_000),
        name="join",
    )(place(), *pieces)


def take(cap, back, target):
    blocks = OWNERS * cap // LANES
    return pl.pallas_call(
        functools.partial(take_kernel, blocks),
        out_shape=shape(K, VEC),
        in_specs=[SMEM, VMEM, VMEM],
        compiler_params=params(),
        cost_estimate=cost(2 * 24 * VEC * OWNERS * cap, 200_000),
        name="take",
    )(place(), back, target)


def on_device(vectors, parent_id, child_id):
    slot = (parent_id * K + child_id).astype(F32).reshape(1, VEC)
    turned = pl.pallas_call(
        turn_kernel,
        out_shape=shape(REPS, ROWS, VEC),
        compiler_params=params(),
        cost_estimate=cost(0, 1_600_000),
        name="turn",
    )(vectors, slot)
    got = lax.all_to_all(
        turned, "rep", 0, 0, axis_index_groups=[BY_CORE], tiled=True
    )
    pieces, back, target, most = refine(LANES, got)
    over = most[0] > LANES

    picked = take(LANES, back, target)

    def wide(got, pieces, picked):
        pieces, back, target, _ = refine(PAIR, got)
        return join(pieces), take(PAIR, back, target)

    def narrow(got, pieces, picked):
        return join(pieces), picked

    centroids, shares = lax.cond(over, wide, narrow, got, pieces, picked)
    return centroids, shares.T


def solution(mesh):
    in_specs = (P(("cluster", "rep"), None), P(("cluster", "rep")), P(("cluster", "rep")))
    out_specs = (P("cluster", None), P(("cluster", "rep"), None))
    return jax.shard_map(
        on_device, mesh=mesh, in_specs=in_specs, out_specs=out_specs, check_vma=False
    )
```
